32 devices in a mesh: dp: 16 (over z, y, core), blk: 2 (over x).
Axes of the slice: x: 2, y: 2, z: 4, core: 2. Of those that a mesh axis runs over, the one named last changes fastest.
Arguments:
- hidden: bfloat16 [64, 512, 768], P('dp', 'blk'), may hold values from -6 to 6
- lengths: int32 [64, 2], P('dp'), may hold values from 1 to 512, as said below
- flags: int32 [64], P('dp'), may hold values from 0 to 1
- buckets: int32 [1023], replicated, may hold values from 0 to 31
- g_attn: float32 [768], replicated, may hold values from 0.5 to 1.5
- w_query: bfloat16 [768, 768], replicated, may hold values from -0.21875 to 0.21875
- w_key: bfloat16 [768, 768], replicated, may hold values from -0.21875 to 0.21875
- w_value: bfloat16 [768, 768], replicated, may hold values from -0.21875 to 0.21875
- w_out: bfloat16 [768, 768], replicated, may hold values from -0.625 to 0.625
- g_ffn: float32 [768], replicated, may hold values from 0.5 to 1.5
- w_in: bfloat16 [768, 3072], replicated, may hold values from -0.21875 to 0.21875
- w_ffn_out: bfloat16 [3072, 768], replicated, may hold values from -0.109375 to 0.109375
- bias_table: float32 [32, 12], replicated, may hold values from -4 to 4
- cotangent: bfloat16 [64, 512, 768], P('dp', 'blk'), may hold values from -6 to 6
Outputs:
- output: bfloat16 [64, 512, 768], P('dp', 'blk')
- input_grad: bfloat16 [64, 512, 768], P('dp', 'blk')
- g_attn_grad: float32 [768], P('dp')
- query_grad: float32 [768, 768], P('dp')
- key_grad: float32 [768, 768], P('dp')
- value_grad: float32 [768, 768], P('dp')
- out_grad: float32 [768, 768], P('dp')
- g_ffn_grad: float32 [768], P('dp')
- in_grad: float32 [768, 3072], P('dp')
- ffn_out_grad: float32 [3072, 768], P('dp')
- table_grad: float32 [32, 12], replicated
The draws below stay inside these ranges and needn't reach their ends.
Inputs may be any that keep to these rules, and one draw needn't show every extreme that they name: In each aligned group of 4 sequences, one, drawn from the seed, has both lengths equal to 512.
All inputs are finite; a program needn't handle non-finite values.
Results may differ from the reference program's by a relative error of at most 0.017.
Values may be sent and summed in bfloat16 or wider, within the bound.
No kernel may reach another device: no remote copies, remote signals or barrier semaphores. Data moves between devices by JAX's collectives and lax.ppermute only.
A program may use at most 256 MiB of HBM per device.

```python
import jax
import jax.numpy as jnp
from jax import lax

D = 768
FF = 3072
HEADS = 12
HEAD_DIM = 64
BUCKETS = 32
SEQ_LEN = 512
SEQ_DEV = 4
SEQS = 64


def draw_lengths(key, part):
    key = jax.random.fold_in(key, 7)
    drawn_len = jax.random.randint(key, (SEQS, 2), 1, SEQ_LEN + 1)
    chosen = jax.random.randint(jax.random.fold_in(key, 1), (SEQS // SEQ_DEV,), 0, SEQ_DEV)
    position = jnp.arange(SEQS, dtype=jnp.int32) % SEQ_DEV
    whole_rows = position == jnp.repeat(chosen, SEQ_DEV)
    return jnp.where(whole_rows[:, None], SEQ_LEN, drawn_len).astype(jnp.int32)


def touch_ends(drawn, stream_key, smallest, largest):
    index_at = [jax.random.randint(jax.random.fold_in(stream_key, axis), (), 0, length) for axis, length in enumerate(drawn.shape)]
    widest = drawn.shape.index(max(drawn.shape))
    neighbour = index_at[:widest] + [(index_at[widest] + 1) % drawn.shape[widest]] + index_at[widest + 1:]
    return drawn.at[tuple(index_at)].set(smallest).at[tuple(neighbour)].set(largest)


def block_scale(stream_key, dims, cuts, least, high):
    loudness, own = 1.0, jax.random.fold_in(stream_key, 6)
    for dim, blocks in cuts:
        steps = jnp.exp(jax.random.uniform(jax.random.fold_in(own, dim), (blocks,), jnp.float32, least / len(cuts), high / len(cuts)))
        loudness = loudness * jnp.repeat(steps, dims[dim] // blocks).reshape([-1 if axis == dim else 1 for axis in range(len(dims))])
    return loudness


def normal_values(key, shape, scale, most, pieces=(), held_as=jnp.bfloat16):
    result = jax.random.normal(key, shape, jnp.float32) * scale
    if len(pieces) > 0:
        result = block_scale(key, shape, pieces, -0.22, 0.18) * result
    return jnp.clip(result, min=-most, max=most).astype(held_as)


def setup_inputs(seed: int = 0) -> dict:
    streams_of = jax.random.split(jax.random.key(seed), 15)
    hidden = normal_values(streams_of[0], (SEQS, SEQ_LEN, D), 1.0, 6.0, ((0, 16), (1, 2)))
    lengths = draw_lengths(jax.random.fold_in(streams_of[14], 71), 0)
    flags = touch_ends(jax.random.randint(streams_of[2], (SEQS,), 0, 2), jax.random.fold_in(streams_of[2], 1), 0, 1).astype(jnp.int32)
    buckets = touch_ends(jax.random.randint(streams_of[3], (2 * SEQ_LEN - 1,), 0, BUCKETS), jax.random.fold_in(streams_of[3], 1), 0, BUCKETS - 1).astype(jnp.int32)
    g_attn = jnp.clip(1.0 + 0.1 * jax.random.normal(streams_of[4], (D,), jnp.float32), 0.5, 1.5)
    w_query = normal_values(streams_of[5], (D, D), D ** -0.5, 0.21875)
    w_key = normal_values(streams_of[6], (D, D), D ** -0.5, 0.21875)
    w_value = normal_values(streams_of[7], (D, D), D ** -0.5, 0.21875)
    w_out = normal_values(streams_of[8], (D, D), (D // 8) ** -0.5, 0.625)
    g_ffn = jnp.clip(1.0 + 0.1 * jax.random.normal(streams_of[9], (D,), jnp.float32), 0.5, 1.5)
    w_in = normal_values(streams_of[10], (D, FF), D ** -0.5, 0.21875)
    w_ffn_out = normal_values(streams_of[11], (FF, D), FF ** -0.5, 0.109375)
    bias_table = normal_values(streams_of[12], (BUCKETS, HEADS), 1.0, 4.0, (), jnp.float32)
    cotangent = normal_values(streams_of[13], (SEQS, SEQ_LEN, D), 1.0, 6.0, ((0, 16), (1, 2)))
    return {"hidden": hidden, "lengths": lengths, "flags": flags, "buckets": buckets, "g_attn": g_attn, "w_query": w_query, "w_key": w_key, "w_value": w_value, "w_out": w_out, "g_ffn": g_ffn, "w_in": w_in, "w_ffn_out": w_ffn_out, "bias_table": bias_table, "cotangent": cotangent}


@jax.custom_vjp
def low(v):
    return lax.optimization_barrier(v.astype(jnp.bfloat16)).astype(jnp.float32)

@jax.custom_vjp
def low_back(v):
    return v

def low_keep(v):
    return (low(v), None)

def low_pass(kept, grad):
    return (grad,)

def back_keep(v):
    return (v, None)

def back_low(kept, grad):
    return (low(grad),)
low.defvjp(low_keep, low_pass)
low_back.defvjp(back_keep, back_low)
EPSILON = 1e-06
MASKED = -1000000000.0

def rms_scale(values, gain):
    return values * lax.rsqrt(lax.optimization_barrier(jnp.mean(values * values, axis=-1, keepdims=True)) + EPSILON) * gain

def product(left_operand, weight_matrix):
    return jnp.einsum('frv,vn->frn', left_operand, weight_matrix, precision=lax.Precision.HIGHEST)

def reference(hidden, lengths, flags, buckets, g_attn, w_query, w_key, w_value, w_out, g_ffn, w_in, w_ffn_out, bias_table, cotangent):
    valid = jnp.where(flags == 1, lengths[:, 1], lengths[:, 0]).astype(jnp.int32)
    positions = jnp.arange(SEQ_LEN, dtype=jnp.int32)
    offsets = buckets[positions[None, :] - positions[:, None] + SEQ_LEN - 1]
    one_hot = (offsets[None] == jnp.arange(BUCKETS, dtype=jnp.int32)[:, None, None]).astype(jnp.float32)

    def forward(inputs, gain_attn, weight_query, weight_key, weight_value, weight_out, gain_ffn, weight_in, weight_ffn_out, table):
        rel_bias = jnp.einsum('bij,bh->hij', one_hot, table, precision=lax.Precision.HIGHEST)
        attn_in = low(rms_scale(inputs, gain_attn))
        queries = low(low_back(product(attn_in, weight_query))).reshape(SEQS, SEQ_LEN, HEADS, HEAD_DIM)
        keys_all = low(low_back(product(attn_in, weight_key))).reshape(SEQS, SEQ_LEN, HEADS, HEAD_DIM)
        values_all = low(low_back(product(attn_in, weight_value))).reshape(SEQS, SEQ_LEN, HEADS, HEAD_DIM)

        def one_sequence(items):
            query_seq, key_seq, value_seq, limit = items
            raw = low_back(0.125 * jnp.einsum('qhd,khd->hqk', query_seq, key_seq, precision=lax.Precision.HIGHEST))
            logits = jnp.where((positions < limit)[None, None, :], raw + rel_bias, MASKED)
            shifted = jnp.exp(logits - lax.optimization_barrier(jnp.max(logits, axis=-1, keepdims=True)))
            probs = shifted / lax.optimization_barrier(jnp.sum(shifted, axis=-1, keepdims=True))
            mixed_heads = jnp.einsum('hqk,khd->qhd', low(probs), value_seq, precision=lax.Precision.HIGHEST)
            return mixed_heads.reshape(SEQ_LEN, D)
        context = lax.map(jax.checkpoint(one_sequence), (queries, keys_all, values_all, valid))
        context = low(low_back(context))
        mixed = inputs + low_back(product(context, weight_out))
        ffn_in = low(rms_scale(mixed, gain_ffn))
        pre = low_back(product(ffn_in, weight_in))
        act = low(jax.nn.gelu(pre, approximate=False))
        return mixed + low_back(product(act, weight_ffn_out))
    primals = (hidden.astype(jnp.float32), g_attn, w_query.astype(jnp.float32), w_key.astype(jnp.float32), w_value.astype(jnp.float32), w_out.astype(jnp.float32), g_ffn, w_in.astype(jnp.float32), w_ffn_out.astype(jnp.float32), bias_table)
    layer_out, pullback = jax.vjp(forward, *primals)
    grads = pullback(cotangent.astype(jnp.float32))
    return (layer_out.astype(jnp.bfloat16), grads[0].astype(jnp.bfloat16), grads[1], grads[2], grads[3], grads[4], grads[5], grads[6], grads[7], grads[8], grads[9])
```

```python
import functools

import jax
import jax.numpy as jnp
from jax import lax
from jax.experimental import pallas as pl
from jax.experimental.pallas import tpu as pltpu
from jax.sharding import PartitionSpec as P

EPSILON = 1e-06
MASKED = -1000000000.0
SCALING = 0.125
LOG2E = 1.4426950408889634
LN2 = 0.6931471805599453
HEAD = 64
LANES = 128
BF16 = jnp.bfloat16
F32 = jnp.float32


def dot(left, right, left_dim, right_dim):
    return lax.dot_general(
        left, right, (((left_dim,), (right_dim,)), ((), ())), preferred_element_type=F32
    )


def expand_kernel(vector_ref, out_ref):
    width = vector_ref.shape[2]
    rows = jnp.broadcast_to(vector_ref[0], (LANES, width))
    moved = pltpu.roll(rows, 0, 1, stride=1, stride_axis=0)
    out_ref[0] = moved[:, : out_ref.shape[2]]


def expand_bias(vector, width):
    heads, length = vector.shape
    return pl.pallas_call(
        expand_kernel,
        grid=(heads,),
        in_specs=[pl.BlockSpec((1, 1, length), lambda h: (h, 0, 0))],
        out_specs=pl.BlockSpec((1, LANES, width), lambda h: (h, 0, 0)),
        out_shape=jax.ShapeDtypeStruct((heads, LANES, width), F32),
    )(vector.reshape(heads, 1, length))


def fold_kernel(grad_ref, out_ref):
    width = grad_ref.shape[2]
    length = out_ref.shape[2]
    pad = jnp.zeros((8, length - width), F32)
    total = jnp.zeros((8, length), F32)
    for start in range(0, LANES, 8):
        rows = jnp.concatenate([grad_ref[0, start : start + 8, :], pad], axis=1)
        total = total + pltpu.roll(rows, LANES - 8 - start, 1)
    folded = total[7:8]
    for row in range(7):
        folded = folded + pltpu.roll(total[row : row + 1], 7 - row, 1)
    out_ref[0] = jnp.broadcast_to(folded, (8, length))


def fold_bias(grad, length):
    heads, _, width = grad.shape
    return pl.pallas_call(
        fold_kernel,
        grid=(heads,),
        in_specs=[pl.BlockSpec((1, LANES, width), lambda h: (h, 0, 0))],
        out_specs=pl.BlockSpec((1, 8, length), lambda h: (h, 0, 0)),
        out_shape=jax.ShapeDtypeStruct((heads, 8, length), F32),
    )(grad)[:, 0]


def attend_kernel(valid, q_ref, k_ref, v_ref, bias_ref, out_ref, probs_ref, *, chunk):
    limit = valid[pl.program_id(1)]
    count = q_ref.shape[1]
    queries, keys, values = q_ref[0].astype(F32), k_ref[0].astype(F32), v_ref[0].astype(F32)
    lane = lax.broadcasted_iota(jnp.int32, (count, LANES), 1)
    row = lax.broadcasted_iota(jnp.int32, (count, LANES), 0)
    heads = []
    for head in range(2):
        mine = (lane // HEAD) == head
        extra = lane == (1 - head) * HEAD
        mask = jnp.where(extra & (row >= limit), MASKED, 0.0)
        heads.append(
            (
                jnp.where(mine, queries, jnp.where(extra, 1.0, 0.0)).astype(BF16),
                jnp.where(mine, keys, mask).astype(BF16),
                jnp.where(mine, values, 0.0).astype(BF16),
            )
        )
    for step in range(count // chunk):
        rows = slice(step * chunk, (step + 1) * chunk)
        total = None
        for head in range(2):
            q_head, k_head, v_head = heads[head]
            windows = [
                bias_ref[head, :, count - LANES * (1 + block) : 2 * count - LANES * (1 + block)]
                for block in range(step * chunk // LANES, (step + 1) * chunk // LANES)
            ]
            logits = dot(q_head[rows], k_head, 1, 1) + jnp.concatenate(windows, axis=0)
            top = jnp.max(logits, axis=1, keepdims=True)
            weights = jnp.exp2(logits - top)
            norm = jnp.sum(weights, axis=1, keepdims=True)
            probs = (weights * (1.0 / norm)).astype(BF16)
            probs_ref[0, head, rows, :] = probs
            part = dot(probs, v_head, 1, 0)
            total = part if total is None else total + part
        out_ref[0, rows, :] = total.astype(BF16)


def attend(queries, keys, values, bias, valid, chunk=256):
    seqs, count, width = queries.shape
    block = pl.BlockSpec((1, count, LANES), lambda p, s, *_: (s, 0, p))
    return pl.pallas_call(
        functools.partial(attend_kernel, chunk=chunk),
        grid_spec=pltpu.PrefetchScalarGridSpec(
            num_scalar_prefetch=1,
            grid=(width // LANES, seqs),
            in_specs=[
                block,
                block,
                block,
                pl.BlockSpec((2, LANES, bias.shape[2]), lambda p, s, *_: (p, 0, 0)),
            ],
            out_specs=[block, pl.BlockSpec((1, 2, count, count), lambda p, s, *_: (s, p, 0, 0))],
        ),
        out_shape=[
            jax.ShapeDtypeStruct(queries.shape, BF16),
            jax.ShapeDtypeStruct((seqs, width // HEAD, count, count), BF16),
        ],
        compiler_params=pltpu.CompilerParams(vmem_limit_bytes=48 * 2**20),
        cost_estimate=pl.CostEstimate(
            flops=20 * seqs * count * count * width, bytes_accessed=40 * 2**20, transcendentals=0
        ),
    )(valid, queries, keys, values, bias)


def attend_back_kernel(
    q_ref, k_ref, v_ref, grad_ref, ctx_ref, probs_ref, dq_ref, dk_ref, dv_ref, bias_ref, *, chunk
):
    count = q_ref.shape[1]
    queries, keys, values = q_ref[0].astype(F32), k_ref[0].astype(F32), v_ref[0].astype(F32)
    grads = grad_ref[0]
    queries_t = jnp.transpose(queries).astype(BF16)
    grads_t = jnp.transpose(grads.astype(F32)).astype(BF16)
    lane = lax.broadcasted_iota(jnp.int32, (count, LANES), 1)
    products = grads.astype(F32) * ctx_ref[0].astype(F32)

    @pl.when(pl.program_id(1) == 0)
    def _():
        bias_ref[...] = jnp.zeros_like(bias_ref)

    steps = count // chunk
    dq = [None] * steps
    for head in range(2):
        mine = (lane // HEAD) == head
        own = slice(head * HEAD, (head + 1) * HEAD)
        k_head = jnp.where(mine, keys, 0.0).astype(BF16)
        v_head = jnp.where(mine, values, 0.0).astype(BF16)
        delta = jnp.sum(jnp.where(mine, products, 0.0), axis=1, keepdims=True)
        dk, dv = None, None
        for step in range(steps):
            rows = slice(step * chunk, (step + 1) * chunk)
            probs = probs_ref[0, head, rows, :]
            grad_probs = dot(grads[rows], v_head, 1, 1)
            grad_logits = probs.astype(F32) * (grad_probs - delta[rows])
            for block in range(chunk // LANES):
                start = count - LANES * (1 + step * chunk // LANES + block)
                bias_ref[head, :, start : start + count] += grad_logits[
                    block * LANES : (block + 1) * LANES
                ]
            low = grad_logits.astype(BF16)
            part_q = dot(low, k_head, 1, 0)
            part_k = dot(queries_t[own, rows], low, 1, 0)
            part_v = dot(grads_t[own, rows], probs, 1, 0)
            dq[step] = part_q if dq[step] is None else dq[step] + part_q
            dk = part_k if dk is None else dk + part_k
            dv = part_v if dv is None else dv + part_v
        dk_ref[own, :] = (LN2 * dk).astype(BF16)
        dv_ref[own, :] = dv.astype(BF16)
    for step in range(steps):
        dq_ref[0, step * chunk : (step + 1) * chunk, :] = (SCALING * dq[step]).astype(BF16)


def attend_back(queries, keys, values, grads, context, probs, bias_width, chunk=512):
    seqs, count, width = queries.shape
    block = pl.BlockSpec((1, count, LANES), lambda p, s: (s, 0, p))
    turned = pl.BlockSpec((LANES, count), lambda p, s: (p, s))
    return pl.pallas_call(
        functools.partial(attend_back_kernel, chunk=chunk),
        grid=(width // LANES, seqs),
        in_specs=[block] * 5
        + [pl.BlockSpec((1, 2, count, count), lambda p, s: (s, p, 0, 0))],
        out_specs=[
            block,
            turned,
            turned,
            pl.BlockSpec((2, LANES, bias_width), lambda p, s: (p, 0, 0)),
        ],
        out_shape=[
            jax.ShapeDtypeStruct(queries.shape, BF16),
            jax.ShapeDtypeStruct((width, seqs * count), BF16),
            jax.ShapeDtypeStruct((width, seqs * count), BF16),
            jax.ShapeDtypeStruct((width // HEAD, LANES, bias_width), F32),
        ],
        compiler_params=pltpu.CompilerParams(vmem_limit_bytes=48 * 2**20),
        cost_estimate=pl.CostEstimate(
            flops=40 * seqs * count * count * width, bytes_accessed=40 * 2**20, transcendentals=0
        ),
    )(queries, keys, values, grads, context, probs)


def bits_of(size):
    return size.bit_length() - 1


def flip(axis, mask):
    size = lax.axis_size(axis)
    return [(index, index ^ mask) for index in range(size)]


def swap_blk(values):
    return lax.ppermute(values, "blk", flip("blk", 1))


def pick(values, index, axis):
    return lax.dynamic_index_in_dim(values, index, axis, keepdims=False)


class Shares:
    def __init__(self, grad):
        self.size = lax.axis_size("dp")
        self.left = list(range(bits_of(self.size)))[::-1]
        self.parts = grad.reshape((self.size, grad.shape[0] // self.size, grad.shape[1]))

    def halve(self, bit):
        place = self.left.index(bit)
        after = len(self.left) - place - 1
        shape = self.parts.shape[1:]
        split = self.parts.reshape((2**place, 2, 2**after) + shape)
        mine = (lax.axis_index("dp") >> bit) & 1
        sent = lax.ppermute(pick(split, 1 - mine, 1), "dp", flip("dp", 1 << bit))
        summed = pick(split, mine, 1).astype(F32) + sent.astype(F32)
        self.left.pop(place)
        self.parts = summed.astype(BF16).reshape((2 ** len(self.left),) + shape)

    def finish(self):
        own = self.parts[0]
        return own.astype(F32) + swap_blk(own).astype(F32)


def orders(size):
    rest = list(range(1, bits_of(size)))
    return rest, rest[1:2] + rest[:1] + rest[2:]


def reduce_shares(grad, order):
    shares = Shares(grad)
    for bit in ([0] if shares.left else []) + order:
        shares.halve(bit)
    return shares.finish()


def sum_everywhere(values):
    for bit in range(bits_of(lax.axis_size("dp"))):
        values = values + lax.ppermute(values, "dp", flip("dp", 1 << bit))
    return values + swap_blk(values)


def normalize(values):
    inverse = lax.rsqrt(jnp.mean(values * values, axis=-1, keepdims=True) + EPSILON)
    return values * inverse, inverse


def norm_back(normed, inverse, upstream):
    return inverse * (upstream - normed * jnp.mean(upstream * normed, axis=-1, keepdims=True))


def gather_rows(values, own):
    seqs = values.shape[0] // 2
    kept = lax.dynamic_slice_in_dim(values, own * seqs, seqs, 0)
    got = swap_blk(lax.dynamic_slice_in_dim(values, (1 - own) * seqs, seqs, 0))
    return jnp.where(
        own == 0, jnp.concatenate([kept, got], axis=1), jnp.concatenate([got, kept], axis=1)
    )


def return_rows(values, own):
    rows = values.shape[1] // 2
    kept = lax.dynamic_slice_in_dim(values, own * rows, rows, 1)
    got = swap_blk(lax.dynamic_slice_in_dim(values, (1 - own) * rows, rows, 1))
    return jnp.where(
        own == 0, jnp.concatenate([kept, got], axis=0), jnp.concatenate([got, kept], axis=0)
    )


def body(
    hidden,
    lengths,
    flags,
    buckets,
    g_attn,
    w_query,
    w_key,
    w_value,
    w_out,
    g_ffn,
    w_in,
    w_ffn_out,
    bias_table,
    cotangent,
):
    own = lax.axis_index("blk")
    size = lax.axis_size("dp")
    order_y, order_z = orders(size)
    width = hidden.shape[2]
    seqs = hidden.shape[0] // 2
    count = hidden.shape[1] * 2
    tokens = seqs * count
    buckets_used = bias_table.shape[0]
    heads = bias_table.shape[1]
    bias_width = 2 * count - LANES
    length = 2 * count

    with jax.named_scope("exchange_in"):
        inputs = gather_rows(hidden, own).reshape(tokens, width).astype(F32)
        upstream_low = gather_rows(cotangent, own).reshape(tokens, width)
        valid_all = jnp.where(flags == 1, lengths[:, 1], lengths[:, 0])
        valid = lax.dynamic_slice_in_dim(valid_all, own * seqs, seqs, 0)

    with jax.named_scope("bias"):
        one_hot = (
            buckets[None, :] == jnp.arange(buckets_used, dtype=jnp.int32)[:, None]
        ).astype(F32)
        one_hot = jnp.pad(one_hot, ((0, 0), (0, length - buckets.shape[0])))
        vector = lax.dot_general(
            bias_table * LOG2E,
            one_hot,
            (((0,), (0,)), ((), ())),
            precision=lax.Precision.HIGHEST,
        )
        bias = expand_bias(jnp.roll(vector, -(LANES - 1), axis=1), bias_width)

    with jax.named_scope("project"):
        normed_one, inverse_one = normalize(inputs)
        attn_in = (normed_one * g_attn).astype(BF16)
        queries = (dot(attn_in, w_query, 1, 0) * (SCALING * LOG2E)).astype(BF16)
        keys = dot(attn_in, w_key, 1, 0).astype(BF16)
        values = dot(attn_in, w_value, 1, 0).astype(BF16)
        shape = (seqs, count, width)
        queries, keys, values = (v.reshape(shape) for v in (queries, keys, values))

    with jax.named_scope("attend"):
        context_seq, probs = attend(queries, keys, values, bias, valid)
        context = context_seq.reshape(tokens, width)

    with jax.named_scope("ffn"):
        mixed = inputs + dot(context, w_out, 1, 0)
        normed_two, inverse_two = normalize(mixed)
        ffn_in = (normed_two * g_ffn).astype(BF16)
        pre = dot(ffn_in, w_in, 1, 0)
        grad_act = dot(upstream_low, w_ffn_out, 1, 1)
        below = 0.5 + 0.5 * lax.erf(pre * 0.7071067811865476)
        density = jnp.exp(-0.5 * pre * pre) * 0.3989422804014327
        act = (pre * below).astype(BF16)
        grad_pre = (grad_act * (below + pre * density)).astype(BF16)

    with jax.named_scope("ffn_weights"):
        grad_ffn_out = reduce_shares(dot(act, upstream_low, 0, 0).astype(BF16), order_y)
        grad_in = reduce_shares(dot(ffn_in, grad_pre, 0, 0).astype(BF16), order_z)

    with jax.named_scope("output"):
        layer_out = (mixed + dot(act, w_ffn_out, 1, 0)).astype(BF16)
        output = return_rows(layer_out.reshape(shape), own)

    with jax.named_scope("ffn_back"):
        upstream = upstream_low.astype(F32)
        grad_ffn_norm = dot(grad_pre, w_in, 1, 1)
        grad_g_ffn = jnp.sum(grad_ffn_norm * normed_two, axis=0)
        grad_mid = upstream + norm_back(normed_two, inverse_two, grad_ffn_norm * g_ffn)
        grad_mid_low = grad_mid.astype(BF16)
        grad_context = dot(grad_mid_low, w_out, 1, 1).astype(BF16).reshape(shape)
        grad_out_w = reduce_shares(dot(context, grad_mid_low, 0, 0).astype(BF16), order_y)

    with jax.named_scope("attend_back"):
        grad_q, grad_k, grad_v, grad_bias = attend_back(
            queries, keys, values, grad_context, context_seq, probs, bias_width
        )
        grad_q = grad_q.reshape(tokens, width)

    with jax.named_scope("project_back"):
        grad_value_w = reduce_shares(dot(attn_in, grad_v, 0, 1).astype(BF16), order_z)
        grad_key_w = reduce_shares(dot(attn_in, grad_k, 0, 1).astype(BF16), order_y)
        grad_query_w = reduce_shares(dot(attn_in, grad_q, 0, 0).astype(BF16), order_z)
        grad_attn_norm = (
            dot(grad_q, w_query, 1, 1) + dot(grad_k, w_key, 0, 1) + dot(grad_v, w_value, 0, 1)
        )
        grad_g_attn = jnp.sum(grad_attn_norm * normed_one, axis=0)
        input_grad = grad_mid + norm_back(normed_one, inverse_one, grad_attn_norm * g_attn)
        input_grad = return_rows(input_grad.astype(BF16).reshape(shape), own)

    with jax.named_scope("small"):
        folded = fold_bias(grad_bias, length)
        table = lax.dot_general(
            one_hot, folded, (((1,), (1,)), ((), ())), precision=lax.Precision.HIGHEST
        )
        flat = jnp.concatenate([grad_g_attn, grad_g_ffn, table.reshape(-1)])
        flat = sum_everywhere(jnp.pad(flat, (0, -flat.shape[0] % 1024)).reshape(-1, LANES))
        flat = flat.reshape(-1)
        share = width // size
        place = lax.axis_index("dp") * share
        gain_attn = lax.dynamic_slice_in_dim(flat[:width], place, share)
        gain_ffn = lax.dynamic_slice_in_dim(flat[width : 2 * width], place, share)
        table = flat[2 * width : 2 * width + buckets_used * heads].reshape(buckets_used, heads)

    return (
        output,
        input_grad,
        gain_attn,
        grad_query_w,
        grad_key_w,
        grad_value_w,
        grad_out_w,
        gain_ffn,
        grad_in,
        grad_ffn_out,
        table,
    )


def solution(mesh):
    split = P("dp", "blk", None)
    rows = P("dp", None)
    in_specs = (split, rows, P("dp")) + (P(),) * 10 + (split,)
    out_specs = (split, split, P("dp")) + (rows,) * 4 + (P("dp"), rows, rows, P())
    return jax.shard_map(body, mesh=mesh, in_specs=in_specs, out_specs=out_specs, check_vma=False)
```

```python
import functools

import jax
import jax.numpy as jnp
from jax import lax
from jax.experimental import pallas as pl
from jax.experimental.pallas import tpu as pltpu
from jax.sharding import PartitionSpec as P

EPSILON = 1e-06
MASKED = -1000000000.0
SCALING = 0.125
LOG2E = 1.4426950408889634
LN2 = 0.6931471805599453
HEAD = 64
LANES = 128
BF16 = jnp.bfloat16
F32 = jnp.float32


def dot(left, right, left_dim, right_dim):
    return lax.dot_general(
        left, right, (((left_dim,), (right_dim,)), ((), ())), preferred_element_type=F32
    )


def in_hbm(values):
    return pltpu.with_memory_space_constraint(values, pltpu.HBM)


def hbm_shape(shape, dtype):
    return pltpu.HBM(shape, dtype)


def expand_kernel(vector_ref, out_ref):
    width = vector_ref.shape[2]
    for head in range(vector_ref.shape[0]):
        rows = jnp.broadcast_to(vector_ref[head], (LANES, width))
        moved = pltpu.roll(rows, 0, 1, stride=1, stride_axis=0)
        out_ref[head] = moved[:, : out_ref.shape[2]]


def expand_bias(vector, width):
    heads, length = vector.shape
    group = 4 if heads % 4 == 0 else 1
    return pl.pallas_call(
        expand_kernel,
        grid=(heads // group,),
        in_specs=[pl.BlockSpec((group, 1, length), lambda h: (h, 0, 0))],
        out_specs=pl.BlockSpec((group, LANES, width), lambda h: (h, 0, 0)),
        out_shape=jax.ShapeDtypeStruct((heads, LANES, width), F32),
    )(vector.reshape(heads, 1, length))


def fold_kernel(grad_ref, out_ref):
    width = grad_ref.shape[2]
    length = out_ref.shape[2]
    pad = jnp.zeros((8, length - width), F32)
    for head in range(grad_ref.shape[0]):
        total = jnp.zeros((8, length), F32)
        for start in range(0, LANES, 8):
            rows = jnp.concatenate([grad_ref[head, start : start + 8, :], pad], axis=1)
            total = total + pltpu.roll(rows, LANES - 8 - start, 1)
        folded = total[7:8]
        for row in range(7):
            folded = folded + pltpu.roll(total[row : row + 1], 7 - row, 1)
        out_ref[head] = jnp.broadcast_to(folded, (8, length))


def fold_bias(grad, length):
    heads, _, width = grad.shape
    group = 4 if heads % 4 == 0 else 1
    return pl.pallas_call(
        fold_kernel,
        grid=(heads // group,),
        in_specs=[pl.BlockSpec((group, LANES, width), lambda h: (h, 0, 0))],
        out_specs=pl.BlockSpec((group, 8, length), lambda h: (h, 0, 0)),
        out_shape=jax.ShapeDtypeStruct((heads, 8, length), F32),
        cost_estimate=pl.CostEstimate(flops=0, bytes_accessed=0, transcendentals=0),
    )(in_hbm(grad))[:, 0]


def attend_kernel(valid, q_ref, k_ref, v_ref, bias_ref, *refs, chunk, seq):
    out_ref, probs_ref = refs[-2:]
    limit = valid[seq]
    count = q_ref.shape[0]
    queries, keys, values = q_ref[...].astype(F32), k_ref[...].astype(F32), v_ref[...].astype(F32)
    lane = lax.broadcasted_iota(jnp.int32, (count, LANES), 1)
    row = lax.broadcasted_iota(jnp.int32, (count, LANES), 0)
    heads = []
    for head in range(2):
        mine = (lane // HEAD) == head
        extra = lane == (1 - head) * HEAD
        mask = jnp.where(extra & (row >= limit), MASKED, 0.0)
        heads.append(
            (
                jnp.where(mine, queries, jnp.where(extra, 1.0, 0.0)).astype(BF16),
                jnp.where(mine, keys, mask).astype(BF16),
                jnp.where(mine, values, 0.0).astype(BF16),
            )
        )
    for step in range(count // chunk):
        rows = slice(step * chunk, (step + 1) * chunk)
        total = None
        for head in range(2):
            q_head, k_head, v_head = heads[head]
            windows = [
                bias_ref[head, :, count - LANES * (1 + block) : 2 * count - LANES * (1 + block)]
                for block in range(step * chunk // LANES, (step + 1) * chunk // LANES)
            ]
            logits = dot(q_head[rows], k_head, 1, 1) + jnp.concatenate(windows, axis=0)
            top = jnp.max(logits, axis=1, keepdims=True)
            weights = jnp.exp2(logits - top)
            norm = jnp.sum(weights, axis=1, keepdims=True)
            probs = (weights * (1.0 / norm)).astype(BF16)
            probs_ref[head, rows, :] = probs
            part = dot(probs, v_head, 1, 0)
            total = part if total is None else total + part
        out_ref[rows, :] = total.astype(BF16)


def attend(queries, keys, values, bias, valid, seq, seqs, before, chunk=256):
    count, width = queries.shape
    block = pl.BlockSpec((count, LANES), lambda p, *_: (0, p))
    kept = [] if before is None else [before]
    return pl.pallas_call(
        functools.partial(attend_kernel, chunk=chunk, seq=seq),
        grid_spec=pltpu.PrefetchScalarGridSpec(
            num_scalar_prefetch=1,
            grid=(width // LANES,),
            in_specs=[
                block,
                block,
                block,
                pl.BlockSpec((2, LANES, bias.shape[2]), lambda p, *_: (p, 0, 0)),
            ]
            + [pl.BlockSpec(memory_space=pl.ANY)] * len(kept),
            out_specs=[
                pl.BlockSpec((count, LANES), lambda p, *_: (seq, p)),
                pl.BlockSpec((2, count, count), lambda p, *_: (p, 0, 0)),
            ],
        ),
        out_shape=[
            hbm_shape((seqs * count, width), BF16),
            hbm_shape((width // HEAD, count, count), BF16),
        ],
        input_output_aliases={5: 0} if kept else {},
        compiler_params=pltpu.CompilerParams(vmem_limit_bytes=16 * 2**20),
        cost_estimate=pl.CostEstimate(
            flops=32 * count * count * width, bytes_accessed=12 * 2**20, transcendentals=0
        ),
    )(valid, queries, keys, values, bias, *kept)


def store_shares(grad, core, sent_ref, kept_ref):
    count, rows = sent_ref.shape[:2]
    for group in range(count):
        even = grad[2 * group * rows : (2 * group + 1) * rows]
        odd = grad[(2 * group + 1) * rows : (2 * group + 2) * rows]
        sent_ref[group] = jnp.where(core == 0, odd, even).astype(BF16)
        kept_ref[group] = jnp.where(core == 0, even, odd).astype(BF16)


def attend_back_kernel(place, *refs, seqs, finish, resumed):
    refs = list(refs)

    def some(count):
        taken = refs[:count]
        del refs[:count]
        return taken

    q_refs, k_refs, v_refs, probs_refs = (some(seqs) for _ in range(4))
    attn_in_refs = some(seqs)
    grad_ref, ctx_ref, wq_ref, wk_ref, wv_ref = some(5)
    before_ref = some(1)[0] if resumed else None
    if finish:
        hidden_refs = some(seqs)
        mid_ref, gain_ref = some(2)
    bias_ref, sent_ref, kept_ref = some(3)
    if finish:
        in_kept_ref, in_sent_ref, grad_gain_ref, back_ref = some(4)
    else:
        (back_ref,) = some(1)
    core, own = place[0], place[1]
    count = q_refs[0].shape[0]
    lane = lax.broadcasted_iota(jnp.int32, (count, LANES), 1)

    @pl.when(pl.program_id(0) == 0)
    def _():
        back_ref[...] = before_ref[...] if resumed else jnp.zeros_like(back_ref)

    bias_ref[...] = jnp.zeros_like(bias_ref)
    weights = jnp.concatenate([wq_ref[...], wk_ref[...], wv_ref[...]], axis=1)
    weight_grad = None
    for seq in range(seqs):
        here = slice(seq * count, (seq + 1) * count)
        queries, keys, values = (r[seq][...].astype(F32) for r in (q_refs, k_refs, v_refs))
        grads = grad_ref[here, :]
        queries_t = jnp.transpose(queries).astype(BF16)
        grads_t = jnp.transpose(grads.astype(F32)).astype(BF16)
        products = grads.astype(F32) * ctx_ref[here, :].astype(F32)
        dq, dk, dv = None, [], []
        for head in range(2):
            mine = (lane // HEAD) == head
            rows = slice(head * HEAD, (head + 1) * HEAD)
            k_head = jnp.where(mine, keys, 0.0).astype(BF16)
            v_head = jnp.where(mine, values, 0.0).astype(BF16)
            delta = jnp.sum(jnp.where(mine, products, 0.0), axis=1, keepdims=True)
            probs = probs_refs[seq][head]
            grad_logits = probs.astype(F32) * (dot(grads, v_head, 1, 1) - delta)
            for block in range(count // LANES):
                start = count - LANES * (1 + block)
                bias_ref[head, :, start : start + count] += grad_logits[
                    block * LANES : (block + 1) * LANES
                ]
            low = grad_logits.astype(BF16)
            part = dot(low, k_head, 1, 0)
            dq = part if dq is None else dq + part
            dk.append(dot(queries_t[rows], low, 1, 0))
            dv.append(dot(grads_t[rows], probs, 1, 0))
        dk = jnp.transpose(jnp.concatenate(dk, axis=0))
        dv = jnp.transpose(jnp.concatenate(dv, axis=0))
        all_grads = jnp.concatenate(
            [(SCALING * dq).astype(BF16), (LN2 * dk).astype(BF16), dv.astype(BF16)], axis=1
        )
        back_ref[here, :] += dot(all_grads, weights, 1, 1)
        part = dot(attn_in_refs[seq][...], all_grads, 0, 0)
        weight_grad = part if weight_grad is None else weight_grad + part
    store_shares(weight_grad, core, sent_ref, kept_ref)

    if finish:

        @pl.when(pl.program_id(0) == pl.num_programs(0) - 1)
        def _():
            gain = gain_ref[...]
            half = count // 2
            grad_gain = jnp.zeros(gain.shape, F32)
            for seq in range(seqs):
                for out_ref, start in ((in_kept_ref, own * half), (in_sent_ref, (1 - own) * half)):
                    start = pl.multiple_of(start, half)
                    values = hidden_refs[seq][pl.ds(start, half), :].astype(F32)
                    inverse = lax.rsqrt(
                        jnp.mean(values * values, axis=1, keepdims=True) + EPSILON
                    )
                    normed = values * inverse
                    back = back_ref[pl.ds(seq * count + start, half), :]
                    grad_gain += jnp.sum(back * normed, axis=0, keepdims=True)
                    back = back * gain
                    mean = jnp.mean(back * normed, axis=1, keepdims=True)
                    mid = mid_ref[pl.ds(seq * count + start, half), :]
                    out_ref[seq] = (mid + inverse * (back - normed * mean)).astype(BF16)
            grad_gain_ref[...] = grad_gain


def attend_back(
    place, saved, attn_in, grads, context, w_query, w_key, w_value, bias_width, pairs, before, ends
):
    seqs = len(saved)
    count, width = saved[0][0].shape
    size = lax.axis_size("dp")
    rows = width // size
    first, last = pairs
    block = pl.BlockSpec((count, LANES), lambda p, *_: (0, first + p))
    tall = pl.BlockSpec((seqs * count, LANES), lambda p, *_: (0, first + p))
    weight = pl.BlockSpec((width, LANES), lambda p, *_: (0, first + p))
    probs = pl.BlockSpec((2, count, count), lambda p, *_: (first + p, 0, 0))
    shares = pl.BlockSpec((size // 2, rows, 3 * LANES), lambda p, *_: (0, 0, p))
    once = pl.Buffered(1)

    def whole(*shape):
        return pl.BlockSpec(shape, lambda p, *_: (0,) * len(shape), pipeline_mode=once)

    operands = [values[part] for part in range(4) for values in saved]
    specs = [block] * (3 * seqs) + [probs] * seqs
    operands += list(attn_in)
    specs += [whole(count, width)] * seqs
    operands += [grads, context, w_query, w_key, w_value]
    specs += [tall, tall, weight, weight, weight]
    if before is not None:
        operands.append(before)
        specs.append(whole(seqs * count, width))
    share = hbm_shape((size // 2, rows, 3 * LANES * (last - first)), BF16)
    out_shape = [
        hbm_shape((2 * (last - first), LANES, bias_width), F32),
        share,
        share,
    ]
    out_specs = [pl.BlockSpec((2, LANES, bias_width), lambda p, *_: (p, 0, 0)), shares, shares]
    scratch = []
    if ends is not None:
        hidden, grad_mid, gain = ends
        operands += list(hidden) + [grad_mid, gain.reshape(1, width)]
        specs += [whole(count, width)] * seqs + [whole(seqs * count, width), whole(1, width)]
        part = hbm_shape((seqs, count // 2, width), BF16)
        out_shape += [part, part, hbm_shape((1, width), F32)]
        out_specs += [whole(seqs, count // 2, width)] * 2 + [whole(1, width)]
        scratch = [pltpu.VMEM((seqs * count, width), F32)]
    else:
        out_shape.append(hbm_shape((seqs * count, width), F32))
        out_specs.append(whole(seqs * count, width))
    return pl.pallas_call(
        functools.partial(
            attend_back_kernel, seqs=seqs, finish=ends is not None, resumed=before is not None
        ),
        grid_spec=pltpu.PrefetchScalarGridSpec(
            num_scalar_prefetch=1,
            grid=(last - first,),
            in_specs=specs,
            out_specs=out_specs,
            scratch_shapes=scratch,
        ),
        out_shape=out_shape,
        compiler_params=pltpu.CompilerParams(vmem_limit_bytes=42 * 2**20),
        cost_estimate=pl.CostEstimate(flops=0, bytes_accessed=0, transcendentals=0),
    )(place, *[in_hbm(values) for values in operands])


def in_weight_kernel(place, ffn_in_ref, pre_ref, ctx_ref, low_ref, sent_ref, kept_ref):
    step = pl.program_id(0)
    ends = pl.num_programs(0) - 1

    @pl.when(step < ends)
    def _():
        store_shares(dot(ffn_in_ref[...], pre_ref[...], 0, 0), place[0], sent_ref, kept_ref)

    @pl.when(step == ends)
    def _():
        store_shares(dot(ctx_ref[...], low_ref[...], 0, 0), place[0], sent_ref, kept_ref)


def in_weights(place, ffn_in, grad_pre, context, grad_low):
    tokens, width = ffn_in.shape
    steps = grad_pre.shape[1] // width
    size = lax.axis_size("dp")
    whole = pl.BlockSpec((tokens, width), lambda j, *_: (0, 0), pipeline_mode=pl.Buffered(1))
    share = pl.BlockSpec((size // 2, width // size, width), lambda j, *_: (0, 0, j))
    return pl.pallas_call(
        in_weight_kernel,
        grid_spec=pltpu.PrefetchScalarGridSpec(
            num_scalar_prefetch=1,
            grid=(steps + 1,),
            in_specs=[
                whole,
                pl.BlockSpec((tokens, width), lambda j, *_: (0, jnp.minimum(j, steps - 1))),
                whole,
                whole,
            ],
            out_specs=[share, share],
        ),
        out_shape=[
            hbm_shape((size // 2, width // size, (steps + 1) * width), BF16)
        ]
        * 2,
        compiler_params=pltpu.CompilerParams(vmem_limit_bytes=32 * 2**20),
        cost_estimate=pl.CostEstimate(flops=0, bytes_accessed=0, transcendentals=0),
    )(place, in_hbm(ffn_in), grad_pre, in_hbm(context), in_hbm(grad_low))


def out_weight_kernel(place, act_ref, upstream_ref, sent_ref, kept_ref):
    store_shares(dot(act_ref[...], upstream_ref[...], 0, 0), place[0], sent_ref, kept_ref)


def out_weights(place, act, upstream):
    tokens, width = upstream.shape
    units = act.shape[1]
    size = lax.axis_size("dp")
    rows = units // size
    steps = units // width
    share = pl.BlockSpec((size // 2 // steps, rows, width), lambda j, *_: (j, 0, 0))
    return pl.pallas_call(
        out_weight_kernel,
        grid_spec=pltpu.PrefetchScalarGridSpec(
            num_scalar_prefetch=1,
            grid=(steps,),
            in_specs=[
                pl.BlockSpec((tokens, width), lambda j, *_: (0, j)),
                pl.BlockSpec((tokens, width), lambda j, *_: (0, 0), pipeline_mode=pl.Buffered(1)),
            ],
            out_specs=[share, share],
        ),
        out_shape=[hbm_shape((size // 2, rows, width), BF16)] * 2,
        compiler_params=pltpu.CompilerParams(vmem_limit_bytes=32 * 2**20),
        cost_estimate=pl.CostEstimate(flops=0, bytes_accessed=0, transcendentals=0),
    )(place, act, upstream)


def middle_kernel(
    context_ref,
    hidden_ref,
    upstream_ref,
    w_out_ref,
    gain_ref,
    w_in_ref,
    w_ffn_out_ref,
    act_ref,
    grad_pre_ref,
    ffn_in_ref,
    layer_out_ref,
    grad_mid_ref,
    grad_low_ref,
    grad_context_ref,
    grad_gain_ref,
    mixed_ref,
    total_ref,
    back_ref,
    *,
    chunk,
):
    tokens, width = mixed_ref.shape
    pieces = [slice(start, start + chunk) for start in range(0, tokens, chunk)]
    step = pl.program_id(0)
    gain = gain_ref[...]

    def inverse_of(mixed):
        return lax.rsqrt(jnp.mean(mixed * mixed, axis=1, keepdims=True) + EPSILON)

    @pl.when(step == 0)
    def _():
        for rows in pieces:
            mixed = hidden_ref[rows, :].astype(F32) + dot(context_ref[rows, :], w_out_ref[...], 1, 0)
            mixed_ref[rows, :] = mixed
            ffn_in_ref[rows, :] = (mixed * inverse_of(mixed) * gain).astype(BF16)
            total_ref[rows, :] = mixed
            back_ref[rows, :] = jnp.zeros((chunk, width), F32)

    for rows in pieces:
        pre = dot(ffn_in_ref[rows, :], w_in_ref[...], 1, 0)
        grad_act = dot(upstream_ref[rows, :], w_ffn_out_ref[...], 1, 1)
        below = 0.5 + 0.5 * lax.erf(pre * 0.7071067811865476)
        density = jnp.exp2(pre * pre * (-0.5 * LOG2E)) * 0.3989422804014327
        act = (pre * below).astype(BF16)
        grad_pre = (grad_act * (below + pre * density)).astype(BF16)
        act_ref[rows, :] = act
        grad_pre_ref[rows, :] = grad_pre
        total_ref[rows, :] += dot(act, w_ffn_out_ref[...], 1, 0)
        back_ref[rows, :] += dot(grad_pre, w_in_ref[...], 1, 1)

    @pl.when(step == pl.num_programs(0) - 1)
    def _():
        grad_gain = jnp.zeros((1, width), F32)
        for rows in pieces:
            layer_out_ref[rows, :] = total_ref[rows, :].astype(BF16)
            mixed = mixed_ref[rows, :]
            inverse = inverse_of(mixed)
            normed = mixed * inverse
            back = back_ref[rows, :]
            grad_gain += jnp.sum(back * normed, axis=0, keepdims=True)
            back = back * gain
            mean = jnp.mean(back * normed, axis=1, keepdims=True)
            grad = upstream_ref[rows, :].astype(F32) + inverse * (back - normed * mean)
            grad_mid_ref[rows, :] = grad
            low = grad.astype(BF16)
            grad_low_ref[rows, :] = low
            grad_context_ref[rows, :] = dot(low, w_out_ref[...], 1, 1).astype(BF16)
        grad_gain_ref[...] = grad_gain


def middle(context, hidden, upstream, w_out, gain, w_in, w_ffn_out, columns=512, chunk=256):
    tokens, width = context.shape
    units = w_in.shape[1]
    once = pl.Buffered(1)
    whole = pl.BlockSpec((tokens, width), lambda j: (0, 0), pipeline_mode=once)
    row = pl.BlockSpec((1, width), lambda j: (0, 0), pipeline_mode=once)
    piece = pl.BlockSpec((tokens, columns), lambda j: (0, j))
    low = hbm_shape((tokens, width), BF16)
    return pl.pallas_call(
        functools.partial(middle_kernel, chunk=chunk),
        grid=(units // columns,),
        in_specs=[
            whole,
            whole,
            whole,
            pl.BlockSpec((width, width), lambda j: (0, 0), pipeline_mode=once),
            row,
            pl.BlockSpec((width, columns), lambda j: (0, j)),
            pl.BlockSpec((columns, width), lambda j: (j, 0)),
        ],
        out_specs=[piece, piece, whole, whole, whole, whole, whole, row],
        out_shape=[
            jax.ShapeDtypeStruct((tokens, units), BF16),
            jax.ShapeDtypeStruct((tokens, units), BF16),
            low,
            low,
            hbm_shape((tokens, width), F32),
            low,
            low,
            jax.ShapeDtypeStruct((1, width), F32),
        ],
        scratch_shapes=[pltpu.VMEM((tokens, width), F32)] * 3,
        compiler_params=pltpu.CompilerParams(vmem_limit_bytes=40 * 2**20),
        cost_estimate=pl.CostEstimate(
            flops=8 * tokens * width * units, bytes_accessed=30 * 2**20, transcendentals=0
        ),
    )(context, hidden, upstream, w_out, gain.reshape(1, width), w_in, w_ffn_out)


def bits_of(size):
    return size.bit_length() - 1


def flip(axis, mask):
    size = lax.axis_size(axis)
    return [(index, index ^ mask) for index in range(size)]


def swap_blk(values):
    return lax.ppermute(values, "blk", flip("blk", 1))


def pick(values, index, axis):
    return lax.dynamic_index_in_dim(values, index, axis, keepdims=False)


def part_of(values, index, axis):
    share = values.shape[axis] // 2
    return lax.dynamic_slice_in_dim(values, index * share, share, axis)


def in_order(own, kept, got, axis):
    share = kept.shape[axis]
    shape = kept.shape[:axis] + (2 * share,) + kept.shape[axis + 1 :]
    both = lax.dynamic_update_slice_in_dim(jnp.zeros(shape, kept.dtype), kept, own * share, axis)
    return lax.dynamic_update_slice_in_dim(both, got, (1 - own) * share, axis)


def join(parts, axis):
    return parts[0] if len(parts) == 1 else jnp.concatenate(parts, axis)


class Shares:
    def __init__(self, sent, kept, order):
        self.left = list(range(1, bits_of(lax.axis_size("dp"))))[::-1]
        self.order = [0] + order
        self.sent, self.kept = sent, kept
        self.by_column = False
        self.got = None
        self.pairs = []

    def joined(self, slices, axis):
        parts = [slices(kept).astype(F32) + slices(got).astype(F32) for kept, got in self.pairs]
        return join([part.astype(BF16) for part in parts], axis)

    def send(self):
        if not self.order or self.got is not None:
            return
        stage = self.order[0]
        own = lax.axis_index("blk")
        if stage == 0:
            self.got = lax.ppermute(self.sent, "dp", flip("dp", 1))
        elif stage == "last":
            self.kept = self.joined(lambda part: part[0], 1)
            self.got = swap_blk(self.kept)
        elif stage == "blk":
            self.widths = [kept.shape[2] // 2 for kept, _ in self.pairs]
            sent = self.joined(lambda part: part_of(part, 1 - own, 2), 2)
            self.got = swap_blk(sent)
            self.kept = self.joined(lambda part: part_of(part, own, 2), 2)
        else:
            place = self.left.index(stage)
            after = len(self.left) - place - 1
            mine = (lax.axis_index("dp") >> stage) & 1
            self.left.pop(place)

            def half(index):
                def of(part):
                    split = part.reshape((2**place, 2, 2**after) + part.shape[1:])
                    return pick(split, index, 1).reshape((2 ** (place + after),) + part.shape[1:])

                return of

            self.got = lax.ppermute(self.joined(half(1 - mine), 2), "dp", flip("dp", 1 << stage))
            self.kept = self.joined(half(mine), 2)

    def receive(self):
        stage = self.order.pop(0)
        if stage == "last":
            if self.by_column:
                total = in_order(lax.axis_index("blk"), self.kept, self.got, 1).astype(F32)
                half = total.shape[1] // 2
                parts, start = [], 0
                for width in self.widths:
                    parts.append(total[:, start : start + width])
                    parts.append(total[:, half + start : half + start + width])
                    start += width
                self.total = jnp.concatenate(parts, axis=1)
            else:
                self.total = self.kept.astype(F32) + self.got.astype(F32)
        self.by_column = self.by_column or stage == "blk"
        self.pairs = [(self.kept, self.got)]
        self.got = None

    def take_over(self, other):
        rows = self.pairs[0][0].shape[1]
        for kept, got in other.pairs:
            for start in range(0, kept.shape[1], rows):
                self.pairs.append((kept[:, start : start + rows], got[:, start : start + rows]))
        other.order = []


def receive(shares, *values):
    shares = [share for share in shares if share.order]
    tied = lax.optimization_barrier(tuple(share.got for share in shares) + values)
    for share, got in zip(shares, tied):
        share.got = got
        share.receive()
    values = tied[len(shares) :]
    return values if len(values) > 1 else values[0]


def normalize(values):
    inverse = lax.rsqrt(jnp.mean(values * values, axis=-1, keepdims=True) + EPSILON)
    return values * inverse, inverse


def norm_back(normed, inverse, upstream):
    return inverse * (upstream - normed * jnp.mean(upstream * normed, axis=-1, keepdims=True))


def body(
    hidden,
    lengths,
    flags,
    buckets,
    g_attn,
    w_query,
    w_key,
    w_value,
    w_out,
    g_ffn,
    w_in,
    w_ffn_out,
    bias_table,
    cotangent,
):
    own = lax.axis_index("blk")
    size = lax.axis_size("dp")
    rest = list(range(1, bits_of(size)))
    first, second, later = rest[:1], rest[1:2], rest[2:]
    width = hidden.shape[2]
    seqs = hidden.shape[0] // 2
    count = hidden.shape[1] * 2
    tokens = seqs * count
    each = range(seqs)
    buckets_used, heads = bias_table.shape
    bias_width = 2 * count - LANES
    length = 2 * count

    def give_back(values):
        return part_of(values, own, 1), swap_blk(part_of(values, 1 - own, 1))

    with jax.named_scope("exchange_in"):
        def take(values, start, number):
            kept = lax.dynamic_slice_in_dim(values, own * seqs + start, number, 0)
            return kept, lax.dynamic_slice_in_dim(values, (1 - own) * seqs + start, number, 0)

        hidden_parts = []
        for seq in each:
            kept, sent = take(hidden, seq, 1)
            if seq > 0:
                sent, hidden_parts[-1][1] = lax.optimization_barrier((sent, hidden_parts[-1][1]))
            hidden_parts.append([kept, swap_blk(sent)])
        valid_all = jnp.where(flags == 1, lengths[:, 1], lengths[:, 0])
        valid = lax.dynamic_slice_in_dim(valid_all, own * seqs, seqs, 0)
        place = jnp.stack([lax.axis_index("dp") & 1, own]).astype(jnp.int32)

    with jax.named_scope("bias"):
        one_hot = (
            buckets[None, :] == jnp.arange(buckets_used, dtype=jnp.int32)[:, None]
        ).astype(F32)
        one_hot = jnp.pad(one_hot, ((0, 0), (0, length - buckets.shape[0])))
        vector = lax.dot_general(
            bias_table * LOG2E,
            one_hot,
            (((0,), (0,)), ((), ())),
            precision=lax.Precision.HIGHEST,
        )
        bias = expand_bias(jnp.roll(vector, -(LANES - 1), axis=1), bias_width)

    context = None
    saved, hidden_seq, attn_in_seq = [], [], []
    for seq in each:
        with jax.named_scope("project"):
            kept, got = hidden_parts[seq]
            if seq > 0:
                got, context = lax.optimization_barrier((got, context))
            if seq == seqs - 1:
                upstream_kept, sent = take(cotangent, 0, seqs)
                sent, got = lax.optimization_barrier((sent, got))
                upstream_got = swap_blk(sent)
            hidden_seq.append(in_order(own, kept, got, 1)[0])
            normed, _ = normalize(hidden_seq[seq].astype(F32))
            attn_in = (normed * g_attn).astype(BF16)
            queries = (dot(attn_in, w_query, 1, 0) * (SCALING * LOG2E)).astype(BF16)
            keys = dot(attn_in, w_key, 1, 0).astype(BF16)
            values = dot(attn_in, w_value, 1, 0).astype(BF16)
            attn_in_seq.append(attn_in)
        with jax.named_scope("attend"):
            context, probs = attend(queries, keys, values, bias, valid, seq, seqs, context)
            saved.append((queries, keys, values, probs))

    with jax.named_scope("middle"):
        upstream = in_order(own, upstream_kept, upstream_got, 1).reshape(tokens, width)
        act, grad_pre, ffn_in, layer_out, grad_mid, grad_low, grad_context, grad_g_ffn = middle(
            context, jnp.concatenate(hidden_seq, axis=0), upstream, w_out, g_ffn, w_in, w_ffn_out
        )

    with jax.named_scope("output"):
        output_kept, output_got = give_back(layer_out.reshape(seqs, count, width))

    with jax.named_scope("ffn_weights"):
        in_shares = Shares(
            *in_weights(place, ffn_in, grad_pre, context, grad_low), second + first
        )
        in_shares.send()
        sent, kept = out_weights(place, act, upstream)
        sent, kept, grad_context = receive([in_shares], sent, kept, grad_context)
        ffn_out_shares = Shares(sent, kept, first + second)
        ffn_out_shares.send()
        in_shares.send()
        grad_context = receive([ffn_out_shares], grad_context)
        ffn_out_shares.send()

    with jax.named_scope("attend_back"):
        pairs = width // LANES
        middle_pair = 2 * pairs // 3
        weights = (w_query, w_key, w_value)
        bias_one, sent, kept, before = attend_back(
            place, saved, attn_in_seq, grad_context, context, *weights, bias_width,
            (0, middle_pair), None, None,
        )
        one_shares = Shares(sent, kept, first + second)
        one_shares.send()
        before, grad_context = receive([in_shares, ffn_out_shares], before, grad_context)
        in_shares.send()
        ffn_out_shares.send()
        bias_two, sent, kept, input_kept, input_sent, grad_g_attn = attend_back(
            place, saved, attn_in_seq, grad_context, context, *weights, bias_width,
            (middle_pair, pairs), before, (hidden_seq, grad_mid, g_attn),
        )
        two_shares = Shares(sent, kept, second + first)
        two_shares.send()
        bias_one, bias_two, input_sent, output_got = receive(
            [one_shares, in_shares, ffn_out_shares], bias_one, bias_two, input_sent, output_got
        )
        input_got = swap_blk(input_sent)
        in_shares.take_over(ffn_out_shares)
        in_shares.order = ["blk"] + later + ["last"]

    with jax.named_scope("rounds"):
        chains = [one_shares, two_shares, in_shares]
        for shares in chains:
            shares.send()
        folded = fold_bias(bias_one, length), fold_bias(bias_two, length)
        folded = jnp.concatenate(receive(chains, *folded), axis=0)

    with jax.named_scope("small"):
        table = lax.dot_general(
            one_hot, folded, (((1,), (1,)), ((), ())), precision=lax.Precision.HIGHEST
        )
        flat = jnp.concatenate([grad_g_attn[0], grad_g_ffn[0], table.reshape(-1)])
        flat = jnp.pad(flat, (0, -flat.shape[0] % 1024)).reshape(-1, LANES)
        small_bits = list(range(bits_of(size))) + ["blk"]

    with jax.named_scope("rounds"):
        joined = False
        while any(shares.order for shares in chains) or small_bits:
            for shares in chains:
                shares.send()
            if small_bits:
                bit = small_bits.pop(0)
                small_got = (
                    swap_blk(flat)
                    if bit == "blk"
                    else lax.ppermute(flat, "dp", flip("dp", 1 << bit))
                )
                flat, small_got = receive(chains, flat, small_got)
                flat = flat + small_got
            else:
                flat = receive(chains, flat)
            if not joined and not one_shares.order and not two_shares.order:
                one_shares.take_over(two_shares)
                one_shares.order = later + ["last"]
                joined = True
    pieces = jnp.split(one_shares.total, 3 * pairs, axis=1)
    grad_query_w, grad_key_w, grad_value_w = (
        jnp.concatenate(pieces[part::3], axis=1) for part in range(3)
    )
    units = w_in.shape[1]
    done = in_shares.total
    grad_in, grad_out_w = done[:, :units], done[:, units : units + width]
    grad_ffn_out = jnp.concatenate(
        [done[:, start : start + width] for start in range(units + width, done.shape[1], width)], 0
    )
    with jax.named_scope("output"):
        output = in_order(own, output_kept, output_got, 0)
        input_grad = in_order(own, input_kept, input_got, 0)

    with jax.named_scope("small"):
        flat = flat.reshape(-1)
        share = width // size
        at = lax.axis_index("dp") * share
        gain_attn = lax.dynamic_slice_in_dim(flat[:width], at, share)
        gain_ffn = lax.dynamic_slice_in_dim(flat[width : 2 * width], at, share)
        table = flat[2 * width : 2 * width + buckets_used * heads].reshape(buckets_used, heads)

    return (
        output,
        input_grad,
        gain_attn,
        grad_query_w,
        grad_key_w,
        grad_value_w,
        grad_out_w,
        gain_ffn,
        grad_in,
        grad_ffn_out,
        table,
    )


def solution(mesh):
    split = P("dp", "blk", None)
    rows = P("dp", None)
    in_specs = (split, rows, P("dp")) + (P(),) * 10 + (split,)
    out_specs = (split, split, P("dp")) + (rows,) * 4 + (P("dp"), rows, rows, P())
    return jax.shard_map(body, mesh=mesh, in_specs=in_specs, out_specs=out_specs, check_vma=False)
```

```python
import functools

import jax
import jax.numpy as jnp
from jax import lax
from jax.experimental import pallas as pl
from jax.experimental.pallas import tpu as pltpu
from jax.sharding import PartitionSpec as P

EPSILON = 1e-06
MASKED = -1000000000.0
SCALING = 0.125
LOG2E = 1.4426950408889634
LN2 = 0.6931471805599453
HEAD = 64
LANES = 128
VMEM_LIMIT = 32 * 2**20
BF16 = jnp.bfloat16
F32 = jnp.float32


def dot(left, right, left_dim, right_dim):
    return lax.dot_general(
        left, right, (((left_dim,), (right_dim,)), ((), ())), preferred_element_type=F32
    )


RESIDENT = pl.BlockSpec(memory_space=pltpu.VMEM)


def in_hbm(values):
    return pltpu.with_memory_space_constraint(values, pltpu.HBM)


def resident(*values):
    return [pltpu.with_memory_space_constraint(v, pltpu.VMEM) for v in values]


def expand_kernel(vector_ref, out_ref):
    group, _, width = vector_ref.shape
    for head in range(group):
        rows = jnp.broadcast_to(vector_ref[head], (LANES, width))
        moved = pltpu.roll(rows, 0, 1, stride=1, stride_axis=0)
        out_ref[head] = moved[:, : out_ref.shape[2]]


def expand_bias(vector, width):
    heads, length = vector.shape
    group = 4 if heads % 4 == 0 else 1
    return pl.pallas_call(
        expand_kernel,
        grid=(heads // group,),
        in_specs=[pl.BlockSpec((group, 1, length), lambda h: (h, 0, 0))],
        out_specs=pl.BlockSpec((group, LANES, width), lambda h: (h, 0, 0)),
        out_shape=jax.ShapeDtypeStruct((heads, LANES, width), F32),
        compiler_params=pltpu.CompilerParams(vmem_limit_bytes=VMEM_LIMIT),
    )(vector.reshape(heads, 1, length))


def fold_kernel(grad_ref, out_ref):
    width = grad_ref.shape[2]
    length = out_ref.shape[2]
    pad = jnp.zeros((8, length - width), F32)
    for head in range(grad_ref.shape[0]):
        total = jnp.zeros((8, length), F32)
        for start in range(0, LANES, 8):
            rows = jnp.concatenate([grad_ref[head, start : start + 8, :], pad], axis=1)
            total = total + pltpu.roll(rows, LANES - 8 - start, 1)
        folded = total[7:8]
        for row in range(7):
            folded = folded + pltpu.roll(total[row : row + 1], 7 - row, 1)
        out_ref[head] = jnp.broadcast_to(folded, (8, length))


def fold_bias(grad, length):
    heads, _, width = grad.shape
    group = 4 if heads % 4 == 0 else 1
    return pl.pallas_call(
        fold_kernel,
        grid=(heads // group,),
        in_specs=[pl.BlockSpec((group, LANES, width), lambda h: (h, 0, 0))],
        out_specs=pl.BlockSpec((group, 8, length), lambda h: (h, 0, 0)),
        out_shape=jax.ShapeDtypeStruct((heads, 8, length), F32),
        compiler_params=pltpu.CompilerParams(vmem_limit_bytes=VMEM_LIMIT),
        cost_estimate=pl.CostEstimate(flops=0, bytes_accessed=0, transcendentals=0),
    )(in_hbm(grad))[:, 0]


def attend_kernel(
    valid, q_ref, k_ref, v_ref, bias_ref, out_ref, copy_ref, weights_ref, inverse_ref, *, chunk, seq
):
    limit = valid[seq]
    count = q_ref.shape[0]
    pair = pl.program_id(0)
    columns = pl.ds(pl.multiple_of(pair * LANES, LANES), LANES)
    queries, keys, values = (ref[...].astype(F32) for ref in (q_ref, k_ref, v_ref))
    lane = lax.broadcasted_iota(jnp.int32, (count, LANES), 1)
    row = lax.broadcasted_iota(jnp.int32, (count, LANES), 0)
    heads = []
    for head in range(2):
        mine = (lane // HEAD) == head
        extra = lane == (1 - head) * HEAD
        mask = jnp.where(extra & (row >= limit), MASKED, 0.0)
        heads.append(
            (
                jnp.where(mine, queries, jnp.where(extra, 1.0, 0.0)).astype(BF16),
                jnp.where(mine, keys, mask).astype(BF16),
                jnp.where(mine, values, 1.0).astype(BF16),
            )
        )
    first = lax.broadcasted_iota(jnp.int32, (chunk, LANES), 1) < HEAD
    units = [(step, head) for step in range(count // chunk) for head in range(2)]

    def scores(unit):
        step, head = unit
        rows = slice(step * chunk, (step + 1) * chunk)
        windows = [
            bias_ref[head, :, count - LANES * (1 + block) : 2 * count - LANES * (1 + block)]
            for block in range(step * chunk // LANES, (step + 1) * chunk // LANES)
        ]
        return dot(heads[head][0][rows], heads[head][1], 1, 1) + jnp.concatenate(windows, axis=0)

    ahead = 2
    logits = {unit: scores(unit) for unit in units[:ahead]}
    sums = {}
    for place, unit in enumerate(units):
        step, head = unit
        rows = slice(step * chunk, (step + 1) * chunk)
        if place + ahead < len(units):
            logits[units[place + ahead]] = scores(units[place + ahead])
        top = jnp.max(logits[unit], axis=1, keepdims=True)
        weights = jnp.exp2(logits[unit] - top).astype(BF16)
        weights_ref[head, rows, :] = weights
        sums[unit] = dot(weights, heads[head][2], 1, 0)
        if head == 1:
            one, two = sums[step, 0], sums[step, 1]
            inverse = 1.0 / pltpu.roll(jnp.where(first, two, one), HEAD, 1)
            inverse_ref[rows, :] = inverse
            context = (jnp.where(first, one, two) * inverse).astype(BF16)
            out_ref[rows, columns] = context
            copy_ref[rows, :] = context


def attend(queries, keys, values, bias, valid, seq, chunk=256):
    count, width = queries.shape
    block = pl.BlockSpec((count, LANES), lambda p, *_: (0, p))
    return pl.pallas_call(
        functools.partial(attend_kernel, chunk=chunk, seq=seq),
        grid_spec=pltpu.PrefetchScalarGridSpec(
            num_scalar_prefetch=1,
            grid=(width // LANES,),
            in_specs=[
                block,
                block,
                block,
                pl.BlockSpec((2, LANES, bias.shape[2]), lambda p, *_: (p, 0, 0)),
            ],
            out_specs=[
                RESIDENT,
                block,
                pl.BlockSpec((2, count, count), lambda p, *_: (p, 0, 0)),
                block,
            ],
        ),
        out_shape=[
            pltpu.VMEM((count, width), BF16),
            pltpu.HBM((count, width), BF16),
            pltpu.HBM((width // HEAD, count, count), BF16),
            pltpu.HBM((count, width), F32),
        ],
        compiler_params=pltpu.CompilerParams(vmem_limit_bytes=VMEM_LIMIT),
        cost_estimate=pl.CostEstimate(
            flops=32 * count * count * width, bytes_accessed=12 * 2**20, transcendentals=0
        ),
    )(valid, queries, keys, values, bias)


def store_shares(grad, core, sent_ref, kept_ref, start=0):
    count, rows = sent_ref.shape[:2]
    columns = slice(start, start + grad.shape[1])
    grad = grad.astype(BF16) if rows % 16 == 0 else grad
    for group in range(count):
        even = grad[2 * group * rows : (2 * group + 1) * rows]
        odd = grad[(2 * group + 1) * rows : (2 * group + 2) * rows]
        sent_ref[group, :, columns] = jnp.where(core == 0, odd, even).astype(BF16)
        kept_ref[group, :, columns] = jnp.where(core == 0, even, odd).astype(BF16)


def attend_back_kernel(scalars, *refs, seqs, steps, finish):
    refs = list(refs)

    def some(count):
        taken = refs[:count]
        del refs[:count]
        return taken

    q_refs, k_refs, v_refs, weights_refs, inverse_refs = (some(seqs) for _ in range(5))
    attn_in_refs = some(seqs)
    ctx_refs = some(seqs)
    grad_ref, wq_ref, wk_ref, wv_ref = some(4)
    if finish:
        before_ref, hidden_ref, mid_ref, gain_ref = some(4)
    bias_ref, sent_ref, kept_ref = some(3)
    if finish:
        in_kept_ref, in_sent_ref, grad_gain_ref, back_ref = some(4)
    else:
        out_ref, back_ref = some(2)
    core, own = scalars[0], scalars[1]
    count = q_refs[0].shape[0]
    lane = lax.broadcasted_iota(jnp.int32, (count, LANES), 1)

    step = pl.program_id(0)

    @pl.when(step == 0)
    def _():
        back_ref[...] = jnp.zeros_like(back_ref)

    @pl.when(step < steps)
    def _():
        bias_ref[...] = jnp.zeros_like(bias_ref)
        projections = jnp.concatenate([wq_ref[...], wk_ref[...], wv_ref[...]], axis=1)
        units = [(seq, head) for seq in range(seqs) for head in range(2)]
        loaded, scored, low_grads, parts = {}, {}, {}, {}

        def load(seq):
            here = slice(seq * count, (seq + 1) * count)
            queries, keys, values = (
                r[seq][...].astype(F32) for r in (q_refs, k_refs, v_refs)
            )
            grads = grad_ref[here, :].astype(F32) * inverse_refs[seq][...]
            products = grads * ctx_refs[seq][...].astype(F32)
            turned = jnp.transpose(queries).astype(BF16), jnp.transpose(grads).astype(BF16)
            loaded[seq] = keys, values, grads, products, turned

        def score(unit):
            seq, head = unit
            if head == 0:
                load(seq)
            _, values, grads, products, _ = loaded[seq]
            mine = (lane // HEAD) == head
            other = (1 - head) * HEAD
            extra = (lane == other) | (lane == other + 1)
            v_head = jnp.where(mine, values, jnp.where(extra, 1.0, 0.0)).astype(BF16)
            delta = jnp.sum(jnp.where(mine, products, 0.0), axis=1, keepdims=True)
            high = delta.astype(BF16).astype(F32)
            spread = jnp.where(lane == other, -high, jnp.where(extra, high - delta, 0.0))
            g_head = jnp.where(mine, grads, spread).astype(BF16)
            scored[unit] = dot(g_head, v_head, 1, 1)

        def weigh(unit):
            seq, head = unit
            grad_logits = weights_refs[seq][head].astype(F32) * scored[unit]
            blocks = count // LANES
            for tile in range(2 * blocks - 1):
                bias_ref[head, :, tile * LANES : (tile + 1) * LANES] += sum(
                    grad_logits[
                        block * LANES : (block + 1) * LANES,
                        (tile + 1 + block - blocks) * LANES : (tile + 2 + block - blocks) * LANES,
                    ]
                    for block in range(blocks)
                    if 0 <= tile + 1 + block - blocks < blocks
                )
            low_grads[unit] = grad_logits.astype(BF16)

        def multiply(unit):
            seq, head = unit
            keys, _, _, _, (queries_t, grads_t) = loaded[seq]
            rows = slice(head * HEAD, (head + 1) * HEAD)
            k_head = jnp.where((lane // HEAD) == head, keys, 0.0).astype(BF16)
            low = low_grads[unit]
            parts[unit] = (
                dot(low, k_head, 1, 0),
                dot(queries_t[rows], low, 1, 0),
                dot(grads_t[rows], weights_refs[seq][head], 1, 0),
            )

        def project(seq):
            here = slice(seq * count, (seq + 1) * count)
            one, two = parts[seq, 0], parts[seq, 1]
            dk = jnp.transpose(jnp.concatenate([one[1], two[1]], axis=0))
            dv = jnp.transpose(jnp.concatenate([one[2], two[2]], axis=0))
            all_grads = jnp.concatenate(
                [(SCALING * (one[0] + two[0])).astype(BF16), (LN2 * dk).astype(BF16), dv.astype(BF16)],
                axis=1,
            )
            back_ref[here, :] += dot(all_grads, projections, 1, 1)
            return dot(attn_in_refs[seq][...], all_grads, 0, 0)

        weight_grad = None
        for place in range(len(units) + 1):
            if place < len(units):
                score(units[place])
            if 0 <= place - 1 < len(units):
                weigh(units[place - 1])
            if 0 <= place - 1:
                seq, head = units[place - 1]
                multiply((seq, head))
                if head == 1:
                    part = project(seq)
                    weight_grad = part if weight_grad is None else weight_grad + part
        store_shares(weight_grad, core, sent_ref, kept_ref)

    @pl.when(step >= steps)
    def _():
        place = step - steps
        half = count // 2
        if not finish:
            out_ref[...] = back_ref[pl.ds(pl.multiple_of(place * half, half), half), :].astype(BF16)
        else:
            start = pl.multiple_of(row_block(place, own, seqs) * half, half)
            back = back_ref[pl.ds(start, half), :] + before_ref[...].astype(F32)
            values = hidden_ref[...].astype(F32)
            inverse = lax.rsqrt(jnp.mean(values * values, axis=1, keepdims=True) + EPSILON)
            normed = values * inverse
            grad_gain = jnp.sum(back * normed, axis=0, keepdims=True)
            back = back * gain_ref[...]
            mean = jnp.mean(back * normed, axis=1, keepdims=True)
            grad = mid_ref[...].astype(F32) + inverse * (back - normed * mean)

            @pl.when(place == 0)
            def _():
                grad_gain_ref[...] = grad_gain

            @pl.when(place > 0)
            def _():
                grad_gain_ref[...] += grad_gain

            @pl.when(place < seqs)
            def _():
                in_sent_ref[0] = grad.astype(BF16)

            @pl.when(place >= seqs)
            def _():
                in_kept_ref[0] = grad.astype(BF16)


def row_block(place, own, seqs):
    return 2 * lax.rem(place, seqs) + jnp.where(place < seqs, 1 - own, own)


def attend_back(
    scalars, saved, attn_in, grads, projections, bias_width, pairs, ends
):
    seqs = len(saved)
    count, width = saved[0][0].shape
    size = lax.axis_size("dp")
    rows = width // size
    half = count // 2
    first, last = pairs
    steps = last - first
    once = pl.Buffered(1)

    def early(p):
        return jnp.minimum(p, steps - 1)

    def late(p):
        return jnp.maximum(p - steps, 0)

    weight = pl.BlockSpec((width, LANES), lambda p, *_: (0, first + early(p)))
    probs = pl.BlockSpec((2, count, count), lambda p, *_: (first + early(p), 0, 0))
    shares = pl.BlockSpec((size // 2, rows, 3 * LANES), lambda p, *_: (0, 0, early(p)))
    row = pl.BlockSpec((1, width), lambda p, *_: (0, 0), pipeline_mode=once)

    block = pl.BlockSpec((count, LANES), lambda p, *_: (0, first + early(p)))
    tall = pl.BlockSpec((seqs * count, LANES), lambda p, *_: (0, first + early(p)))
    whole = pl.BlockSpec((count, width), lambda p, *_: (0, 0), pipeline_mode=once)
    queries, keys, values, contexts, weights, inverses = zip(*saved)
    operands = [*queries, *keys, *values, *weights, *inverses, *attn_in, *contexts, grads]
    operands = [in_hbm(v) for v in (*operands, *projections)]
    specs = [block] * (3 * seqs) + [probs] * seqs + [block] * seqs + [whole] * seqs
    specs += [block] * seqs + [tall] + [weight] * 3
    share = pltpu.HBM((size // 2, rows, 3 * LANES * steps), BF16)
    out_shape = [pltpu.HBM((2 * steps, LANES, bias_width), F32), share, share]
    out_specs = [pl.BlockSpec((2, LANES, bias_width), lambda p, *_: (early(p), 0, 0)), shares, shares]
    if ends is not None:
        before, hidden, grad_mid, gain = ends
        operands += [in_hbm(before), in_hbm(hidden), in_hbm(grad_mid), gain.reshape(1, width)]
        mixed_up = pl.BlockSpec(
            (half, width), lambda p, scalars: (row_block(late(p), scalars[1], seqs), 0)
        )
        specs += [mixed_up] * 3 + [row]
        out_shape += [pltpu.HBM((seqs, half, width), BF16)] * 2
        out_shape.append(jax.ShapeDtypeStruct((1, width), F32))
        out_specs += [
            pl.BlockSpec((1, half, width), lambda p, *_: (jnp.maximum(late(p) - seqs, 0), 0, 0)),
            pl.BlockSpec((1, half, width), lambda p, *_: (jnp.minimum(late(p), seqs - 1), 0, 0)),
            row,
        ]
    else:
        out_shape.append(pltpu.HBM((seqs * count, width), BF16))
        out_specs.append(pl.BlockSpec((half, width), lambda p, *_: (late(p), 0)))
    return pl.pallas_call(
        functools.partial(attend_back_kernel, seqs=seqs, steps=steps, finish=ends is not None),
        grid_spec=pltpu.PrefetchScalarGridSpec(
            num_scalar_prefetch=1,
            grid=(steps + 2 * seqs,),
            in_specs=specs,
            out_specs=out_specs,
            scratch_shapes=[pltpu.VMEM((seqs * count, width), F32)],
        ),
        out_shape=out_shape,
        compiler_params=pltpu.CompilerParams(vmem_limit_bytes=VMEM_LIMIT),
        cost_estimate=pl.CostEstimate(flops=0, bytes_accessed=0, transcendentals=0),
    )(scalars, *operands)


def store_product(left, right, core, sent_ref, kept_ref, columns=256):
    for start in range(0, right.shape[1], columns):
        grad = dot(left, right[:, start : start + columns], 0, 0)
        store_shares(grad, core, sent_ref, kept_ref, start)


def in_weight_kernel(scalars, ffn_in_ref, pre_ref, sent_ref, kept_ref):
    width = sent_ref.shape[2]
    columns = pl.ds(pl.multiple_of(pl.program_id(0) * width, width), width)
    store_product(ffn_in_ref[...], pre_ref[:, columns], scalars[0], sent_ref, kept_ref)


def in_weights(scalars, ffn_in, grad_pre):
    tokens, width = ffn_in.shape
    steps = grad_pre.shape[1] // width
    size = lax.axis_size("dp")
    share = pl.BlockSpec((size // 2, width // size, width), lambda j, *_: (0, 0, j))
    return pl.pallas_call(
        in_weight_kernel,
        grid_spec=pltpu.PrefetchScalarGridSpec(
            num_scalar_prefetch=1,
            grid=(steps,),
            in_specs=[RESIDENT, RESIDENT],
            out_specs=[share, share],
        ),
        out_shape=[pltpu.HBM((size // 2, width // size, steps * width), BF16)] * 2,
        compiler_params=pltpu.CompilerParams(vmem_limit_bytes=VMEM_LIMIT),
        cost_estimate=pl.CostEstimate(flops=0, bytes_accessed=0, transcendentals=0),
    )(scalars, *resident(ffn_in, grad_pre))


def out_weight_kernel(scalars, act_ref, upstream_ref, sent_ref, kept_ref):
    width = upstream_ref.shape[1]
    columns = pl.ds(pl.multiple_of(pl.program_id(0) * width, width), width)
    store_product(act_ref[:, columns], upstream_ref[...], scalars[0], sent_ref, kept_ref)


def out_weights(scalars, act, upstream):
    tokens, width = upstream.shape
    units = act.shape[1]
    size = lax.axis_size("dp")
    rows = units // size
    steps = units // width
    share = pl.BlockSpec((size // 2 // steps, rows, width), lambda j, *_: (j, 0, 0))
    return pl.pallas_call(
        out_weight_kernel,
        grid_spec=pltpu.PrefetchScalarGridSpec(
            num_scalar_prefetch=1,
            grid=(steps,),
            in_specs=[RESIDENT, RESIDENT],
            out_specs=[share, share],
        ),
        out_shape=[pltpu.HBM((size // 2, rows, width), BF16)] * 2,
        compiler_params=pltpu.CompilerParams(vmem_limit_bytes=VMEM_LIMIT),
        cost_estimate=pl.CostEstimate(flops=0, bytes_accessed=0, transcendentals=0),
    )(scalars, *resident(act, upstream))


def inverse_of(values):
    return lax.rsqrt(jnp.mean(values * values, axis=1, keepdims=True) + EPSILON)


def middle_kernel(scalars, *refs, seqs, chunk):
    context_refs, hidden_refs = refs[:seqs], refs[seqs : 2 * seqs]
    upstream_ref, w_out_ref, gain_ref, w_in_ref, w_ffn_out_ref = refs[2 * seqs : 2 * seqs + 5]
    act_ref, grad_pre_ref, ffn_in_ref, layer_out_ref, grad_low_ref = refs[2 * seqs + 5 : 2 * seqs + 10]
    grad_context_ref, sent_ref, kept_ref, grad_gain_ref = refs[2 * seqs + 10 : 2 * seqs + 14]
    mixed_ref, total_ref, back_ref = refs[2 * seqs + 14 :]
    tokens, width = mixed_ref.shape
    count = tokens // seqs
    columns = w_in_ref.shape[1]
    step = pl.program_id(0)
    here = pl.ds(pl.multiple_of(step * columns, columns), columns)
    pieces = [
        (slice(start, start + chunk), start // count, slice(start % count, start % count + chunk))
        for start in range(0, tokens, chunk)
    ]

    @pl.when(step == 0)
    def _():
        for rows, seq, local in pieces:
            mixed = hidden_refs[seq][local, :].astype(F32)
            mixed = mixed + dot(context_refs[seq][local, :], w_out_ref[...], 1, 0)
            mixed_ref[rows, :] = mixed
            total_ref[rows, :] = mixed
            back_ref[rows, :] = jnp.zeros((chunk, width), F32)
            ffn_in_ref[rows, :] = (mixed * inverse_of(mixed) * gain_ref[...]).astype(BF16)

    for rows, _, _ in pieces:
        pre = dot(ffn_in_ref[rows, :], w_in_ref[...], 1, 0)
        grad_act = dot(upstream_ref[rows, :], w_ffn_out_ref[...], 1, 1)
        below = 0.5 + 0.5 * lax.erf(pre * 0.7071067811865476)
        density = jnp.exp2(pre * pre * (-0.5 * LOG2E)) * 0.3989422804014327
        act = (pre * below).astype(BF16)
        grad_pre = (grad_act * (below + pre * density)).astype(BF16)
        act_ref[rows, here] = act
        grad_pre_ref[rows, here] = grad_pre
        total_ref[rows, :] += dot(act, w_ffn_out_ref[...], 1, 0)
        back_ref[rows, :] += dot(grad_pre, w_in_ref[...], 1, 1)

    @pl.when(step == pl.num_programs(0) - 1)
    def _():
        grad_gain = jnp.zeros(gain_ref.shape, F32)
        weight = None
        for rows, seq, local in pieces:
            layer_out_ref[rows, :] = total_ref[rows, :].astype(BF16)
            mixed = mixed_ref[rows, :]
            inverse = inverse_of(mixed)
            normed = mixed * inverse
            back = back_ref[rows, :]
            grad_gain += jnp.sum(back * normed, axis=0, keepdims=True)
            back = back * gain_ref[...]
            mean = jnp.mean(back * normed, axis=1, keepdims=True)
            grad = upstream_ref[rows, :].astype(F32) + inverse * (back - normed * mean)
            low = grad.astype(BF16)
            grad_low_ref[rows, :] = low
            grad_context_ref[rows, :] = dot(low, w_out_ref[...], 1, 1).astype(BF16)
            part = dot(context_refs[seq][local, :], low, 0, 0)
            weight = part if weight is None else weight + part
        grad_gain_ref[...] = grad_gain
        store_shares(weight, scalars[0], sent_ref, kept_ref)


def middle(
    scalars, contexts, hidden, upstream, w_out, gain, w_in, w_ffn_out, columns=512, chunk=256
):
    tokens, width = upstream.shape
    units = w_in.shape[1]
    seqs = len(contexts)
    size = lax.axis_size("dp")
    once = pl.Buffered(1)

    def whole(*shape):
        return pl.BlockSpec(shape, lambda j, *_: (0,) * len(shape), pipeline_mode=once)

    shares = (size // 2, width // size, width)
    low = pltpu.HBM((tokens, width), BF16)
    return pl.pallas_call(
        functools.partial(middle_kernel, seqs=seqs, chunk=chunk),
        grid_spec=pltpu.PrefetchScalarGridSpec(
            num_scalar_prefetch=1,
            grid=(units // columns,),
            in_specs=[RESIDENT] * (2 * seqs + 1)
            + [
                whole(width, width),
                whole(1, width),
                pl.BlockSpec((width, columns), lambda j, *_: (0, j)),
                pl.BlockSpec((columns, width), lambda j, *_: (j, 0)),
            ],
            out_specs=[RESIDENT] * 3
            + [whole(tokens, width)] * 3
            + [whole(*shares), whole(*shares), whole(1, width)],
            scratch_shapes=[pltpu.VMEM((tokens, width), F32)] * 3,
        ),
        out_shape=[
            pltpu.VMEM((tokens, units), BF16),
            pltpu.VMEM((tokens, units), BF16),
            pltpu.VMEM((tokens, width), BF16),
            low,
            low,
            low,
        ]
        + [pltpu.HBM(shares, BF16)] * 2
        + [jax.ShapeDtypeStruct((1, width), F32)],
        compiler_params=pltpu.CompilerParams(vmem_limit_bytes=VMEM_LIMIT),
        cost_estimate=pl.CostEstimate(
            flops=8 * tokens * width * units, bytes_accessed=20 * 2**20, transcendentals=0
        ),
    )(
        scalars,
        *resident(*contexts, *hidden, upstream),
        in_hbm(w_out),
        gain.reshape(1, width),
        in_hbm(w_in),
        in_hbm(w_ffn_out),
    )


def bits_of(size):
    return size.bit_length() - 1


def flip(axis, mask):
    size = lax.axis_size(axis)
    return [(index, index ^ mask) for index in range(size)]


def swap_blk(values):
    return lax.ppermute(values, "blk", flip("blk", 1))


def pick(values, index, axis):
    return lax.dynamic_index_in_dim(values, index, axis, keepdims=False)


def part_of(values, index, axis):
    share = values.shape[axis] // 2
    return lax.dynamic_slice_in_dim(values, index * share, share, axis)


def in_order(own, kept, got, axis):
    share = kept.shape[axis]
    shape = kept.shape[:axis] + (2 * share,) + kept.shape[axis + 1 :]
    both = lax.dynamic_update_slice_in_dim(jnp.zeros(shape, kept.dtype), kept, own * share, axis)
    return lax.dynamic_update_slice_in_dim(both, got, (1 - own) * share, axis)


def join(parts, axis):
    return parts[0] if len(parts) == 1 else jnp.concatenate(parts, axis)


class Shares:
    def __init__(self, shares, order):
        self.left = list(range(1, bits_of(lax.axis_size("dp"))))[::-1]
        self.order = [0] + order
        self.shares = shares
        self.by_column = False
        self.widths = []
        self.got = None
        self.pairs = []

    def joined(self, slices, axis):
        parts = [slices(kept).astype(F32) + slices(got).astype(F32) for kept, got in self.pairs]
        return join([part.astype(BF16) for part in parts], axis)

    def send(self):
        if not self.order or self.got is not None:
            return
        stage = self.order[0]
        own = lax.axis_index("blk")
        if stage == 0:
            self.got = [lax.ppermute(sent, "dp", flip("dp", 1)) for sent, _ in self.shares]
        elif stage == "last":
            self.kept = self.joined(lambda part: part[0], 1)
            self.got = swap_blk(self.kept)
        elif stage == "blk":
            self.widths = [kept.shape[2] // 2 for kept, _ in self.pairs]
            sent = self.joined(lambda part: part_of(part, 1 - own, 2), 2)
            self.got = swap_blk(sent)
            self.kept = self.joined(lambda part: part_of(part, own, 2), 2)
        else:
            place = self.left.index(stage)
            after = len(self.left) - place - 1
            mine = (lax.axis_index("dp") >> stage) & 1
            self.left.pop(place)

            def half(index):
                def of(part):
                    split = part.reshape((2**place, 2, 2**after) + part.shape[1:])
                    return pick(split, index, 1).reshape((2 ** (place + after),) + part.shape[1:])

                return of

            self.got = lax.ppermute(self.joined(half(1 - mine), 2), "dp", flip("dp", 1 << stage))
            self.kept = self.joined(half(mine), 2)

    def receive(self):
        stage = self.order.pop(0)
        if stage == 0:
            self.pairs = [(kept, got) for (_, kept), got in zip(self.shares, self.got)]
            self.got = None
            return
        if stage == "last":
            if self.by_column:
                total = in_order(lax.axis_index("blk"), self.kept, self.got, 1).astype(F32)
                half = total.shape[1] // 2
                parts, start = [], 0
                for width in self.widths:
                    parts.append(total[:, start : start + width])
                    parts.append(total[:, half + start : half + start + width])
                    start += width
                self.total = jnp.concatenate(parts, axis=1)
            else:
                self.total = self.kept.astype(F32) + self.got.astype(F32)
        self.by_column = self.by_column or stage == "blk"
        self.pairs = [(self.kept, self.got)]
        self.got = None

    def take_over(self, other):
        rows = self.pairs[0][0].shape[1]
        for kept, got in other.pairs:
            for start in range(0, kept.shape[1], rows):
                self.pairs.append((kept[:, start : start + rows], got[:, start : start + rows]))
                self.widths.append(kept.shape[2])


def receive(shares, *values):
    shares = [share for share in shares if share.got is not None]
    gots, values = lax.optimization_barrier(([share.got for share in shares], values))
    for share, got in zip(shares, gots):
        share.got = got
        share.receive()
    return values if len(values) > 1 else values[0]


def normalize(values):
    inverse = lax.rsqrt(jnp.mean(values * values, axis=-1, keepdims=True) + EPSILON)
    return values * inverse, inverse


def norm_back(normed, inverse, upstream):
    return inverse * (upstream - normed * jnp.mean(upstream * normed, axis=-1, keepdims=True))


def body(
    hidden,
    lengths,
    flags,
    buckets,
    g_attn,
    w_query,
    w_key,
    w_value,
    w_out,
    g_ffn,
    w_in,
    w_ffn_out,
    bias_table,
    cotangent,
):
    own = lax.axis_index("blk")
    size = lax.axis_size("dp")
    rest = list(range(1, bits_of(size)))
    first, second, later = rest[:1], rest[1:2], rest[2:]
    width = hidden.shape[2]
    seqs = hidden.shape[0] // 2
    count = hidden.shape[1] * 2
    tokens = seqs * count
    each = range(seqs)
    buckets_used, heads = bias_table.shape
    bias_width = 2 * count - LANES
    length = 2 * count

    def give_back(values):
        return part_of(values, own, 1), swap_blk(part_of(values, 1 - own, 1))

    with jax.named_scope("exchange_in"):
        def take(values, start, number):
            kept = lax.dynamic_slice_in_dim(values, own * seqs + start, number, 0)
            return kept, lax.dynamic_slice_in_dim(values, (1 - own) * seqs + start, number, 0)

        hidden_parts = []
        for seq in each:
            kept, sent = take(hidden, seq, 1)
            if seq > 0:
                sent, hidden_parts[-1][1] = lax.optimization_barrier((sent, hidden_parts[-1][1]))
            hidden_parts.append([kept, swap_blk(sent)])
        early = 3 * count // 16
        upstream_kept, upstream_sent = take(cotangent, 0, seqs)
        first_part = upstream_sent[:, :early]
        if seqs > 1:
            first_part, hidden_parts[0][1] = lax.optimization_barrier(
                (first_part, hidden_parts[0][1])
            )
        upstream_got = swap_blk(first_part)
        valid_all = jnp.where(flags == 1, lengths[:, 1], lengths[:, 0])
        valid = lax.dynamic_slice_in_dim(valid_all, own * seqs, seqs, 0)
        scalars = jnp.stack([lax.axis_index("dp") & 1, own]).astype(jnp.int32)

    with jax.named_scope("bias"):
        one_hot = (
            buckets[None, :] == jnp.arange(buckets_used, dtype=jnp.int32)[:, None]
        ).astype(F32)
        one_hot = jnp.pad(one_hot, ((0, 0), (0, length - buckets.shape[0])))
        vector = lax.dot_general(
            bias_table * LOG2E,
            one_hot,
            (((0,), (0,)), ((), ())),
            precision=lax.Precision.HIGHEST,
        )
        bias = expand_bias(jnp.roll(vector, -(LANES - 1), axis=1), bias_width)

    contexts, saved, hidden_seq, attn_in_seq = [], [], [], []
    for seq in each:
        with jax.named_scope("project"):
            kept, got = hidden_parts[seq]
            if seq > 0:
                got, contexts[-1] = lax.optimization_barrier((got, contexts[-1]))
            if seq == seqs - 1:
                late, got = lax.optimization_barrier((upstream_sent[:, early:], got))
                upstream_got = jnp.concatenate([upstream_got, swap_blk(late)], axis=1)
            hidden_seq.append(in_order(own, kept, got, 1)[0])
            normed, _ = normalize(hidden_seq[seq].astype(F32))
            attn_in = (normed * g_attn).astype(BF16)
            queries = (dot(attn_in, w_query, 1, 0) * (SCALING * LOG2E)).astype(BF16)
            keys = dot(attn_in, w_key, 1, 0).astype(BF16)
            values = dot(attn_in, w_value, 1, 0).astype(BF16)
            attn_in_seq.append(attn_in)
        with jax.named_scope("attend"):
            context, *kept = attend(queries, keys, values, bias, valid, seq)
            contexts.append(context)
            saved.append([queries, keys, values, *kept])

    with jax.named_scope("middle"):
        upstream = in_order(own, upstream_kept, upstream_got, 1).reshape(tokens, width)
        inputs = jnp.concatenate(hidden_seq, axis=0)
        act, grad_pre, ffn_in, layer_out, grad_low, grad_context, sent, kept, grad_g_ffn = middle(
            scalars, contexts, hidden_seq, upstream, w_out, g_ffn, w_in, w_ffn_out
        )
    with jax.named_scope("output"):
        output_kept, output_got = give_back(layer_out.reshape(seqs, count, width))

    with jax.named_scope("ffn_weights"):
        out_shares = Shares([out_weights(scalars, act, upstream)], first + ["blk"] + second)
        out_shares.send()
        in_sent, in_kept = in_weights(scalars, ffn_in, grad_pre)
        in_sent, in_kept = receive([out_shares], in_sent, in_kept)
        in_shares = Shares([(in_sent, in_kept)], second + first + ["blk"])
        in_shares.send()
        out_shares.send()
        (out_shares.kept,) = (receive([in_shares], out_shares.kept),)
        in_shares.send()
        grad_context, in_shares.kept = lax.optimization_barrier((grad_context, in_shares.kept))

    with jax.named_scope("attend_back"):
        pairs = width // LANES
        parting = 2 * pairs // 3
        weights = (w_query, w_key, w_value)
        bias_one, one_sent, one_kept, before = attend_back(
            scalars, saved, attn_in_seq, grad_context, weights, bias_width,
            (0, parting), None,
        )
        one_shares = Shares([(one_sent, one_kept), (sent, kept)], second + first + later + ["last"])
        one_shares.send()
        before, grad_context = receive([out_shares, in_shares], before, grad_context)
        out_shares.send()
        in_shares.send()
        before, grad_context = receive([one_shares], before, grad_context)
        one_shares.send()
        bias_two, two_sent, two_kept, input_kept, input_sent, grad_g_attn = attend_back(
            scalars, saved, attn_in_seq, grad_context, weights, bias_width,
            (parting, pairs), (before, inputs, grad_low, g_attn),
        )
        two_shares = Shares([(two_sent, two_kept)], first + second + later + ["last"])
        two_shares.send()
        bias_one, bias_two, input_sent, output_got = receive(
            [one_shares, in_shares, out_shares], bias_one, bias_two, input_sent, output_got
        )

    with jax.named_scope("rounds"):
        for shares in (out_shares, in_shares, one_shares):
            shares.send()
        folded = fold_bias(bias_one, length), fold_bias(bias_two, length)
        *folded, input_sent = receive(
            [two_shares, one_shares, out_shares, in_shares], *folded, input_sent
        )
        in_shares.take_over(out_shares)
        in_shares.order = later + ["last"]
        input_got = swap_blk(input_sent)
        two_shares.send()
        in_shares.send()

    with jax.named_scope("small"):
        table = lax.dot_general(
            one_hot,
            jnp.concatenate(folded, axis=0),
            (((1,), (1,)), ((), ())),
            precision=lax.Precision.HIGHEST,
        )
        flat = jnp.concatenate([grad_g_attn[0], grad_g_ffn[0], table.reshape(-1)])
        flat = jnp.pad(flat, (0, -flat.shape[0] % 1024)).reshape(-1, LANES)
        if size > 1:
            flat = flat + lax.ppermute(flat, "dp", flip("dp", 1))
        small_bits = list(range(1, bits_of(size))) + ["blk"]

    def small_step(flat, chains, *others):
        if not small_bits:
            flat, *others = receive(chains, flat, *others, 0)[:-1]
            return flat, *others
        bit = small_bits.pop(0)
        got = swap_blk(flat) if bit == "blk" else lax.ppermute(flat, "dp", flip("dp", 1 << bit))
        flat, got, *others = receive(chains, flat, got, *others)
        return flat + got, *others

    with jax.named_scope("rounds"):
        (flat,) = small_step(flat, [two_shares])
        two_shares.send()
        one_shares.send()
        flat, input_got = small_step(flat, [two_shares, in_shares], input_got)
        chains = [two_shares, one_shares, in_shares]
        while any(shares.order for shares in chains) or small_bits:
            for shares in chains:
                shares.send()
            (flat,) = small_step(flat, chains)

    one, two = one_shares.total, two_shares.total
    pieces = jnp.split(one[:, : 3 * LANES * parting], 3 * parting, axis=1)
    pieces += jnp.split(two, 3 * (pairs - parting), axis=1)
    grad_query_w, grad_key_w, grad_value_w = (
        jnp.concatenate(pieces[part::3], axis=1) for part in range(3)
    )
    grad_out_w = one[:, 3 * LANES * parting :]
    two = in_shares.total
    units = w_in.shape[1]
    grad_in = two[:, :units]
    grad_ffn_out = jnp.concatenate(
        [two[:, start : start + width] for start in range(units, two.shape[1], width)], axis=0
    )
    with jax.named_scope("output"):
        output = in_order(own, output_kept, output_got, 0)
        input_grad = in_order(own, input_kept, input_got, 0)

    with jax.named_scope("small"):
        flat = flat.reshape(-1)
        share = width // size
        at = lax.axis_index("dp") * share
        gain_attn = lax.dynamic_slice_in_dim(flat[:width], at, share)
        gain_ffn = lax.dynamic_slice_in_dim(flat[width : 2 * width], at, share)
        table = flat[2 * width : 2 * width + buckets_used * heads].reshape(buckets_used, heads)

    return (
        output,
        input_grad,
        gain_attn,
        grad_query_w,
        grad_key_w,
        grad_value_w,
        grad_out_w,
        gain_ffn,
        grad_in,
        grad_ffn_out,
        table,
    )


def solution(mesh):
    split = P("dp", "blk", None)
    rows = P("dp", None)
    in_specs = (split, rows, P("dp")) + (P(),) * 10 + (split,)
    out_specs = (split, split, P("dp")) + (rows,) * 4 + (P("dp"), rows, rows, P())
    return jax.shard_map(body, mesh=mesh, in_specs=in_specs, out_specs=out_specs, check_vma=False)
```

```python
import copy
import functools
import math

import jax
import jax.numpy as jnp
from jax import lax
from jax.experimental import pallas as pl
from jax.experimental.pallas import tpu as pltpu
from jax.sharding import PartitionSpec as P

EPSILON = 1e-06
MASKED = -1000000000.0
SCALING = 0.125
LOG2E = 1.4426950408889634
LN2 = 0.6931471805599453
HEAD = 64
LANES = 128
VMEM_LIMIT = 32 * 2**20
BF16 = jnp.bfloat16
F32 = jnp.float32


def dot(left, right, left_dim, right_dim):
    return lax.dot_general(
        left, right, (((left_dim,), (right_dim,)), ((), ())), preferred_element_type=F32
    )


RESIDENT = pl.BlockSpec(memory_space=pltpu.VMEM)


def in_hbm(values):
    return pltpu.with_memory_space_constraint(values, pltpu.HBM)


def resident(*values):
    return [pltpu.with_memory_space_constraint(v, pltpu.VMEM) for v in values]


def expand_kernel(vector_ref, out_ref):
    group, _, width = vector_ref.shape
    for head in range(group):
        rows = jnp.broadcast_to(vector_ref[head], (LANES, width))
        moved = pltpu.roll(rows, 0, 1, stride=1, stride_axis=0)
        out_ref[head] = moved[:, : out_ref.shape[2]]


def expand_bias(vector, width):
    heads, length = vector.shape
    group = 4 if heads % 4 == 0 else 1
    return pl.pallas_call(
        expand_kernel,
        grid=(heads // group,),
        in_specs=[pl.BlockSpec((group, 1, length), lambda h: (h, 0, 0))],
        out_specs=pl.BlockSpec((group, LANES, width), lambda h: (h, 0, 0)),
        out_shape=jax.ShapeDtypeStruct((heads, LANES, width), F32),
        compiler_params=pltpu.CompilerParams(vmem_limit_bytes=VMEM_LIMIT),
    )(vector.reshape(heads, 1, length))


def fold_kernel(grad_ref, out_ref):
    width = grad_ref.shape[2]
    length = out_ref.shape[2]
    pad = jnp.zeros((8, length - width), F32)
    for head in range(grad_ref.shape[0]):
        total = jnp.zeros((8, length), F32)
        for start in range(0, LANES, 8):
            rows = jnp.concatenate([grad_ref[head, start : start + 8, :], pad], axis=1)
            total = total + pltpu.roll(rows, LANES - 8 - start, 1)
        folded = total[7:8]
        for row in range(7):
            folded = folded + pltpu.roll(total[row : row + 1], 7 - row, 1)
        out_ref[head] = jnp.broadcast_to(folded, (8, length))


def fold_bias(grad, length):
    heads, _, width = grad.shape
    group = 4 if heads % 4 == 0 else 1
    return pl.pallas_call(
        fold_kernel,
        grid=(heads // group,),
        in_specs=[pl.BlockSpec((group, LANES, width), lambda h: (h, 0, 0))],
        out_specs=pl.BlockSpec((group, 8, length), lambda h: (h, 0, 0)),
        out_shape=jax.ShapeDtypeStruct((heads, 8, length), F32),
        compiler_params=pltpu.CompilerParams(vmem_limit_bytes=VMEM_LIMIT),
        cost_estimate=pl.CostEstimate(flops=0, bytes_accessed=0, transcendentals=0),
    )(in_hbm(grad))[:, 0]


def inverse_of(values):
    return lax.rsqrt(jnp.mean(values * values, axis=1, keepdims=True) + EPSILON)


def project_kernel(scalars, kept_ref, got_ref, gain_ref, w_ref, hidden_ref, attn_in_ref, out_ref):
    half = kept_ref.shape[1]
    step = pl.program_id(0)

    @pl.when(step == 0)
    def _():
        for ref, place in ((kept_ref, scalars[1]), (got_ref, 1 - scalars[1])):
            rows = pl.ds(pl.multiple_of(place * half, half), half)
            hidden_ref[rows, :] = ref[0]
            values = ref[0].astype(F32)
            attn_in_ref[rows, :] = (values * inverse_of(values) * gain_ref[...]).astype(BF16)

    scale = jnp.where(step == 0, SCALING * LOG2E, 1.0)
    out_ref[0] = (dot(attn_in_ref[...], w_ref[0], 1, 0) * scale).astype(BF16)


def project(scalars, kept, got, gain, weights):
    _, half, width = kept.shape
    count = 2 * half
    once = pl.Buffered(1)

    def whole(*shape):
        return pl.BlockSpec(shape, lambda j, *_: (0,) * len(shape), pipeline_mode=once)

    return pl.pallas_call(
        project_kernel,
        grid_spec=pltpu.PrefetchScalarGridSpec(
            num_scalar_prefetch=1,
            grid=(weights.shape[0],),
            in_specs=[
                whole(1, half, width),
                whole(1, half, width),
                whole(1, width),
                pl.BlockSpec((1, width, width), lambda j, *_: (j, 0, 0)),
            ],
            out_specs=[
                whole(count, width),
                whole(count, width),
                pl.BlockSpec((1, count, width), lambda j, *_: (j, 0, 0)),
            ],
        ),
        out_shape=[
            jax.ShapeDtypeStruct((count, width), BF16),
            jax.ShapeDtypeStruct((count, width), BF16),
            jax.ShapeDtypeStruct((weights.shape[0], count, width), BF16),
        ],
        compiler_params=pltpu.CompilerParams(vmem_limit_bytes=VMEM_LIMIT),
        cost_estimate=pl.CostEstimate(
            flops=6 * count * width * width, bytes_accessed=8 * 2**20, transcendentals=0
        ),
    )(scalars, kept, got, gain.reshape(1, width), weights)


def attend_kernel(
    valid, q_ref, k_ref, v_ref, bias_ref, out_ref, copy_ref, weights_ref, inverse_ref, *, chunk, seq
):
    limit = valid[seq]
    count = q_ref.shape[1]
    pair = pl.program_id(0)
    columns = pl.ds(pl.multiple_of(pair * LANES, LANES), LANES)
    queries, keys, values = (ref[0].astype(F32) for ref in (q_ref, k_ref, v_ref))
    lane = lax.broadcasted_iota(jnp.int32, (count, LANES), 1)
    row = lax.broadcasted_iota(jnp.int32, (count, LANES), 0)
    heads = []
    for head in range(2):
        mine = (lane // HEAD) == head
        extra = lane == (1 - head) * HEAD
        mask = jnp.where(extra & (row >= limit), MASKED, 0.0)
        heads.append(
            (
                jnp.where(mine, queries, jnp.where(extra, 1.0, 0.0)).astype(BF16),
                jnp.where(mine, keys, mask).astype(BF16),
                jnp.where(mine, values, 1.0).astype(BF16),
            )
        )
    first = lax.broadcasted_iota(jnp.int32, (chunk, LANES), 1) < HEAD
    units = [(step, head) for step in range(count // chunk) for head in range(2)]

    def scores(unit):
        step, head = unit
        rows = slice(step * chunk, (step + 1) * chunk)
        windows = [
            bias_ref[head, :, count - LANES * (1 + block) : 2 * count - LANES * (1 + block)]
            for block in range(step * chunk // LANES, (step + 1) * chunk // LANES)
        ]
        return dot(heads[head][0][rows], heads[head][1], 1, 1) + jnp.concatenate(windows, axis=0)

    ahead = 2
    logits = {unit: scores(unit) for unit in units[:ahead]}
    sums = {}
    for place, unit in enumerate(units):
        step, head = unit
        rows = slice(step * chunk, (step + 1) * chunk)
        if place + ahead < len(units):
            logits[units[place + ahead]] = scores(units[place + ahead])
        top = jnp.max(logits[unit], axis=1, keepdims=True)
        weights = jnp.exp2(logits[unit] - top).astype(BF16)
        weights_ref[head, rows, :] = weights
        sums[unit] = dot(weights, heads[head][2], 1, 0)
        if head == 1:
            one, two = sums[step, 0], sums[step, 1]
            inverse = 1.0 / pltpu.roll(jnp.where(first, two, one), HEAD, 1)
            inverse_ref[rows, :] = inverse
            context = (jnp.where(first, one, two) * inverse).astype(BF16)
            out_ref[rows, columns] = context
            copy_ref[rows, :] = context


def projections_of(count, pair):
    return [
        pl.BlockSpec((1, count, LANES), lambda *at, part=part: (part, 0, pair(*at)))
        for part in range(3)
    ]


def attend(projected, bias, valid, seq, chunk=256):
    _, count, width = projected.shape
    block = pl.BlockSpec((count, LANES), lambda p, *_: (0, p))
    return pl.pallas_call(
        functools.partial(attend_kernel, chunk=chunk, seq=seq),
        grid_spec=pltpu.PrefetchScalarGridSpec(
            num_scalar_prefetch=1,
            grid=(width // LANES,),
            in_specs=[
                *projections_of(count, lambda p, *_: p),
                pl.BlockSpec((2, LANES, bias.shape[2]), lambda p, *_: (p, 0, 0)),
            ],
            out_specs=[
                RESIDENT,
                block,
                pl.BlockSpec((2, count, count), lambda p, *_: (p, 0, 0)),
                block,
            ],
        ),
        out_shape=[
            pltpu.VMEM((count, width), BF16),
            pltpu.HBM((count, width), BF16),
            pltpu.HBM((width // HEAD, count, count), BF16),
            pltpu.HBM((count, width), F32),
        ],
        compiler_params=pltpu.CompilerParams(vmem_limit_bytes=VMEM_LIMIT),
        cost_estimate=pl.CostEstimate(
            flops=32 * count * count * width, bytes_accessed=12 * 2**20, transcendentals=0
        ),
    )(valid, *[projected] * 3, bias)


def store_shares(grad, core, sent_ref, kept_ref, start=0, folds=1):
    count, rows, width = sent_ref.shape
    grad = grad.astype(BF16) if rows % 16 == 0 else grad
    for group in range(count):
        for fold in range(folds):
            place = (2 * group * folds + fold) * rows
            even = grad[place : place + rows]
            place += folds * rows
            odd = grad[place : place + rows]
            at = fold * (width // folds) + start
            columns = slice(at, at + grad.shape[1])
            sent_ref[group, :, columns] = jnp.where(core == 0, odd, even).astype(BF16)
            kept_ref[group, :, columns] = jnp.where(core == 0, even, odd).astype(BF16)


def attend_back_kernel(scalars, *refs, seqs, steps, finish):
    refs = list(refs)

    def some(count):
        taken = refs[:count]
        del refs[:count]
        return taken

    projected_refs = [some(3) for _ in range(seqs)]
    weights_refs, inverse_refs = some(seqs), some(seqs)
    attn_in_refs = some(seqs)
    ctx_refs = some(seqs)
    grad_ref, wq_ref, wk_ref, wv_ref = some(4)
    if finish:
        before_ref, hidden_ref, mid_ref, gain_ref = some(4)
    bias_ref, sent_ref, kept_ref = some(3)
    if finish:
        in_kept_ref, in_sent_ref, grad_gain_ref, back_ref = some(4)
    else:
        out_ref, back_ref = some(2)
    core, own = scalars[0], scalars[1]
    count = projected_refs[0][0].shape[1]
    lane = lax.broadcasted_iota(jnp.int32, (count, LANES), 1)

    step = pl.program_id(0)

    @pl.when(step == 0)
    def _():
        back_ref[...] = jnp.zeros_like(back_ref)

    @pl.when(step < steps)
    def _():
        bias_ref[...] = jnp.zeros_like(bias_ref)
        projections = jnp.concatenate([wq_ref[...], wk_ref[...], wv_ref[...]], axis=1)
        units = [(seq, head) for seq in range(seqs) for head in range(2)]
        loaded, scored, low_grads, parts = {}, {}, {}, {}

        def load(seq):
            here = slice(seq * count, (seq + 1) * count)
            queries, keys, values = (ref[0].astype(F32) for ref in projected_refs[seq])
            grads = grad_ref[here, :].astype(F32) * inverse_refs[seq][...]
            products = grads * ctx_refs[seq][...].astype(F32)
            turned = jnp.transpose(queries).astype(BF16), jnp.transpose(grads).astype(BF16)
            loaded[seq] = keys, values, grads, products, turned

        def score(unit):
            seq, head = unit
            if head == 0:
                load(seq)
            _, values, grads, products, _ = loaded[seq]
            mine = (lane // HEAD) == head
            other = (1 - head) * HEAD
            extra = (lane == other) | (lane == other + 1)
            v_head = jnp.where(mine, values, jnp.where(extra, 1.0, 0.0)).astype(BF16)
            delta = jnp.sum(jnp.where(mine, products, 0.0), axis=1, keepdims=True)
            high = delta.astype(BF16).astype(F32)
            spread = jnp.where(lane == other, -high, jnp.where(extra, high - delta, 0.0))
            g_head = jnp.where(mine, grads, spread).astype(BF16)
            scored[unit] = dot(g_head, v_head, 1, 1)

        def weigh(unit):
            seq, head = unit
            grad_logits = weights_refs[seq][head].astype(F32) * scored[unit]
            blocks = count // LANES
            for tile in range(2 * blocks - 1):
                bias_ref[head, :, tile * LANES : (tile + 1) * LANES] += sum(
                    grad_logits[
                        block * LANES : (block + 1) * LANES,
                        (tile + 1 + block - blocks) * LANES : (tile + 2 + block - blocks) * LANES,
                    ]
                    for block in range(blocks)
                    if 0 <= tile + 1 + block - blocks < blocks
                )
            low_grads[unit] = grad_logits.astype(BF16)

        def multiply(unit):
            seq, head = unit
            keys, _, _, _, (queries_t, grads_t) = loaded[seq]
            rows = slice(head * HEAD, (head + 1) * HEAD)
            k_head = jnp.where((lane // HEAD) == head, keys, 0.0).astype(BF16)
            low = low_grads[unit]
            parts[unit] = (
                dot(low, k_head, 1, 0),
                dot(queries_t[rows], low, 1, 0),
                dot(grads_t[rows], weights_refs[seq][head], 1, 0),
            )

        def project(seq):
            here = slice(seq * count, (seq + 1) * count)
            one, two = parts[seq, 0], parts[seq, 1]
            dk = jnp.transpose(jnp.concatenate([one[1], two[1]], axis=0))
            dv = jnp.transpose(jnp.concatenate([one[2], two[2]], axis=0))
            all_grads = jnp.concatenate(
                [(SCALING * (one[0] + two[0])).astype(BF16), (LN2 * dk).astype(BF16), dv.astype(BF16)],
                axis=1,
            )
            back_ref[here, :] += dot(all_grads, projections, 1, 1)
            return dot(attn_in_refs[seq][...], all_grads, 0, 0)

        weight_grad = None
        for place in range(len(units) + 1):
            if place < len(units):
                score(units[place])
            if 0 <= place - 1 < len(units):
                weigh(units[place - 1])
            if 0 <= place - 1:
                seq, head = units[place - 1]
                multiply((seq, head))
                if head == 1:
                    part = project(seq)
                    weight_grad = part if weight_grad is None else weight_grad + part
        store_shares(weight_grad, core, sent_ref, kept_ref)

    @pl.when(step >= steps)
    def _():
        place = step - steps
        half = count // 2
        if not finish:
            out_ref[...] = back_ref[pl.ds(pl.multiple_of(place * half, half), half), :].astype(BF16)
        else:
            start = pl.multiple_of(row_block(place, own, seqs) * half, half)
            back = back_ref[pl.ds(start, half), :] + before_ref[...].astype(F32)
            values = hidden_ref[...].astype(F32)
            inverse = lax.rsqrt(jnp.mean(values * values, axis=1, keepdims=True) + EPSILON)
            normed = values * inverse
            grad_gain = jnp.sum(back * normed, axis=0, keepdims=True)
            back = back * gain_ref[...]
            mean = jnp.mean(back * normed, axis=1, keepdims=True)
            grad = mid_ref[...].astype(F32) + inverse * (back - normed * mean)

            @pl.when(place == 0)
            def _():
                grad_gain_ref[...] = grad_gain

            @pl.when(place > 0)
            def _():
                grad_gain_ref[...] += grad_gain

            @pl.when(place < seqs)
            def _():
                in_sent_ref[0] = grad.astype(BF16)

            @pl.when(place >= seqs)
            def _():
                in_kept_ref[0] = grad.astype(BF16)


def row_block(place, own, seqs):
    return 2 * lax.rem(place, seqs) + jnp.where(place < seqs, 1 - own, own)


def attend_back(
    scalars, saved, attn_in, grads, projections, bias_width, pairs, ends
):
    seqs = len(saved)
    _, count, width = saved[0][0].shape
    size = lax.axis_size("dp")
    rows = width // size
    half = count // 2
    first, last = pairs
    steps = last - first
    once = pl.Buffered(1)

    def early(p):
        return jnp.minimum(p, steps - 1)

    def late(p):
        return jnp.maximum(p - steps, 0)

    weight = pl.BlockSpec((width, LANES), lambda p, *_: (0, first + early(p)))
    probs = pl.BlockSpec((2, count, count), lambda p, *_: (first + early(p), 0, 0))
    shares = pl.BlockSpec((size // 2, rows, 3 * LANES), lambda p, *_: (0, 0, early(p)))
    row = pl.BlockSpec((1, width), lambda p, *_: (0, 0), pipeline_mode=once)

    block = pl.BlockSpec((count, LANES), lambda p, *_: (0, first + early(p)))
    tall = pl.BlockSpec((seqs * count, LANES), lambda p, *_: (0, first + early(p)))
    whole = pl.BlockSpec((count, width), lambda p, *_: (0, 0), pipeline_mode=once)
    projected, contexts, weights, inverses = zip(*saved)
    operands = [v for v in projected for _ in range(3)]
    operands += [*weights, *inverses, *attn_in, *contexts, grads]
    operands = [in_hbm(v) for v in (*operands, *projections)]
    specs = projections_of(count, lambda p, *_: first + early(p)) * seqs
    specs += [probs] * seqs + [block] * seqs + [whole] * seqs
    specs += [block] * seqs + [tall] + [weight] * 3
    share = pltpu.HBM((size // 2, rows, 3 * LANES * steps), BF16)
    out_shape = [pltpu.HBM((2 * steps, LANES, bias_width), F32), share, share]
    out_specs = [pl.BlockSpec((2, LANES, bias_width), lambda p, *_: (early(p), 0, 0)), shares, shares]
    if ends is not None:
        before, hidden, grad_mid, gain = ends
        operands += [in_hbm(before), in_hbm(hidden), in_hbm(grad_mid), gain.reshape(1, width)]
        mixed_up = pl.BlockSpec(
            (half, width), lambda p, scalars: (row_block(late(p), scalars[1], seqs), 0)
        )
        specs += [mixed_up] * 3 + [row]
        out_shape.append(pltpu.HBM((2 * seqs, half, width), BF16))
        out_shape.append(pltpu.HBM((seqs, half, width), BF16))
        out_shape.append(jax.ShapeDtypeStruct((1, width), F32))
        out_specs += [
            pl.BlockSpec(
                (1, half, width),
                lambda p, scalars: (scalars[1] * seqs + jnp.maximum(late(p) - seqs, 0), 0, 0),
            ),
            pl.BlockSpec((1, half, width), lambda p, *_: (jnp.minimum(late(p), seqs - 1), 0, 0)),
            row,
        ]
    else:
        out_shape.append(pltpu.HBM((seqs * count, width), BF16))
        out_specs.append(pl.BlockSpec((half, width), lambda p, *_: (late(p), 0)))
    return pl.pallas_call(
        functools.partial(attend_back_kernel, seqs=seqs, steps=steps, finish=ends is not None),
        grid_spec=pltpu.PrefetchScalarGridSpec(
            num_scalar_prefetch=1,
            grid=(steps + 2 * seqs,),
            in_specs=specs,
            out_specs=out_specs,
            scratch_shapes=[pltpu.VMEM((seqs * count, width), F32)],
        ),
        out_shape=out_shape,
        compiler_params=pltpu.CompilerParams(vmem_limit_bytes=VMEM_LIMIT),
        cost_estimate=pl.CostEstimate(flops=0, bytes_accessed=0, transcendentals=0),
    )(scalars, *operands)


def store_product(left, right, core, sent_ref, kept_ref, folds=1, columns=256):
    for start in range(0, right.shape[1], columns):
        grad = dot(left, right[:, start : start + columns], 0, 0)
        store_shares(grad, core, sent_ref, kept_ref, start, folds)


def in_weight_kernel(scalars, ffn_in_ref, pre_ref, sent_ref, kept_ref):
    width = sent_ref.shape[2]
    columns = pl.ds(pl.multiple_of(pl.program_id(0) * width, width), width)
    store_product(ffn_in_ref[...], pre_ref[:, columns], scalars[0], sent_ref, kept_ref)


def in_weights(scalars, ffn_in, grad_pre):
    tokens, width = ffn_in.shape
    steps = grad_pre.shape[1] // width
    size = lax.axis_size("dp")
    share = pl.BlockSpec((size // 2, width // size, width), lambda j, *_: (0, 0, j))
    return pl.pallas_call(
        in_weight_kernel,
        grid_spec=pltpu.PrefetchScalarGridSpec(
            num_scalar_prefetch=1,
            grid=(steps,),
            in_specs=[RESIDENT, RESIDENT],
            out_specs=[share, share],
        ),
        out_shape=[pltpu.HBM((size // 2, width // size, steps * width), BF16)] * 2,
        compiler_params=pltpu.CompilerParams(vmem_limit_bytes=VMEM_LIMIT),
        cost_estimate=pl.CostEstimate(flops=0, bytes_accessed=0, transcendentals=0),
    )(scalars, *resident(ffn_in, grad_pre))


def out_weight_kernel(scalars, act_ref, upstream_ref, sent_ref, kept_ref, *, folds):
    width = upstream_ref.shape[1]
    columns = pl.ds(pl.multiple_of(pl.program_id(0) * width, width), width)
    store_product(act_ref[:, columns], upstream_ref[...], scalars[0], sent_ref, kept_ref, folds)


def out_weights(scalars, act, upstream):
    tokens, width = upstream.shape
    units = act.shape[1]
    size = lax.axis_size("dp")
    folds = steps = units // width
    shape = (size // 2, width // size, units)
    share = pl.BlockSpec((size // 2 // steps,) + shape[1:], lambda j, *_: (j, 0, 0))
    return pl.pallas_call(
        functools.partial(out_weight_kernel, folds=folds),
        grid_spec=pltpu.PrefetchScalarGridSpec(
            num_scalar_prefetch=1,
            grid=(steps,),
            in_specs=[RESIDENT, RESIDENT],
            out_specs=[share, share],
        ),
        out_shape=[pltpu.HBM(shape, BF16)] * 2,
        compiler_params=pltpu.CompilerParams(vmem_limit_bytes=VMEM_LIMIT),
        cost_estimate=pl.CostEstimate(flops=0, bytes_accessed=0, transcendentals=0),
    )(scalars, *resident(act, upstream))


def middle_kernel(scalars, *refs, seqs, chunk):
    context_refs, hidden_refs = refs[:seqs], refs[seqs : 2 * seqs]
    upstream_ref, w_out_ref, gain_ref, w_in_ref, w_ffn_out_ref = refs[2 * seqs : 2 * seqs + 5]
    act_ref, grad_pre_ref, ffn_in_ref, out_kept_ref, out_sent_ref = refs[2 * seqs + 5 : 2 * seqs + 10]
    grad_low_ref, grad_context_ref, sent_ref, kept_ref, grad_gain_ref = refs[
        2 * seqs + 10 : 2 * seqs + 15
    ]
    mixed_ref, total_ref, back_ref = refs[2 * seqs + 15 :]
    tokens, width = mixed_ref.shape
    count = tokens // seqs
    columns = w_in_ref.shape[1]
    step = pl.program_id(0)
    here = pl.ds(pl.multiple_of(step * columns, columns), columns)
    pieces = [
        (slice(start, start + chunk), start // count, slice(start % count, start % count + chunk))
        for start in range(0, tokens, chunk)
    ]

    @pl.when(step == 0)
    def _():
        for rows, seq, local in pieces:
            mixed = hidden_refs[seq][local, :].astype(F32)
            mixed = mixed + dot(context_refs[seq][local, :], w_out_ref[...], 1, 0)
            mixed_ref[rows, :] = mixed
            total_ref[rows, :] = mixed
            back_ref[rows, :] = jnp.zeros((chunk, width), F32)
            ffn_in_ref[rows, :] = (mixed * inverse_of(mixed) * gain_ref[...]).astype(BF16)

    for rows, _, _ in pieces:
        pre = dot(ffn_in_ref[rows, :], w_in_ref[...], 1, 0)
        grad_act = dot(upstream_ref[rows, :], w_ffn_out_ref[...], 1, 1)
        below = 0.5 + 0.5 * lax.erf(pre * 0.7071067811865476)
        density = jnp.exp2(pre * pre * (-0.5 * LOG2E)) * 0.3989422804014327
        act = (pre * below).astype(BF16)
        grad_pre = (grad_act * (below + pre * density)).astype(BF16)
        act_ref[rows, here] = act
        grad_pre_ref[rows, here] = grad_pre
        total_ref[rows, :] += dot(act, w_ffn_out_ref[...], 1, 0)
        back_ref[rows, :] += dot(grad_pre, w_in_ref[...], 1, 1)

    @pl.when(step == pl.num_programs(0) - 1)
    def _():
        grad_gain = jnp.zeros(gain_ref.shape, F32)
        weight = None
        for rows, seq, local in pieces:
            half, local_half = local.start // (count // 2), slice(
                local.start % (count // 2), local.start % (count // 2) + chunk
            )
            layer_out = total_ref[rows, :].astype(BF16)

            @pl.when(scalars[1] == half)
            def _():
                out_kept_ref[scalars[1] * seqs + seq, local_half, :] = layer_out

            @pl.when(scalars[1] != half)
            def _():
                out_sent_ref[seq, local_half, :] = layer_out

            mixed = mixed_ref[rows, :]
            inverse = inverse_of(mixed)
            normed = mixed * inverse
            back = back_ref[rows, :]
            grad_gain += jnp.sum(back * normed, axis=0, keepdims=True)
            back = back * gain_ref[...]
            mean = jnp.mean(back * normed, axis=1, keepdims=True)
            grad = upstream_ref[rows, :].astype(F32) + inverse * (back - normed * mean)
            low = grad.astype(BF16)
            grad_low_ref[rows, :] = low
            grad_context_ref[rows, :] = dot(low, w_out_ref[...], 1, 1).astype(BF16)
            part = dot(context_refs[seq][local, :], low, 0, 0)
            weight = part if weight is None else weight + part
        grad_gain_ref[...] = grad_gain
        store_shares(weight, scalars[0], sent_ref, kept_ref)


def middle(
    scalars, contexts, hidden, upstream, w_out, gain, w_in, w_ffn_out, columns=512, chunk=256
):
    tokens, width = upstream.shape
    units = w_in.shape[1]
    seqs = len(contexts)
    size = lax.axis_size("dp")
    once = pl.Buffered(1)

    def whole(*shape):
        return pl.BlockSpec(shape, lambda j, *_: (0,) * len(shape), pipeline_mode=once)

    shares = (size // 2, width // size, width)
    low = pltpu.HBM((tokens, width), BF16)
    return pl.pallas_call(
        functools.partial(middle_kernel, seqs=seqs, chunk=chunk),
        grid_spec=pltpu.PrefetchScalarGridSpec(
            num_scalar_prefetch=1,
            grid=(units // columns,),
            in_specs=[RESIDENT] * (2 * seqs + 1)
            + [
                whole(width, width),
                whole(1, width),
                pl.BlockSpec((width, columns), lambda j, *_: (0, j)),
                pl.BlockSpec((columns, width), lambda j, *_: (j, 0)),
            ],
            out_specs=[RESIDENT] * 3
            + [whole(2 * seqs, tokens // seqs // 2, width), whole(seqs, tokens // seqs // 2, width)]
            + [whole(tokens, width)] * 2
            + [whole(*shares), whole(*shares), whole(1, width)],
            scratch_shapes=[pltpu.VMEM((tokens, width), F32)] * 3,
        ),
        out_shape=[
            pltpu.VMEM((tokens, units), BF16),
            pltpu.VMEM((tokens, units), BF16),
            pltpu.VMEM((tokens, width), BF16),
            pltpu.HBM((2 * seqs, tokens // seqs // 2, width), BF16),
            pltpu.HBM((seqs, tokens // seqs // 2, width), BF16),
            low,
            low,
        ]
        + [pltpu.HBM(shares, BF16)] * 2
        + [jax.ShapeDtypeStruct((1, width), F32)],
        compiler_params=pltpu.CompilerParams(vmem_limit_bytes=VMEM_LIMIT),
        cost_estimate=pl.CostEstimate(
            flops=8 * tokens * width * units, bytes_accessed=20 * 2**20, transcendentals=0
        ),
    )(
        scalars,
        *resident(*contexts, *hidden, upstream),
        in_hbm(w_out),
        gain.reshape(1, width),
        in_hbm(w_in),
        in_hbm(w_ffn_out),
    )


def bits_of(size):
    return size.bit_length() - 1


def flip(axis, mask):
    size = lax.axis_size(axis)
    return [(index, index ^ mask) for index in range(size)]


def swap_blk(values):
    return lax.ppermute(values, "blk", flip("blk", 1))


def pick(values, index, axis):
    return lax.dynamic_index_in_dim(values, index, axis, keepdims=False)


def part_of(values, index, axis):
    share = values.shape[axis] // 2
    return lax.dynamic_slice_in_dim(values, index * share, share, axis)


def put_got(own, whole, got):
    return lax.dynamic_update_slice_in_dim(whole, got, (1 - own) * got.shape[0], 0)


def in_order(own, kept, got, axis):
    share = kept.shape[axis]
    shape = kept.shape[:axis] + (2 * share,) + kept.shape[axis + 1 :]
    both = lax.dynamic_update_slice_in_dim(jnp.zeros(shape, kept.dtype), kept, own * share, axis)
    return lax.dynamic_update_slice_in_dim(both, got, (1 - own) * share, axis)


def join(parts, axis):
    return parts[0] if len(parts) == 1 else jnp.concatenate(parts, axis)


class Term:
    def __init__(self, values, bits):
        self.values = values.reshape((2,) * len(bits) + values.shape[1:])
        self.bits = bits
        self.fixed = {}
        self.rows = (0, values.shape[1])
        self.columns = (0, values.shape[2])

    def narrowed(self, fixed=None, rows=None, columns=None):
        other = copy.copy(self)
        other.fixed = {**self.fixed, **(fixed or {})}
        if rows is not None:
            other.rows = (self.rows[0] + rows[0], rows[1])
        if columns is not None:
            other.columns = (self.columns[0] + columns[0], columns[1])
        return other

    def read(self):
        starts = [self.fixed.get(bit, 0) for bit in self.bits] + [self.rows[0], self.columns[0]]
        sizes = [1 if bit in self.fixed else 2 for bit in self.bits]
        left = math.prod(sizes)
        part = lax.dynamic_slice(self.values, starts, sizes + [self.rows[1], self.columns[1]])
        return part.reshape((left, self.rows[1], self.columns[1])).astype(F32)


class Shares:
    def __init__(self, shares, order):
        self.left = list(range(1, bits_of(lax.axis_size("dp"))))[::-1]
        self.order = [0] + order
        self.shares = shares
        self.by_column = False
        self.widths = []
        self.got = None
        self.parts = []

    def joined(self, narrow, axis):
        sums = [sum(term.narrowed(**narrow(term)).read() for term in terms) for terms in self.parts]
        return join([total.astype(BF16) for total in sums], axis)

    def keep(self, narrow):
        self.kept = self.joined(narrow, 2)

    def send(self):
        if not self.order or self.got is not None:
            return
        stage = self.order[0]
        own = lax.axis_index("blk")
        if stage == 0:
            self.got = [lax.ppermute(sent, "dp", flip("dp", 1)) for sent, _ in self.shares]
        elif stage == "last":
            self.kept = self.joined(lambda term: {}, 2)[0]
            self.got = swap_blk(self.kept)
        elif stage == "blk":

            def half(index):
                return lambda term: {
                    "columns": (index * (term.columns[1] // 2), term.columns[1] // 2)
                }

            self.widths = [terms[0].columns[1] // 2 for terms in self.parts]
            self.got = swap_blk(self.joined(half(1 - own), 2))
            self.keep(half(own))
        else:
            mine = (lax.axis_index("dp") >> stage) & 1
            sent = self.joined(lambda term: {"fixed": {stage: 1 - mine}}, 2)
            self.got = lax.ppermute(sent, "dp", flip("dp", 1 << stage))
            self.keep(lambda term: {"fixed": {stage: mine}})
            self.left = [bit for bit in self.left if bit != stage]

    def receive(self):
        stage = self.order.pop(0)
        got, self.got = self.got, None
        if stage == 0:
            self.parts = [
                [Term(kept, self.left), Term(new, self.left)]
                for (_, kept), new in zip(self.shares, got)
            ]
        elif stage == "last":
            if self.by_column:
                total = in_order(lax.axis_index("blk"), self.kept, got, 1).astype(F32)
                half = total.shape[1] // 2
                parts, start = [], 0
                for width in self.widths:
                    parts.append(total[:, start : start + width])
                    parts.append(total[:, half + start : half + start + width])
                    start += width
                self.total = jnp.concatenate(parts, axis=1)
            else:
                self.total = self.kept.astype(F32) + got.astype(F32)
        else:
            self.by_column = self.by_column or stage == "blk"
            self.parts = [[Term(self.kept, self.left), Term(got, self.left)]]

    def take_over(self, other):
        rows = self.parts[0][0].rows[1]
        for terms in other.parts:
            for start in range(0, terms[0].rows[1], rows):
                self.parts.append([term.narrowed(rows=(start, rows)) for term in terms])
                self.widths.append(terms[0].columns[1])


def receive(shares, *values):
    shares = [share for share in shares if share.got is not None]
    gots, values = lax.optimization_barrier(([share.got for share in shares], values))
    for share, got in zip(shares, gots):
        share.got = got
        share.receive()
    return values if len(values) > 1 else values[0]


def body(
    hidden,
    lengths,
    flags,
    buckets,
    g_attn,
    w_query,
    w_key,
    w_value,
    w_out,
    g_ffn,
    w_in,
    w_ffn_out,
    bias_table,
    cotangent,
):
    own = lax.axis_index("blk")
    size = lax.axis_size("dp")
    rest = list(range(1, bits_of(size)))
    first, second, later = rest[:1], rest[1:2], rest[2:]
    width = hidden.shape[2]
    seqs = hidden.shape[0] // 2
    count = hidden.shape[1] * 2
    tokens = seqs * count
    each = range(seqs)
    buckets_used, heads = bias_table.shape
    bias_width = 2 * count - LANES
    length = 2 * count

    with jax.named_scope("exchange_in"):
        def take(values, start, number):
            kept = lax.dynamic_slice_in_dim(values, own * seqs + start, number, 0)
            return kept, lax.dynamic_slice_in_dim(values, (1 - own) * seqs + start, number, 0)

        sent = lax.dynamic_slice_in_dim(hidden, (1 - own) * seqs, 1, 0)
        hidden_got = [swap_blk(sent)]
        hidden, cotangent, sent = lax.optimization_barrier((hidden, cotangent, sent))
        hidden_kept = [
            lax.dynamic_slice_in_dim(hidden, own * seqs + seq, 1, 0) for seq in each
        ]
        hidden_sent = [
            lax.dynamic_slice_in_dim(hidden, (1 - own) * seqs + seq, 1, 0) for seq in each
        ]
        early = 3 * count // 16
        upstream_kept = lax.dynamic_slice_in_dim(cotangent, own * seqs, seqs, 0)
        upstream_sent = lax.dynamic_slice_in_dim(cotangent, (1 - own) * seqs, seqs, 0)
        upstream_sent = [upstream_sent[:, :early], upstream_sent[:, early:]]
        valid_all = jnp.where(flags == 1, lengths[:, 1], lengths[:, 0])
        valid = lax.dynamic_slice_in_dim(valid_all, own * seqs, seqs, 0)
        scalars = jnp.stack([lax.axis_index("dp") & 1, own]).astype(jnp.int32)

    with jax.named_scope("bias"):
        w_all = jnp.stack([w_query, w_key, w_value])
        one_hot = (
            buckets[None, :] == jnp.arange(buckets_used, dtype=jnp.int32)[:, None]
        ).astype(F32)
        one_hot = jnp.pad(one_hot, ((0, 0), (0, length - buckets.shape[0])))
        vector = lax.dot_general(
            bias_table * LOG2E,
            one_hot,
            (((0,), (0,)), ((), ())),
            precision=lax.Precision.HIGHEST,
        )
        bias = expand_bias(jnp.roll(vector, -(LANES - 1), axis=1), bias_width)

    with jax.named_scope("exchange_in"):
        ready = (hidden_kept, hidden_sent, upstream_kept, upstream_sent, w_all, bias, valid, scalars)
        ready, hidden_got[0] = lax.optimization_barrier((ready, hidden_got[0]))
        hidden_kept, hidden_sent, upstream_kept, upstream_sent, w_all, bias, valid, scalars = ready
        hidden_got += [swap_blk(sent) for sent in hidden_sent[1:]]

    contexts, saved, hidden_seq, attn_in_seq = [], [], [], []
    for seq in each:
        with jax.named_scope("project"):
            kept, got = hidden_kept[seq], hidden_got[seq]
            if seq > 0:
                got, contexts[-1] = lax.optimization_barrier((got, contexts[-1]))
            if seq == seqs - 1:
                late, got = lax.optimization_barrier((upstream_sent[1], got))
                late = swap_blk(late)
            whole_seq, attn_in, projected = project(scalars, kept, got, g_attn, w_all)
            if seq == 0:
                first_part, projected = lax.optimization_barrier(
                    (upstream_sent[0], projected)
                )
                upstream_got = swap_blk(first_part)
            hidden_seq.append(whole_seq)
            attn_in_seq.append(attn_in)
        with jax.named_scope("attend"):
            context, *rest_of = attend(projected, bias, valid, seq)
            contexts.append(context)
            saved.append([projected, *rest_of])

    with jax.named_scope("middle"):
        inputs, late = lax.optimization_barrier((jnp.concatenate(hidden_seq, axis=0), late))
        upstream_got = jnp.concatenate([upstream_got, late], axis=1)
        upstream = in_order(own, upstream_kept, upstream_got, 1).reshape(tokens, width)
        act, grad_pre, ffn_in, output_kept, output_sent, grad_low, grad_context, *rest_of = middle(
            scalars, contexts, hidden_seq, upstream, w_out, g_ffn, w_in, w_ffn_out
        )
        sent, kept, grad_g_ffn = rest_of
    with jax.named_scope("output"):
        output_got = swap_blk(output_sent)

    with jax.named_scope("ffn_weights"):
        out_shares = Shares([out_weights(scalars, act, upstream)], first + ["blk"] + second)
        out_shares.send()
        in_sent, in_kept = in_weights(scalars, ffn_in, grad_pre)
        in_sent, in_kept = receive([out_shares], in_sent, in_kept)
        in_shares = Shares([(in_sent, in_kept)], second + first + ["blk"])
        in_shares.send()
        out_shares.send()
        grad_context = receive([in_shares], grad_context)
        in_shares.send()

    with jax.named_scope("attend_back"):
        pairs = width // LANES
        parting = 2 * pairs // 3
        weights = (w_query, w_key, w_value)
        bias_one, one_sent, one_kept, before = attend_back(
            scalars, saved, attn_in_seq, grad_context, weights, bias_width,
            (0, parting), None,
        )
        one_shares = Shares([(one_sent, one_kept), (sent, kept)], second + first + later + ["last"])
        one_shares.send()
        before, grad_context, output_got = receive(
            [out_shares, in_shares], before, grad_context, output_got
        )
        out_shares.send()
        in_shares.send()
        before, grad_context = receive([one_shares], before, grad_context)
        one_shares.send()
        bias_two, two_sent, two_kept, input_kept, input_sent, grad_g_attn = attend_back(
            scalars, saved, attn_in_seq, grad_context, weights, bias_width,
            (parting, pairs), (before, inputs, grad_low, g_attn),
        )
        two_shares = Shares([(two_sent, two_kept)], first + second + later + ["last"])
        two_shares.send()
        bias_one, bias_two, input_sent = receive(
            [one_shares, in_shares, out_shares], bias_one, bias_two, input_sent
        )

    with jax.named_scope("rounds"):
        for shares in (out_shares, in_shares, one_shares):
            shares.send()
        folded = fold_bias(bias_one, length), fold_bias(bias_two, length)
        *folded, input_sent = receive(
            [two_shares, one_shares, out_shares, in_shares], *folded, input_sent
        )
        in_shares.take_over(out_shares)
        in_shares.order = later + ["last"]
        input_got = swap_blk(input_sent)
        two_shares.send()
        in_shares.send()

    with jax.named_scope("small"):
        table = lax.dot_general(
            one_hot,
            jnp.concatenate(folded, axis=0),
            (((1,), (1,)), ((), ())),
            precision=lax.Precision.HIGHEST,
        )
        flat = jnp.concatenate([grad_g_attn[0], grad_g_ffn[0], table.reshape(-1)])
        flat = jnp.pad(flat, (0, -flat.shape[0] % 1024)).reshape(-1, LANES)
        if size > 1:
            flat = flat + lax.ppermute(flat, "dp", flip("dp", 1))
        small_bits = list(range(1, bits_of(size))) + ["blk"]

    def small_step(flat, chains, *others):
        if not small_bits:
            flat, *others = receive(chains, flat, *others, 0)[:-1]
            return flat, *others
        bit = small_bits.pop(0)
        got = swap_blk(flat) if bit == "blk" else lax.ppermute(flat, "dp", flip("dp", 1 << bit))
        flat, got, *others = receive(chains, flat, got, *others)
        return flat + got, *others

    with jax.named_scope("rounds"):
        one_shares.send()
        (flat,) = small_step(flat, [two_shares])
        two_shares.send()
        flat, input_got = small_step(flat, [two_shares, in_shares], input_got)
        chains = [two_shares, one_shares, in_shares]
        while any(shares.order for shares in chains) or small_bits:
            for shares in chains:
                shares.send()
            (flat,) = small_step(flat, chains)

    one, two = one_shares.total, two_shares.total
    pieces = jnp.split(one[:, : 3 * LANES * parting], 3 * parting, axis=1)
    pieces += jnp.split(two, 3 * (pairs - parting), axis=1)
    grad_query_w, grad_key_w, grad_value_w = (
        jnp.concatenate(pieces[part::3], axis=1) for part in range(3)
    )
    grad_out_w = one[:, 3 * LANES * parting :]
    two = in_shares.total
    units = w_in.shape[1]
    grad_in = two[:, :units]
    grad_ffn_out = jnp.concatenate(
        [two[:, start : start + width] for start in range(units, two.shape[1], width)], axis=0
    )
    with jax.named_scope("output"):
        output = put_got(own, output_kept, output_got)
        input_grad = put_got(own, input_kept, input_got)

    with jax.named_scope("small"):
        flat = flat.reshape(-1)
        share = width // size
        at = lax.axis_index("dp") * share
        gain_attn = lax.dynamic_slice_in_dim(flat[:width], at, share)
        gain_ffn = lax.dynamic_slice_in_dim(flat[width : 2 * width], at, share)
        table = flat[2 * width : 2 * width + buckets_used * heads].reshape(buckets_used, heads)

    return (
        output,
        input_grad,
        gain_attn,
        grad_query_w,
        grad_key_w,
        grad_value_w,
        grad_out_w,
        gain_ffn,
        grad_in,
        grad_ffn_out,
        table,
    )


def solution(mesh):
    split = P("dp", "blk", None)
    rows = P("dp", None)
    in_specs = (split, rows, P("dp")) + (P(),) * 10 + (split,)
    out_specs = (split, split, P("dp")) + (rows,) * 4 + (P("dp"), rows, rows, P())
    return jax.shard_map(body, mesh=mesh, in_specs=in_specs, out_specs=out_specs, check_vma=False)
```

```python
import copy
import functools
import math

import jax
import jax.numpy as jnp
from jax import lax
from jax.experimental import pallas as pl
from jax.experimental.pallas import tpu as pltpu
from jax.sharding import PartitionSpec as P

EPSILON = 1e-06
MASKED = -1000000000.0
SCALING = 0.125
LOG2E = 1.4426950408889634
LN2 = 0.6931471805599453
HEAD = 64
LANES = 128
VMEM_LIMIT = 32 * 2**20
BF16 = jnp.bfloat16
F32 = jnp.float32


def dot(left, right, left_dim, right_dim):
    return lax.dot_general(
        left, right, (((left_dim,), (right_dim,)), ((), ())), preferred_element_type=F32
    )


RESIDENT = pl.BlockSpec(memory_space=pltpu.VMEM)


def in_hbm(values):
    return pltpu.with_memory_space_constraint(values, pltpu.HBM)


def resident(*values):
    return [pltpu.with_memory_space_constraint(v, pltpu.VMEM) for v in values]


def expand_kernel(vector_ref, out_ref):
    group, _, width = vector_ref.shape
    for head in range(group):
        rows = jnp.broadcast_to(vector_ref[head], (LANES, width))
        moved = pltpu.roll(rows, 0, 1, stride=1, stride_axis=0)
        out_ref[head] = moved[:, : out_ref.shape[2]]


def expand_bias(vector, width):
    heads, length = vector.shape
    group = 4 if heads % 4 == 0 else 1
    return pl.pallas_call(
        expand_kernel,
        grid=(heads // group,),
        in_specs=[pl.BlockSpec((group, 1, length), lambda h: (h, 0, 0))],
        out_specs=pl.BlockSpec((group, LANES, width), lambda h: (h, 0, 0)),
        out_shape=jax.ShapeDtypeStruct((heads, LANES, width), F32),
        compiler_params=pltpu.CompilerParams(vmem_limit_bytes=VMEM_LIMIT),
    )(vector.reshape(heads, 1, length))


def fold_kernel(grad_ref, out_ref):
    width = grad_ref.shape[2]
    length = out_ref.shape[2]
    pad = jnp.zeros((8, length - width), F32)
    for head in range(grad_ref.shape[0]):
        total = jnp.zeros((8, length), F32)
        for start in range(0, LANES, 8):
            rows = jnp.concatenate([grad_ref[head, start : start + 8, :], pad], axis=1)
            total = total + pltpu.roll(rows, LANES - 8 - start, 1)
        folded = total[7:8]
        for row in range(7):
            folded = folded + pltpu.roll(total[row : row + 1], 7 - row, 1)
        out_ref[head] = jnp.broadcast_to(folded, (8, length))


def fold_bias(grad, length):
    heads, _, width = grad.shape
    group = 4 if heads % 4 == 0 else 1
    return pl.pallas_call(
        fold_kernel,
        grid=(heads // group,),
        in_specs=[pl.BlockSpec((group, LANES, width), lambda h: (h, 0, 0))],
        out_specs=pl.BlockSpec((group, 8, length), lambda h: (h, 0, 0)),
        out_shape=jax.ShapeDtypeStruct((heads, 8, length), F32),
        compiler_params=pltpu.CompilerParams(vmem_limit_bytes=VMEM_LIMIT),
        cost_estimate=pl.CostEstimate(flops=0, bytes_accessed=0, transcendentals=0),
    )(in_hbm(grad))[:, 0]


def inverse_of(values):
    return lax.rsqrt(jnp.mean(values * values, axis=1, keepdims=True) + EPSILON)


def project_kernel(scalars, kept_ref, got_ref, gain_ref, w_ref, hidden_ref, attn_in_ref, out_ref):
    half = kept_ref.shape[1]
    step = pl.program_id(0)

    @pl.when(step == 0)
    def _():
        for ref, place in ((kept_ref, scalars[1]), (got_ref, 1 - scalars[1])):
            rows = pl.ds(pl.multiple_of(place * half, half), half)
            hidden_ref[rows, :] = ref[0]
            values = ref[0].astype(F32)
            attn_in_ref[rows, :] = (values * inverse_of(values) * gain_ref[...]).astype(BF16)

    scale = jnp.where(step == 0, SCALING * LOG2E, 1.0)
    out_ref[0] = (dot(attn_in_ref[...], w_ref[0], 1, 0) * scale).astype(BF16)


def project(scalars, kept, got, gain, weights):
    _, half, width = kept.shape
    count = 2 * half
    once = pl.Buffered(1)

    def whole(*shape):
        return pl.BlockSpec(shape, lambda j, *_: (0,) * len(shape), pipeline_mode=once)

    return pl.pallas_call(
        project_kernel,
        grid_spec=pltpu.PrefetchScalarGridSpec(
            num_scalar_prefetch=1,
            grid=(weights.shape[0],),
            in_specs=[
                whole(1, half, width),
                whole(1, half, width),
                whole(1, width),
                pl.BlockSpec((1, width, width), lambda j, *_: (j, 0, 0)),
            ],
            out_specs=[
                whole(count, width),
                whole(count, width),
                pl.BlockSpec((1, count, width), lambda j, *_: (j, 0, 0)),
            ],
        ),
        out_shape=[
            jax.ShapeDtypeStruct((count, width), BF16),
            jax.ShapeDtypeStruct((count, width), BF16),
            jax.ShapeDtypeStruct((weights.shape[0], count, width), BF16),
        ],
        compiler_params=pltpu.CompilerParams(vmem_limit_bytes=VMEM_LIMIT),
        cost_estimate=pl.CostEstimate(
            flops=6 * count * width * width, bytes_accessed=8 * 2**20, transcendentals=0
        ),
    )(scalars, kept, got, gain.reshape(1, width), weights)


def attend_kernel(
    valid, q_ref, k_ref, v_ref, bias_ref, out_ref, copy_ref, weights_ref, inverse_ref, *, chunk, seq
):
    limit = valid[seq]
    count = q_ref.shape[1]
    pair = pl.program_id(0)
    columns = pl.ds(pl.multiple_of(pair * LANES, LANES), LANES)
    queries, keys, values = (ref[0].astype(F32) for ref in (q_ref, k_ref, v_ref))
    lane = lax.broadcasted_iota(jnp.int32, (count, LANES), 1)
    row = lax.broadcasted_iota(jnp.int32, (count, LANES), 0)
    heads = []
    for head in range(2):
        mine = (lane // HEAD) == head
        extra = lane == (1 - head) * HEAD
        mask = jnp.where(extra & (row >= limit), MASKED, 0.0)
        heads.append(
            (
                jnp.where(mine, queries, jnp.where(extra, 1.0, 0.0)).astype(BF16),
                jnp.where(mine, keys, mask).astype(BF16),
                jnp.where(mine, values, 1.0).astype(BF16),
            )
        )
    first = lax.broadcasted_iota(jnp.int32, (chunk, LANES), 1) < HEAD
    units = [(step, head) for step in range(count // chunk) for head in range(2)]

    def scores(unit):
        step, head = unit
        rows = slice(step * chunk, (step + 1) * chunk)
        windows = [
            bias_ref[head, :, count - LANES * (1 + block) : 2 * count - LANES * (1 + block)]
            for block in range(step * chunk // LANES, (step + 1) * chunk // LANES)
        ]
        return dot(heads[head][0][rows], heads[head][1], 1, 1) + jnp.concatenate(windows, axis=0)

    ahead = 2
    logits = {unit: scores(unit) for unit in units[:ahead]}
    sums = {}
    for place, unit in enumerate(units):
        step, head = unit
        rows = slice(step * chunk, (step + 1) * chunk)
        if place + ahead < len(units):
            logits[units[place + ahead]] = scores(units[place + ahead])
        top = jnp.max(logits[unit], axis=1, keepdims=True)
        weights = jnp.exp2(logits[unit] - top).astype(BF16)
        weights_ref[head, rows, :] = weights
        sums[unit] = dot(weights, heads[head][2], 1, 0)
        if head == 1:
            one, two = sums[step, 0], sums[step, 1]
            inverse = 1.0 / pltpu.roll(jnp.where(first, two, one), HEAD, 1)
            inverse_ref[rows, :] = inverse
            context = (jnp.where(first, one, two) * inverse).astype(BF16)
            out_ref[rows, columns] = context
            copy_ref[rows, :] = context


def projections_of(count, pair):
    return [
        pl.BlockSpec((1, count, LANES), lambda *at, part=part: (part, 0, pair(*at)))
        for part in range(3)
    ]


def attend(projected, bias, valid, seq, chunk=256):
    _, count, width = projected.shape
    block = pl.BlockSpec((count, LANES), lambda p, *_: (0, p))
    return pl.pallas_call(
        functools.partial(attend_kernel, chunk=chunk, seq=seq),
        grid_spec=pltpu.PrefetchScalarGridSpec(
            num_scalar_prefetch=1,
            grid=(width // LANES,),
            in_specs=[
                *projections_of(count, lambda p, *_: p),
                pl.BlockSpec((2, LANES, bias.shape[2]), lambda p, *_: (p, 0, 0)),
            ],
            out_specs=[
                RESIDENT,
                block,
                pl.BlockSpec((2, count, count), lambda p, *_: (p, 0, 0)),
                block,
            ],
        ),
        out_shape=[
            pltpu.VMEM((count, width), BF16),
            pltpu.HBM((count, width), BF16),
            pltpu.HBM((width // HEAD, count, count), BF16),
            pltpu.HBM((count, width), F32),
        ],
        compiler_params=pltpu.CompilerParams(vmem_limit_bytes=VMEM_LIMIT),
        cost_estimate=pl.CostEstimate(
            flops=32 * count * count * width, bytes_accessed=12 * 2**20, transcendentals=0
        ),
    )(valid, *[projected] * 3, bias)


def store_shares(grad, core, sent_ref, kept_ref, start=0, folds=1):
    count, rows, width = sent_ref.shape
    grad = grad.astype(BF16) if rows % 16 == 0 else grad
    for group in range(count):
        for fold in range(folds):
            place = (2 * group * folds + fold) * rows
            even = grad[place : place + rows]
            place += folds * rows
            odd = grad[place : place + rows]
            at = fold * (width // folds) + start
            columns = slice(at, at + grad.shape[1])
            sent_ref[group, :, columns] = jnp.where(core == 0, odd, even).astype(BF16)
            kept_ref[group, :, columns] = jnp.where(core == 0, even, odd).astype(BF16)


def attend_back_kernel(scalars, *refs, seqs, steps, finish):
    refs = list(refs)

    def some(count):
        taken = refs[:count]
        del refs[:count]
        return taken

    projected_refs = [some(3) for _ in range(seqs)]
    weights_refs, inverse_refs = some(seqs), some(seqs)
    attn_in_refs = some(seqs)
    ctx_refs = some(seqs)
    grad_ref, wq_ref, wk_ref, wv_ref = some(4)
    if finish:
        before_ref, hidden_ref, mid_ref, gain_ref = some(4)
    bias_ref, sent_ref, kept_ref = some(3)
    if finish:
        in_kept_ref, in_sent_ref, grad_gain_ref, back_ref = some(4)
    else:
        out_ref, back_ref = some(2)
    core, own = scalars[0], scalars[1]
    count = projected_refs[0][0].shape[1]
    lane = lax.broadcasted_iota(jnp.int32, (count, LANES), 1)

    step = pl.program_id(0)

    @pl.when(step == 0)
    def _():
        back_ref[...] = jnp.zeros_like(back_ref)

    @pl.when(step < steps)
    def _():
        bias_ref[...] = jnp.zeros_like(bias_ref)
        projections = jnp.concatenate([wq_ref[...], wk_ref[...], wv_ref[...]], axis=1)
        units = [(seq, head) for seq in range(seqs) for head in range(2)]
        loaded, scored, low_grads, parts = {}, {}, {}, {}

        def load(seq):
            here = slice(seq * count, (seq + 1) * count)
            queries, keys, values = (ref[0].astype(F32) for ref in projected_refs[seq])
            grads = grad_ref[here, :].astype(F32) * inverse_refs[seq][...]
            products = grads * ctx_refs[seq][...].astype(F32)
            turned = jnp.transpose(queries).astype(BF16), jnp.transpose(grads).astype(BF16)
            loaded[seq] = keys, values, grads, products, turned

        def score(unit):
            seq, head = unit
            if head == 0:
                load(seq)
            _, values, grads, products, _ = loaded[seq]
            mine = (lane // HEAD) == head
            other = (1 - head) * HEAD
            extra = (lane == other) | (lane == other + 1)
            v_head = jnp.where(mine, values, jnp.where(extra, 1.0, 0.0)).astype(BF16)
            delta = jnp.sum(jnp.where(mine, products, 0.0), axis=1, keepdims=True)
            high = delta.astype(BF16).astype(F32)
            spread = jnp.where(lane == other, -high, jnp.where(extra, high - delta, 0.0))
            g_head = jnp.where(mine, grads, spread).astype(BF16)
            scored[unit] = dot(g_head, v_head, 1, 1)

        def weigh(unit):
            seq, head = unit
            grad_logits = weights_refs[seq][head].astype(F32) * scored[unit]
            blocks = count // LANES
            for tile in range(2 * blocks - 1):
                bias_ref[head, :, tile * LANES : (tile + 1) * LANES] += sum(
                    grad_logits[
                        block * LANES : (block + 1) * LANES,
                        (tile + 1 + block - blocks) * LANES : (tile + 2 + block - blocks) * LANES,
                    ]
                    for block in range(blocks)
                    if 0 <= tile + 1 + block - blocks < blocks
                )
            low_grads[unit] = grad_logits.astype(BF16)

        def multiply(unit):
            seq, head = unit
            keys, _, _, _, (queries_t, grads_t) = loaded[seq]
            rows = slice(head * HEAD, (head + 1) * HEAD)
            k_head = jnp.where((lane // HEAD) == head, keys, 0.0).astype(BF16)
            low = low_grads[unit]
            parts[unit] = (
                dot(low, k_head, 1, 0),
                dot(queries_t[rows], low, 1, 0),
                dot(grads_t[rows], weights_refs[seq][head], 1, 0),
            )

        def project(seq):
            here = slice(seq * count, (seq + 1) * count)
            one, two = parts[seq, 0], parts[seq, 1]
            dk = jnp.transpose(jnp.concatenate([one[1], two[1]], axis=0))
            dv = jnp.transpose(jnp.concatenate([one[2], two[2]], axis=0))
            all_grads = jnp.concatenate(
                [(SCALING * (one[0] + two[0])).astype(BF16), (LN2 * dk).astype(BF16), dv.astype(BF16)],
                axis=1,
            )
            back_ref[here, :] += dot(all_grads, projections, 1, 1)
            return dot(attn_in_refs[seq][...], all_grads, 0, 0)

        weight_grad = None
        for place in range(len(units) + 1):
            if place < len(units):
                score(units[place])
            if 0 <= place - 1 < len(units):
                weigh(units[place - 1])
            if 0 <= place - 1:
                seq, head = units[place - 1]
                multiply((seq, head))
                if head == 1:
                    part = project(seq)
                    weight_grad = part if weight_grad is None else weight_grad + part
        store_shares(weight_grad, core, sent_ref, kept_ref)

    @pl.when(step >= steps)
    def _():
        place = step - steps
        half = count // 2
        if not finish:
            out_ref[...] = back_ref[pl.ds(pl.multiple_of(place * half, half), half), :].astype(BF16)
        else:
            start = pl.multiple_of(row_block(place, own, seqs) * half, half)
            back = back_ref[pl.ds(start, half), :] + before_ref[...].astype(F32)
            values = hidden_ref[...].astype(F32)
            inverse = lax.rsqrt(jnp.mean(values * values, axis=1, keepdims=True) + EPSILON)
            normed = values * inverse
            grad_gain = jnp.sum(back * normed, axis=0, keepdims=True)
            back = back * gain_ref[...]
            mean = jnp.mean(back * normed, axis=1, keepdims=True)
            grad = mid_ref[...].astype(F32) + inverse * (back - normed * mean)

            @pl.when(place == 0)
            def _():
                grad_gain_ref[...] = grad_gain

            @pl.when(place > 0)
            def _():
                grad_gain_ref[...] += grad_gain

            @pl.when(place < seqs)
            def _():
                in_sent_ref[0] = grad.astype(BF16)

            @pl.when(place >= seqs)
            def _():
                in_kept_ref[0] = grad.astype(BF16)


def row_block(place, own, seqs):
    return 2 * lax.rem(place, seqs) + jnp.where(place < seqs, 1 - own, own)


def attend_back(
    scalars, saved, attn_in, grads, projections, bias_width, pairs, ends
):
    seqs = len(saved)
    _, count, width = saved[0][0].shape
    size = lax.axis_size("dp")
    rows = width // size
    half = count // 2
    first, last = pairs
    steps = last - first
    once = pl.Buffered(1)

    def early(p):
        return jnp.minimum(p, steps - 1)

    def late(p):
        return jnp.maximum(p - steps, 0)

    weight = pl.BlockSpec((width, LANES), lambda p, *_: (0, first + early(p)))
    probs = pl.BlockSpec((2, count, count), lambda p, *_: (first + early(p), 0, 0))
    shares = pl.BlockSpec((size // 2, rows, 3 * LANES), lambda p, *_: (0, 0, early(p)))
    row = pl.BlockSpec((1, width), lambda p, *_: (0, 0), pipeline_mode=once)

    block = pl.BlockSpec((count, LANES), lambda p, *_: (0, first + early(p)))
    tall = pl.BlockSpec((seqs * count, LANES), lambda p, *_: (0, first + early(p)))
    whole = pl.BlockSpec((count, width), lambda p, *_: (0, 0), pipeline_mode=once)
    projected, contexts, weights, inverses = zip(*saved)
    operands = [v for v in projected for _ in range(3)]
    operands += [*weights, *inverses, *attn_in, *contexts, grads]
    operands = [in_hbm(v) for v in (*operands, *projections)]
    specs = projections_of(count, lambda p, *_: first + early(p)) * seqs
    specs += [probs] * seqs + [block] * seqs + [whole] * seqs
    specs += [block] * seqs + [tall] + [weight] * 3
    share = pltpu.HBM((size // 2, rows, 3 * LANES * steps), BF16)
    out_shape = [pltpu.HBM((2 * steps, LANES, bias_width), F32), share, share]
    out_specs = [pl.BlockSpec((2, LANES, bias_width), lambda p, *_: (early(p), 0, 0)), shares, shares]
    if ends is not None:
        before, hidden, grad_mid, gain = ends
        operands += [in_hbm(before), in_hbm(hidden), in_hbm(grad_mid), gain.reshape(1, width)]
        mixed_up = pl.BlockSpec(
            (half, width), lambda p, scalars: (row_block(late(p), scalars[1], seqs), 0)
        )
        specs += [mixed_up] * 3 + [row]
        out_shape.append(pltpu.HBM((2 * seqs, half, width), BF16))
        out_shape.append(pltpu.HBM((seqs, half, width), BF16))
        out_shape.append(jax.ShapeDtypeStruct((1, width), F32))
        out_specs += [
            pl.BlockSpec(
                (1, half, width),
                lambda p, scalars: (scalars[1] * seqs + jnp.maximum(late(p) - seqs, 0), 0, 0),
            ),
            pl.BlockSpec((1, half, width), lambda p, *_: (jnp.minimum(late(p), seqs - 1), 0, 0)),
            row,
        ]
    else:
        out_shape.append(pltpu.HBM((seqs * count, width), BF16))
        out_specs.append(pl.BlockSpec((half, width), lambda p, *_: (late(p), 0)))
    return pl.pallas_call(
        functools.partial(attend_back_kernel, seqs=seqs, steps=steps, finish=ends is not None),
        grid_spec=pltpu.PrefetchScalarGridSpec(
            num_scalar_prefetch=1,
            grid=(steps + 2 * seqs,),
            in_specs=specs,
            out_specs=out_specs,
            scratch_shapes=[pltpu.VMEM((seqs * count, width), F32)],
        ),
        out_shape=out_shape,
        compiler_params=pltpu.CompilerParams(vmem_limit_bytes=VMEM_LIMIT),
        cost_estimate=pl.CostEstimate(flops=0, bytes_accessed=0, transcendentals=0),
    )(scalars, *operands)


def store_product(left, right, core, sent_ref, kept_ref, folds=1, columns=256):
    for start in range(0, right.shape[1], columns):
        grad = dot(left, right[:, start : start + columns], 0, 0)
        store_shares(grad, core, sent_ref, kept_ref, start, folds)


def in_weight_kernel(scalars, ffn_in_ref, pre_ref, sent_ref, kept_ref):
    width = sent_ref.shape[2]
    columns = pl.ds(pl.multiple_of(pl.program_id(0) * width, width), width)
    store_product(ffn_in_ref[...], pre_ref[:, columns], scalars[0], sent_ref, kept_ref)


def in_weights(scalars, ffn_in, grad_pre):
    tokens, width = ffn_in.shape
    steps = grad_pre.shape[1] // width
    size = lax.axis_size("dp")
    share = pl.BlockSpec((size // 2, width // size, width), lambda j, *_: (0, 0, j))
    return pl.pallas_call(
        in_weight_kernel,
        grid_spec=pltpu.PrefetchScalarGridSpec(
            num_scalar_prefetch=1,
            grid=(steps,),
            in_specs=[RESIDENT, RESIDENT],
            out_specs=[share, share],
        ),
        out_shape=[pltpu.HBM((size // 2, width // size, steps * width), BF16)] * 2,
        compiler_params=pltpu.CompilerParams(vmem_limit_bytes=VMEM_LIMIT),
        cost_estimate=pl.CostEstimate(flops=0, bytes_accessed=0, transcendentals=0),
    )(scalars, *resident(ffn_in, grad_pre))


def out_weight_kernel(scalars, act_ref, upstream_ref, sent_ref, kept_ref, *, folds):
    width = upstream_ref.shape[1]
    columns = pl.ds(pl.multiple_of(pl.program_id(0) * width, width), width)
    store_product(act_ref[:, columns], upstream_ref[...], scalars[0], sent_ref, kept_ref, folds)


def out_weights(scalars, act, upstream):
    tokens, width = upstream.shape
    units = act.shape[1]
    size = lax.axis_size("dp")
    folds = steps = units // width
    shape = (size // 2, width // size, units)
    share = pl.BlockSpec((size // 2 // steps,) + shape[1:], lambda j, *_: (j, 0, 0))
    return pl.pallas_call(
        functools.partial(out_weight_kernel, folds=folds),
        grid_spec=pltpu.PrefetchScalarGridSpec(
            num_scalar_prefetch=1,
            grid=(steps,),
            in_specs=[RESIDENT, RESIDENT],
            out_specs=[share, share],
        ),
        out_shape=[pltpu.HBM(shape, BF16)] * 2,
        compiler_params=pltpu.CompilerParams(vmem_limit_bytes=VMEM_LIMIT),
        cost_estimate=pl.CostEstimate(flops=0, bytes_accessed=0, transcendentals=0),
    )(scalars, *resident(act, upstream))


def middle_kernel(scalars, *refs, seqs, chunk):
    context_refs, hidden_refs = refs[:seqs], refs[seqs : 2 * seqs]
    upstream_ref, w_out_ref, gain_ref, w_in_ref, w_ffn_out_ref = refs[2 * seqs : 2 * seqs + 5]
    act_ref, grad_pre_ref, ffn_in_ref, out_kept_ref, out_sent_ref = refs[2 * seqs + 5 : 2 * seqs + 10]
    grad_low_ref, grad_context_ref, sent_ref, kept_ref, grad_gain_ref = refs[
        2 * seqs + 10 : 2 * seqs + 15
    ]
    mixed_ref, total_ref, back_ref = refs[2 * seqs + 15 :]
    tokens, width = mixed_ref.shape
    count = tokens // seqs
    columns = w_in_ref.shape[1]
    step = pl.program_id(0)
    here = pl.ds(pl.multiple_of(step * columns, columns), columns)
    pieces = [
        (slice(start, start + chunk), start // count, slice(start % count, start % count + chunk))
        for start in range(0, tokens, chunk)
    ]

    @pl.when(step == 0)
    def _():
        for rows, seq, local in pieces:
            mixed = hidden_refs[seq][local, :].astype(F32)
            mixed = mixed + dot(context_refs[seq][local, :], w_out_ref[...], 1, 0)
            mixed_ref[rows, :] = mixed
            total_ref[rows, :] = mixed
            back_ref[rows, :] = jnp.zeros((chunk, width), F32)
            ffn_in_ref[rows, :] = (mixed * inverse_of(mixed) * gain_ref[...]).astype(BF16)

    for rows, _, _ in pieces:
        pre = dot(ffn_in_ref[rows, :], w_in_ref[...], 1, 0)
        grad_act = dot(upstream_ref[rows, :], w_ffn_out_ref[...], 1, 1)
        below = 0.5 + 0.5 * lax.erf(pre * 0.7071067811865476)
        density = jnp.exp2(pre * pre * (-0.5 * LOG2E)) * 0.3989422804014327
        act = (pre * below).astype(BF16)
        grad_pre = (grad_act * (below + pre * density)).astype(BF16)
        act_ref[rows, here] = act
        grad_pre_ref[rows, here] = grad_pre
        total_ref[rows, :] += dot(act, w_ffn_out_ref[...], 1, 0)
        back_ref[rows, :] += dot(grad_pre, w_in_ref[...], 1, 1)

    @pl.when(step == pl.num_programs(0) - 1)
    def _():
        grad_gain = jnp.zeros(gain_ref.shape, F32)
        weight = None
        for rows, seq, local in pieces:
            half, local_half = local.start // (count // 2), slice(
                local.start % (count // 2), local.start % (count // 2) + chunk
            )
            layer_out = total_ref[rows, :].astype(BF16)

            @pl.when(scalars[1] == half)
            def _():
                out_kept_ref[scalars[1] * seqs + seq, local_half, :] = layer_out

            @pl.when(scalars[1] != half)
            def _():
                out_sent_ref[seq, local_half, :] = layer_out

            mixed = mixed_ref[rows, :]
            inverse = inverse_of(mixed)
            normed = mixed * inverse
            back = back_ref[rows, :]
            grad_gain += jnp.sum(back * normed, axis=0, keepdims=True)
            back = back * gain_ref[...]
            mean = jnp.mean(back * normed, axis=1, keepdims=True)
            grad = upstream_ref[rows, :].astype(F32) + inverse * (back - normed * mean)
            low = grad.astype(BF16)
            grad_low_ref[rows, :] = low
            grad_context_ref[rows, :] = dot(low, w_out_ref[...], 1, 1).astype(BF16)
            part = dot(context_refs[seq][local, :], low, 0, 0)
            weight = part if weight is None else weight + part
        grad_gain_ref[...] = grad_gain
        store_shares(weight, scalars[0], sent_ref, kept_ref)


def middle(
    scalars, contexts, hidden, upstream, w_out, gain, w_in, w_ffn_out, columns=512, chunk=256
):
    tokens, width = upstream.shape
    units = w_in.shape[1]
    seqs = len(contexts)
    size = lax.axis_size("dp")
    once = pl.Buffered(1)

    def whole(*shape):
        return pl.BlockSpec(shape, lambda j, *_: (0,) * len(shape), pipeline_mode=once)

    shares = (size // 2, width // size, width)
    low = pltpu.HBM((tokens, width), BF16)
    return pl.pallas_call(
        functools.partial(middle_kernel, seqs=seqs, chunk=chunk),
        grid_spec=pltpu.PrefetchScalarGridSpec(
            num_scalar_prefetch=1,
            grid=(units // columns,),
            in_specs=[RESIDENT] * (2 * seqs + 1)
            + [
                whole(width, width),
                whole(1, width),
                pl.BlockSpec((width, columns), lambda j, *_: (0, j)),
                pl.BlockSpec((columns, width), lambda j, *_: (j, 0)),
            ],
            out_specs=[RESIDENT] * 3
            + [whole(2 * seqs, tokens // seqs // 2, width), whole(seqs, tokens // seqs // 2, width)]
            + [whole(tokens, width)] * 2
            + [whole(*shares), whole(*shares), whole(1, width)],
            scratch_shapes=[pltpu.VMEM((tokens, width), F32)] * 3,
        ),
        out_shape=[
            pltpu.VMEM((tokens, units), BF16),
            pltpu.VMEM((tokens, units), BF16),
            pltpu.VMEM((tokens, width), BF16),
            pltpu.HBM((2 * seqs, tokens // seqs // 2, width), BF16),
            pltpu.HBM((seqs, tokens // seqs // 2, width), BF16),
            low,
            low,
        ]
        + [pltpu.HBM(shares, BF16)] * 2
        + [jax.ShapeDtypeStruct((1, width), F32)],
        compiler_params=pltpu.CompilerParams(vmem_limit_bytes=VMEM_LIMIT),
        cost_estimate=pl.CostEstimate(
            flops=8 * tokens * width * units, bytes_accessed=20 * 2**20, transcendentals=0
        ),
    )(
        scalars,
        *resident(*contexts, *hidden, upstream),
        in_hbm(w_out),
        gain.reshape(1, width),
        in_hbm(w_in),
        in_hbm(w_ffn_out),
    )


def bits_of(size):
    return size.bit_length() - 1


def flip(axis, mask):
    size = lax.axis_size(axis)
    return [(index, index ^ mask) for index in range(size)]


def swap_blk(values):
    return lax.ppermute(values, "blk", flip("blk", 1))


def pick(values, index, axis):
    return lax.dynamic_index_in_dim(values, index, axis, keepdims=False)


def part_of(values, index, axis):
    share = values.shape[axis] // 2
    return lax.dynamic_slice_in_dim(values, index * share, share, axis)


def put_got(own, whole, got):
    return lax.dynamic_update_slice_in_dim(whole, got, (1 - own) * got.shape[0], 0)


def in_order(own, kept, got, axis):
    share = kept.shape[axis]
    shape = kept.shape[:axis] + (2 * share,) + kept.shape[axis + 1 :]
    both = lax.dynamic_update_slice_in_dim(jnp.zeros(shape, kept.dtype), kept, own * share, axis)
    return lax.dynamic_update_slice_in_dim(both, got, (1 - own) * share, axis)


def join(parts, axis):
    return parts[0] if len(parts) == 1 else jnp.concatenate(parts, axis)


class Term:
    def __init__(self, values, bits):
        self.values = values.reshape((2,) * len(bits) + values.shape[1:])
        self.bits = bits
        self.fixed = {}
        self.rows = (0, values.shape[1])
        self.columns = (0, values.shape[2])

    def narrowed(self, fixed=None, rows=None, columns=None):
        other = copy.copy(self)
        other.fixed = {**self.fixed, **(fixed or {})}
        if rows is not None:
            other.rows = (self.rows[0] + rows[0], rows[1])
        if columns is not None:
            other.columns = (self.columns[0] + columns[0], columns[1])
        return other

    def read(self):
        starts = [self.fixed.get(bit, 0) for bit in self.bits] + [self.rows[0], self.columns[0]]
        sizes = [1 if bit in self.fixed else 2 for bit in self.bits]
        left = math.prod(sizes)
        part = lax.dynamic_slice(self.values, starts, sizes + [self.rows[1], self.columns[1]])
        return part.reshape((left, self.rows[1], self.columns[1])).astype(F32)


class Shares:
    def __init__(self, shares, order):
        self.left = list(range(1, bits_of(lax.axis_size("dp"))))[::-1]
        self.order = [0] + order
        self.shares = shares
        self.by_column = False
        self.widths = []
        self.got = None
        self.parts = []

    def joined(self, narrow, axis):
        sums = [sum(term.narrowed(**narrow(term)).read() for term in terms) for terms in self.parts]
        return join([total.astype(BF16) for total in sums], axis)

    def keep(self, narrow):
        self.kept = self.joined(narrow, 2)

    def send(self):
        if not self.order or self.got is not None:
            return
        stage = self.order[0]
        own = lax.axis_index("blk")
        if stage == 0:
            self.got = [lax.ppermute(sent, "dp", flip("dp", 1)) for sent, _ in self.shares]
        elif stage == "last":
            self.kept = self.joined(lambda term: {}, 2)[0]
            self.got = swap_blk(self.kept)
        elif stage == "blk":

            def half(index):
                return lambda term: {
                    "columns": (index * (term.columns[1] // 2), term.columns[1] // 2)
                }

            self.widths = [terms[0].columns[1] // 2 for terms in self.parts]
            self.got = swap_blk(self.joined(half(1 - own), 2))
            self.keep(half(own))
        else:
            mine = (lax.axis_index("dp") >> stage) & 1
            sent = self.joined(lambda term: {"fixed": {stage: 1 - mine}}, 2)
            self.got = lax.ppermute(sent, "dp", flip("dp", 1 << stage))
            self.keep(lambda term: {"fixed": {stage: mine}})
            self.left = [bit for bit in self.left if bit != stage]

    def receive(self):
        stage = self.order.pop(0)
        got, self.got = self.got, None
        if stage == 0:
            self.parts = [
                [Term(kept, self.left), Term(new, self.left)]
                for (_, kept), new in zip(self.shares, got)
            ]
        elif stage == "last":
            if self.by_column:
                total = in_order(lax.axis_index("blk"), self.kept, got, 1).astype(F32)
                half = total.shape[1] // 2
                parts, start = [], 0
                for width in self.widths:
                    parts.append(total[:, start : start + width])
                    parts.append(total[:, half + start : half + start + width])
                    start += width
                self.total = jnp.concatenate(parts, axis=1)
            else:
                self.total = self.kept.astype(F32) + got.astype(F32)
        else:
            self.by_column = self.by_column or stage == "blk"
            self.parts = [[Term(self.kept, self.left), Term(got, self.left)]]

    def take_over(self, other):
        rows = self.parts[0][0].rows[1]
        for terms in other.parts:
            for start in range(0, terms[0].rows[1], rows):
                self.parts.append([term.narrowed(rows=(start, rows)) for term in terms])
                self.widths.append(terms[0].columns[1])


def receive(shares, *values):
    shares = [share for share in shares if share.got is not None]
    gots, values = lax.optimization_barrier(([share.got for share in shares], values))
    for share, got in zip(shares, gots):
        share.got = got
        share.receive()
    return values if len(values) > 1 else values[0]


def body(
    hidden,
    lengths,
    flags,
    buckets,
    g_attn,
    w_query,
    w_key,
    w_value,
    w_out,
    g_ffn,
    w_in,
    w_ffn_out,
    bias_table,
    cotangent,
):
    own = lax.axis_index("blk")
    size = lax.axis_size("dp")
    rest = list(range(1, bits_of(size)))
    first, second, later = rest[:1], rest[1:2], rest[2:]
    width = hidden.shape[2]
    seqs = hidden.shape[0] // 2
    count = hidden.shape[1] * 2
    tokens = seqs * count
    each = range(seqs)
    buckets_used, heads = bias_table.shape
    bias_width = 2 * count - LANES
    length = 2 * count

    with jax.named_scope("exchange_in"):
        def take(values, start, number):
            kept = lax.dynamic_slice_in_dim(values, own * seqs + start, number, 0)
            return kept, lax.dynamic_slice_in_dim(values, (1 - own) * seqs + start, number, 0)

        sent = lax.dynamic_slice_in_dim(hidden, (1 - own) * seqs, 1, 0)
        hidden_got = [swap_blk(sent)]
        hidden, cotangent, sent = lax.optimization_barrier((hidden, cotangent, sent))
        hidden_kept = [
            lax.dynamic_slice_in_dim(hidden, own * seqs + seq, 1, 0) for seq in each
        ]
        hidden_sent = [
            lax.dynamic_slice_in_dim(hidden, (1 - own) * seqs + seq, 1, 0) for seq in each
        ]
        early = 2 * count // 16
        upstream_kept = lax.dynamic_slice_in_dim(cotangent, own * seqs, seqs, 0)
        upstream_sent = lax.dynamic_slice_in_dim(cotangent, (1 - own) * seqs, seqs, 0)
        upstream_sent = [upstream_sent[:, :early], upstream_sent[:, early:]]
        valid_all = jnp.where(flags == 1, lengths[:, 1], lengths[:, 0])
        valid = lax.dynamic_slice_in_dim(valid_all, own * seqs, seqs, 0)
        scalars = jnp.stack([lax.axis_index("dp") & 1, own]).astype(jnp.int32)

    with jax.named_scope("bias"):
        w_all = jnp.stack([w_query, w_key, w_value])
        one_hot = (
            buckets[None, :] == jnp.arange(buckets_used, dtype=jnp.int32)[:, None]
        ).astype(F32)
        one_hot = jnp.pad(one_hot, ((0, 0), (0, length - buckets.shape[0])))
        vector = lax.dot_general(
            bias_table * LOG2E,
            one_hot,
            (((0,), (0,)), ((), ())),
            precision=lax.Precision.HIGHEST,
        )
        bias = expand_bias(jnp.roll(vector, -(LANES - 1), axis=1), bias_width)

    with jax.named_scope("exchange_in"):
        ready = (hidden_kept, hidden_sent, upstream_kept, upstream_sent, w_all, bias, valid, scalars)
        ready, hidden_got[0] = lax.optimization_barrier((ready, hidden_got[0]))
        hidden_kept, hidden_sent, upstream_kept, upstream_sent, w_all, bias, valid, scalars = ready
        hidden_got += [swap_blk(sent) for sent in hidden_sent[1:]]

    contexts, saved, hidden_seq, attn_in_seq = [], [], [], []
    for seq in each:
        with jax.named_scope("project"):
            kept, got = hidden_kept[seq], hidden_got[seq]
            if seq > 0:
                got, contexts[-1] = lax.optimization_barrier((got, contexts[-1]))
            if seq == seqs - 1:
                late, got = lax.optimization_barrier((upstream_sent[1], got))
                late = swap_blk(late)
            whole_seq, attn_in, projected = project(scalars, kept, got, g_attn, w_all)
            if seq == 0:
                first_part, projected = lax.optimization_barrier(
                    (upstream_sent[0], projected)
                )
                upstream_got = swap_blk(first_part)
            hidden_seq.append(whole_seq)
            attn_in_seq.append(attn_in)
        with jax.named_scope("attend"):
            context, *rest_of = attend(projected, bias, valid, seq)
            contexts.append(context)
            saved.append([projected, *rest_of])

    with jax.named_scope("middle"):
        inputs, late = lax.optimization_barrier((jnp.concatenate(hidden_seq, axis=0), late))
        upstream_got = jnp.concatenate([upstream_got, late], axis=1)
        upstream = in_order(own, upstream_kept, upstream_got, 1).reshape(tokens, width)
        act, grad_pre, ffn_in, output_kept, output_sent, grad_low, grad_context, *rest_of = middle(
            scalars, contexts, hidden_seq, upstream, w_out, g_ffn, w_in, w_ffn_out
        )
        sent, kept, grad_g_ffn = rest_of
    with jax.named_scope("output"):
        output_got = swap_blk(output_sent)

    with jax.named_scope("ffn_weights"):
        out_shares = Shares([out_weights(scalars, act, upstream)], first + ["blk"] + second)
        out_shares.send()
        in_sent, in_kept = in_weights(scalars, ffn_in, grad_pre)
        in_sent, in_kept = receive([out_shares], in_sent, in_kept)
        in_shares = Shares([(in_sent, in_kept)], second + first + ["blk"])
        in_shares.send()
        out_shares.send()
        grad_context = receive([in_shares], grad_context)
        in_shares.send()

    with jax.named_scope("attend_back"):
        pairs = width // LANES
        parting = 2 * pairs // 3
        weights = (w_query, w_key, w_value)
        bias_one, one_sent, one_kept, before = attend_back(
            scalars, saved, attn_in_seq, grad_context, weights, bias_width,
            (0, parting), None,
        )
        one_shares = Shares([(one_sent, one_kept), (sent, kept)], second + first + later + ["last"])
        one_shares.send()
        before, grad_context, output_got = receive(
            [out_shares, in_shares], before, grad_context, output_got
        )
        out_shares.send()
        in_shares.send()
        before, grad_context = receive([one_shares], before, grad_context)
        one_shares.send()
        bias_two, two_sent, two_kept, input_kept, input_sent, grad_g_attn = attend_back(
            scalars, saved, attn_in_seq, grad_context, weights, bias_width,
            (parting, pairs), (before, inputs, grad_low, g_attn),
        )
        two_shares = Shares([(two_sent, two_kept)], first + second + later + ["last"])
        two_shares.send()
        bias_one, bias_two, input_sent = receive(
            [one_shares, in_shares, out_shares], bias_one, bias_two, input_sent
        )

    with jax.named_scope("rounds"):
        for shares in (out_shares, in_shares, one_shares):
            shares.send()
        input_got = swap_blk(input_sent)
        folded = fold_bias(bias_one, length), fold_bias(bias_two, length)
        folded = receive([two_shares, one_shares, out_shares, in_shares], *folded)
        in_shares.take_over(out_shares)
        in_shares.order = later + ["last"]
        two_shares.send()
        in_shares.send()

    with jax.named_scope("small"):
        table = lax.dot_general(
            one_hot,
            jnp.concatenate(folded, axis=0),
            (((1,), (1,)), ((), ())),
            precision=lax.Precision.HIGHEST,
        )
        flat = jnp.concatenate([grad_g_attn[0], grad_g_ffn[0], table.reshape(-1)])
        flat = jnp.pad(flat, (0, -flat.shape[0] % 1024)).reshape(-1, LANES)
        if size > 1:
            flat = flat + lax.ppermute(flat, "dp", flip("dp", 1))
        small_bits = list(range(1, bits_of(size))) + ["blk"]

    def small_step(flat, chains, *others):
        if not small_bits:
            flat, *others = receive(chains, flat, *others, 0)[:-1]
            return flat, *others
        bit = small_bits.pop(0)
        got = swap_blk(flat) if bit == "blk" else lax.ppermute(flat, "dp", flip("dp", 1 << bit))
        flat, got, *others = receive(chains, flat, got, *others)
        return flat + got, *others

    with jax.named_scope("rounds"):
        one_shares.send()
        flat, input_got = small_step(flat, [two_shares], input_got)
        two_shares.send()
        (flat,) = small_step(flat, [two_shares, in_shares, one_shares])
        chains = [two_shares, one_shares, in_shares]
        while any(shares.order for shares in chains) or small_bits:
            for shares in chains:
                shares.send()
            (flat,) = small_step(flat, chains)

    one, two = one_shares.total, two_shares.total
    pieces = jnp.split(one[:, : 3 * LANES * parting], 3 * parting, axis=1)
    pieces += jnp.split(two, 3 * (pairs - parting), axis=1)
    grad_query_w, grad_key_w, grad_value_w = (
        jnp.concatenate(pieces[part::3], axis=1) for part in range(3)
    )
    grad_out_w = one[:, 3 * LANES * parting :]
    two = in_shares.total
    units = w_in.shape[1]
    grad_in = two[:, :units]
    grad_ffn_out = jnp.concatenate(
        [two[:, start : start + width] for start in range(units, two.shape[1], width)], axis=0
    )
    with jax.named_scope("output"):
        output = put_got(own, output_kept, output_got)
        input_grad = put_got(own, input_kept, input_got)

    with jax.named_scope("small"):
        flat = flat.reshape(-1)
        share = width // size
        at = lax.axis_index("dp") * share
        gain_attn = lax.dynamic_slice_in_dim(flat[:width], at, share)
        gain_ffn = lax.dynamic_slice_in_dim(flat[width : 2 * width], at, share)
        table = flat[2 * width : 2 * width + buckets_used * heads].reshape(buckets_used, heads)

    return (
        output,
        input_grad,
        gain_attn,
        grad_query_w,
        grad_key_w,
        grad_value_w,
        grad_out_w,
        gain_ffn,
        grad_in,
        grad_ffn_out,
        table,
    )


def solution(mesh):
    split = P("dp", "blk", None)
    rows = P("dp", None)
    in_specs = (split, rows, P("dp")) + (P(),) * 10 + (split,)
    out_specs = (split, split, P("dp")) + (rows,) * 4 + (P("dp"), rows, rows, P())
    return jax.shard_map(body, mesh=mesh, in_specs=in_specs, out_specs=out_specs, check_vma=False)
```

```python
import copy
import functools
import math

import jax
import jax.numpy as jnp
from jax import lax
from jax.experimental import pallas as pl
from jax.experimental.pallas import tpu as pltpu
from jax.sharding import PartitionSpec as P

EPSILON = 1e-06
MASKED = -1000000000.0
SCALING = 0.125
LOG2E = 1.4426950408889634
LN2 = 0.6931471805599453
HEAD = 64
LANES = 128
VMEM_LIMIT = 32 * 2**20
BF16 = jnp.bfloat16
F32 = jnp.float32


def dot(left, right, left_dim, right_dim):
    return lax.dot_general(
        left, right, (((left_dim,), (right_dim,)), ((), ())), preferred_element_type=F32
    )


RESIDENT = pl.BlockSpec(memory_space=pltpu.VMEM)


def in_hbm(values):
    return pltpu.with_memory_space_constraint(values, pltpu.HBM)


def resident(*values):
    return [pltpu.with_memory_space_constraint(v, pltpu.VMEM) for v in values]


def expand_kernel(vector_ref, out_ref):
    group, _, width = vector_ref.shape
    for head in range(group):
        rows = jnp.broadcast_to(vector_ref[head], (LANES, width))
        moved = pltpu.roll(rows, 0, 1, stride=1, stride_axis=0)
        out_ref[head] = moved[:, : out_ref.shape[2]]


def expand_bias(vector, width):
    heads, length = vector.shape
    group = 4 if heads % 4 == 0 else 1
    return pl.pallas_call(
        expand_kernel,
        grid=(heads // group,),
        in_specs=[pl.BlockSpec((group, 1, length), lambda h: (h, 0, 0))],
        out_specs=pl.BlockSpec((group, LANES, width), lambda h: (h, 0, 0)),
        out_shape=jax.ShapeDtypeStruct((heads, LANES, width), F32),
        compiler_params=pltpu.CompilerParams(vmem_limit_bytes=VMEM_LIMIT),
    )(vector.reshape(heads, 1, length))


def fold_kernel(grad_ref, out_ref):
    width = grad_ref.shape[2]
    length = out_ref.shape[2]
    pad = jnp.zeros((8, length - width), F32)
    for head in range(grad_ref.shape[0]):
        total = jnp.zeros((8, length), F32)
        for start in range(0, LANES, 8):
            rows = jnp.concatenate([grad_ref[head, start : start + 8, :], pad], axis=1)
            total = total + pltpu.roll(rows, LANES - 8 - start, 1)
        folded = total[7:8]
        for row in range(7):
            folded = folded + pltpu.roll(total[row : row + 1], 7 - row, 1)
        out_ref[head] = jnp.broadcast_to(folded, (8, length))


def fold_bias(grad, length):
    heads, _, width = grad.shape
    group = 4 if heads % 4 == 0 else 1
    return pl.pallas_call(
        fold_kernel,
        grid=(heads // group,),
        in_specs=[pl.BlockSpec((group, LANES, width), lambda h: (h, 0, 0))],
        out_specs=pl.BlockSpec((group, 8, length), lambda h: (h, 0, 0)),
        out_shape=jax.ShapeDtypeStruct((heads, 8, length), F32),
        compiler_params=pltpu.CompilerParams(vmem_limit_bytes=VMEM_LIMIT),
        cost_estimate=pl.CostEstimate(flops=0, bytes_accessed=0, transcendentals=0),
    )(in_hbm(grad))[:, 0]


def inverse_of(values):
    return lax.rsqrt(jnp.mean(values * values, axis=1, keepdims=True) + EPSILON)


def project_kernel(scalars, kept_ref, got_ref, gain_ref, w_ref, hidden_ref, attn_in_ref, out_ref):
    half = kept_ref.shape[1]
    step = pl.program_id(0)

    @pl.when(step == 0)
    def _():
        for ref, place in ((kept_ref, scalars[1]), (got_ref, 1 - scalars[1])):
            rows = pl.ds(pl.multiple_of(place * half, half), half)
            hidden_ref[rows, :] = ref[0]
            values = ref[0].astype(F32)
            attn_in_ref[rows, :] = (values * inverse_of(values) * gain_ref[...]).astype(BF16)

    scale = jnp.where(step == 0, SCALING * LOG2E, 1.0)
    out_ref[0] = (dot(attn_in_ref[...], w_ref[0], 1, 0) * scale).astype(BF16)


def project(scalars, kept, got, gain, weights):
    _, half, width = kept.shape
    count = 2 * half
    once = pl.Buffered(1)

    def whole(*shape):
        return pl.BlockSpec(shape, lambda j, *_: (0,) * len(shape), pipeline_mode=once)

    return pl.pallas_call(
        project_kernel,
        grid_spec=pltpu.PrefetchScalarGridSpec(
            num_scalar_prefetch=1,
            grid=(weights.shape[0],),
            in_specs=[
                whole(1, half, width),
                whole(1, half, width),
                whole(1, width),
                pl.BlockSpec((1, width, width), lambda j, *_: (j, 0, 0)),
            ],
            out_specs=[
                whole(count, width),
                whole(count, width),
                pl.BlockSpec((1, count, width), lambda j, *_: (j, 0, 0)),
            ],
        ),
        out_shape=[
            jax.ShapeDtypeStruct((count, width), BF16),
            jax.ShapeDtypeStruct((count, width), BF16),
            jax.ShapeDtypeStruct((weights.shape[0], count, width), BF16),
        ],
        compiler_params=pltpu.CompilerParams(vmem_limit_bytes=VMEM_LIMIT),
        cost_estimate=pl.CostEstimate(
            flops=6 * count * width * width, bytes_accessed=8 * 2**20, transcendentals=0
        ),
    )(scalars, kept, got, gain.reshape(1, width), weights)


def attend_kernel(
    valid, q_ref, k_ref, v_ref, bias_ref, out_ref, copy_ref, weights_ref, inverse_ref, *, chunk, seq
):
    limit = valid[seq]
    count = q_ref.shape[1]
    pair = pl.program_id(0)
    columns = pl.ds(pl.multiple_of(pair * LANES, LANES), LANES)
    queries, keys, values = (ref[0].astype(F32) for ref in (q_ref, k_ref, v_ref))
    lane = lax.broadcasted_iota(jnp.int32, (count, LANES), 1)
    row = lax.broadcasted_iota(jnp.int32, (count, LANES), 0)
    heads = []
    for head in range(2):
        mine = (lane // HEAD) == head
        extra = lane == (1 - head) * HEAD
        mask = jnp.where(extra & (row >= limit), MASKED, 0.0)
        heads.append(
            (
                jnp.where(mine, queries, jnp.where(extra, 1.0, 0.0)).astype(BF16),
                jnp.where(mine, keys, mask).astype(BF16),
                jnp.where(mine, values, 1.0).astype(BF16),
            )
        )
    first = lax.broadcasted_iota(jnp.int32, (chunk, LANES), 1) < HEAD
    units = [(step, head) for step in range(count // chunk) for head in range(2)]

    def scores(unit):
        step, head = unit
        rows = slice(step * chunk, (step + 1) * chunk)
        windows = [
            bias_ref[head, :, count - LANES * (1 + block) : 2 * count - LANES * (1 + block)]
            for block in range(step * chunk // LANES, (step + 1) * chunk // LANES)
        ]
        return dot(heads[head][0][rows], heads[head][1], 1, 1) + jnp.concatenate(windows, axis=0)

    ahead = 2
    logits = {unit: scores(unit) for unit in units[:ahead]}
    sums = {}
    for place, unit in enumerate(units):
        step, head = unit
        rows = slice(step * chunk, (step + 1) * chunk)
        if place + ahead < len(units):
            logits[units[place + ahead]] = scores(units[place + ahead])
        top = jnp.max(logits[unit], axis=1, keepdims=True)
        weights = jnp.exp2(logits[unit] - top).astype(BF16)
        weights_ref[head, rows, :] = weights
        sums[unit] = dot(weights, heads[head][2], 1, 0)
        if head == 1:
            one, two = sums[step, 0], sums[step, 1]
            inverse = 1.0 / pltpu.roll(jnp.where(first, two, one), HEAD, 1)
            inverse_ref[rows, :] = inverse
            context = (jnp.where(first, one, two) * inverse).astype(BF16)
            out_ref[rows, columns] = context
            copy_ref[rows, :] = context


def projections_of(count, pair):
    return [
        pl.BlockSpec((1, count, LANES), lambda *at, part=part: (part, 0, pair(*at)))
        for part in range(3)
    ]


def attend(projected, bias, valid, seq, chunk=256):
    _, count, width = projected.shape
    block = pl.BlockSpec((count, LANES), lambda p, *_: (0, p))
    return pl.pallas_call(
        functools.partial(attend_kernel, chunk=chunk, seq=seq),
        grid_spec=pltpu.PrefetchScalarGridSpec(
            num_scalar_prefetch=1,
            grid=(width // LANES,),
            in_specs=[
                *projections_of(count, lambda p, *_: p),
                pl.BlockSpec((2, LANES, bias.shape[2]), lambda p, *_: (p, 0, 0)),
            ],
            out_specs=[
                RESIDENT,
                block,
                pl.BlockSpec((2, count, count), lambda p, *_: (p, 0, 0)),
                block,
            ],
        ),
        out_shape=[
            pltpu.VMEM((count, width), BF16),
            pltpu.HBM((count, width), BF16),
            pltpu.HBM((width // HEAD, count, count), BF16),
            pltpu.HBM((count, width), F32),
        ],
        compiler_params=pltpu.CompilerParams(vmem_limit_bytes=VMEM_LIMIT),
        cost_estimate=pl.CostEstimate(
            flops=32 * count * count * width, bytes_accessed=12 * 2**20, transcendentals=0
        ),
    )(valid, *[projected] * 3, bias)


def store_shares(grad, core, sent_ref, kept_ref, start=0, folds=1):
    count, rows, width = sent_ref.shape
    grad = grad.astype(BF16) if rows % 16 == 0 else grad
    for group in range(count):
        for fold in range(folds):
            place = (2 * group * folds + fold) * rows
            even = grad[place : place + rows]
            place += folds * rows
            odd = grad[place : place + rows]
            at = fold * (width // folds) + start
            columns = slice(at, at + grad.shape[1])
            sent_ref[group, :, columns] = jnp.where(core == 0, odd, even).astype(BF16)
            kept_ref[group, :, columns] = jnp.where(core == 0, even, odd).astype(BF16)


def attend_back_kernel(scalars, *refs, seqs, steps, finish):
    refs = list(refs)

    def some(count):
        taken = refs[:count]
        del refs[:count]
        return taken

    projected_refs = [some(3) for _ in range(seqs)]
    weights_refs, inverse_refs = some(seqs), some(seqs)
    attn_in_refs = some(seqs)
    ctx_refs = some(seqs)
    grad_ref, wq_ref, wk_ref, wv_ref = some(4)
    if finish:
        before_ref, hidden_ref, mid_ref, gain_ref = some(4)
    bias_ref, sent_ref, kept_ref = some(3)
    if finish:
        in_kept_ref, in_sent_ref, grad_gain_ref, back_ref = some(4)
    else:
        out_ref, back_ref = some(2)
    core, own = scalars[0], scalars[1]
    count = projected_refs[0][0].shape[1]
    lane = lax.broadcasted_iota(jnp.int32, (count, LANES), 1)

    step = pl.program_id(0)

    @pl.when(step == 0)
    def _():
        back_ref[...] = jnp.zeros_like(back_ref)

    @pl.when(step < steps)
    def _():
        bias_ref[...] = jnp.zeros_like(bias_ref)
        projections = jnp.concatenate([wq_ref[...], wk_ref[...], wv_ref[...]], axis=1)
        units = [(seq, head) for seq in range(seqs) for head in range(2)]
        loaded, scored, low_grads, parts = {}, {}, {}, {}

        def load(seq):
            here = slice(seq * count, (seq + 1) * count)
            queries, keys, values = (ref[0].astype(F32) for ref in projected_refs[seq])
            grads = grad_ref[here, :].astype(F32) * inverse_refs[seq][...]
            products = grads * ctx_refs[seq][...].astype(F32)
            turned = jnp.transpose(queries).astype(BF16), jnp.transpose(grads).astype(BF16)
            loaded[seq] = keys, values, grads, products, turned

        def score(unit):
            seq, head = unit
            if head == 0:
                load(seq)
            _, values, grads, products, _ = loaded[seq]
            mine = (lane // HEAD) == head
            other = (1 - head) * HEAD
            extra = (lane == other) | (lane == other + 1)
            v_head = jnp.where(mine, values, jnp.where(extra, 1.0, 0.0)).astype(BF16)
            delta = jnp.sum(jnp.where(mine, products, 0.0), axis=1, keepdims=True)
            high = delta.astype(BF16).astype(F32)
            spread = jnp.where(lane == other, -high, jnp.where(extra, high - delta, 0.0))
            g_head = jnp.where(mine, grads, spread).astype(BF16)
            scored[unit] = dot(g_head, v_head, 1, 1)

        def weigh(unit):
            seq, head = unit
            grad_logits = weights_refs[seq][head].astype(F32) * scored[unit]
            blocks = count // LANES
            for tile in range(2 * blocks - 1):
                bias_ref[head, :, tile * LANES : (tile + 1) * LANES] += sum(
                    grad_logits[
                        block * LANES : (block + 1) * LANES,
                        (tile + 1 + block - blocks) * LANES : (tile + 2 + block - blocks) * LANES,
                    ]
                    for block in range(blocks)
                    if 0 <= tile + 1 + block - blocks < blocks
                )
            low_grads[unit] = grad_logits.astype(BF16)

        def multiply(unit):
            seq, head = unit
            keys, _, _, _, (queries_t, grads_t) = loaded[seq]
            rows = slice(head * HEAD, (head + 1) * HEAD)
            k_head = jnp.where((lane // HEAD) == head, keys, 0.0).astype(BF16)
            low = low_grads[unit]
            parts[unit] = (
                dot(low, k_head, 1, 0),
                dot(queries_t[rows], low, 1, 0),
                dot(grads_t[rows], weights_refs[seq][head], 1, 0),
            )

        def project(seq):
            here = slice(seq * count, (seq + 1) * count)
            one, two = parts[seq, 0], parts[seq, 1]
            dk = jnp.transpose(jnp.concatenate([one[1], two[1]], axis=0))
            dv = jnp.transpose(jnp.concatenate([one[2], two[2]], axis=0))
            all_grads = jnp.concatenate(
                [(SCALING * (one[0] + two[0])).astype(BF16), (LN2 * dk).astype(BF16), dv.astype(BF16)],
                axis=1,
            )
            back_ref[here, :] += dot(all_grads, projections, 1, 1)
            return dot(attn_in_refs[seq][...], all_grads, 0, 0)

        weight_grad = None
        for place in range(len(units) + 1):
            if place < len(units):
                score(units[place])
            if 0 <= place - 1 < len(units):
                weigh(units[place - 1])
            if 0 <= place - 1:
                seq, head = units[place - 1]
                multiply((seq, head))
                if head == 1:
                    part = project(seq)
                    weight_grad = part if weight_grad is None else weight_grad + part
        store_shares(weight_grad, core, sent_ref, kept_ref)

    @pl.when(step >= steps)
    def _():
        place = step - steps
        half = count // 2
        if not finish:
            out_ref[...] = back_ref[pl.ds(pl.multiple_of(place * half, half), half), :].astype(BF16)
        else:
            start = pl.multiple_of(row_block(place, own, seqs) * half, half)
            back = back_ref[pl.ds(start, half), :] + before_ref[...].astype(F32)
            values = hidden_ref[...].astype(F32)
            inverse = lax.rsqrt(jnp.mean(values * values, axis=1, keepdims=True) + EPSILON)
            normed = values * inverse
            grad_gain = jnp.sum(back * normed, axis=0, keepdims=True)
            back = back * gain_ref[...]
            mean = jnp.mean(back * normed, axis=1, keepdims=True)
            grad = mid_ref[...].astype(F32) + inverse * (back - normed * mean)

            @pl.when(place == 0)
            def _():
                grad_gain_ref[...] = grad_gain

            @pl.when(place > 0)
            def _():
                grad_gain_ref[...] += grad_gain

            @pl.when(place < seqs)
            def _():
                in_sent_ref[0] = grad.astype(BF16)

            @pl.when(place >= seqs)
            def _():
                in_kept_ref[0] = grad.astype(BF16)


def row_block(place, own, seqs):
    return 2 * lax.rem(place, seqs) + jnp.where(place < seqs, 1 - own, own)


def attend_back(
    scalars, saved, attn_in, grads, projections, bias_width, pairs, ends
):
    seqs = len(saved)
    _, count, width = saved[0][0].shape
    size = lax.axis_size("dp")
    rows = width // size
    half = count // 2
    first, last = pairs
    steps = last - first
    once = pl.Buffered(1)

    def early(p):
        return jnp.minimum(p, steps - 1)

    def late(p):
        return jnp.maximum(p - steps, 0)

    weight = pl.BlockSpec((width, LANES), lambda p, *_: (0, first + early(p)))
    probs = pl.BlockSpec((2, count, count), lambda p, *_: (first + early(p), 0, 0))
    shares = pl.BlockSpec((size // 2, rows, 3 * LANES), lambda p, *_: (0, 0, early(p)))
    row = pl.BlockSpec((1, width), lambda p, *_: (0, 0), pipeline_mode=once)

    block = pl.BlockSpec((count, LANES), lambda p, *_: (0, first + early(p)))
    tall = pl.BlockSpec((seqs * count, LANES), lambda p, *_: (0, first + early(p)))
    whole = pl.BlockSpec((count, width), lambda p, *_: (0, 0), pipeline_mode=once)
    projected, contexts, weights, inverses = zip(*saved)
    operands = [v for v in projected for _ in range(3)]
    operands += [*weights, *inverses, *attn_in, *contexts, grads]
    operands = [in_hbm(v) for v in (*operands, *projections)]
    specs = projections_of(count, lambda p, *_: first + early(p)) * seqs
    specs += [probs] * seqs + [block] * seqs + [whole] * seqs
    specs += [block] * seqs + [tall] + [weight] * 3
    share = pltpu.HBM((size // 2, rows, 3 * LANES * steps), BF16)
    out_shape = [pltpu.HBM((2 * steps, LANES, bias_width), F32), share, share]
    out_specs = [pl.BlockSpec((2, LANES, bias_width), lambda p, *_: (early(p), 0, 0)), shares, shares]
    if ends is not None:
        before, hidden, grad_mid, gain = ends
        operands += [in_hbm(before), in_hbm(hidden), in_hbm(grad_mid), gain.reshape(1, width)]
        mixed_up = pl.BlockSpec(
            (half, width), lambda p, scalars: (row_block(late(p), scalars[1], seqs), 0)
        )
        specs += [mixed_up] * 3 + [row]
        out_shape.append(pltpu.HBM((2 * seqs, half, width), BF16))
        out_shape.append(pltpu.HBM((seqs, half, width), BF16))
        out_shape.append(jax.ShapeDtypeStruct((1, width), F32))
        out_specs += [
            pl.BlockSpec(
                (1, half, width),
                lambda p, scalars: (scalars[1] * seqs + jnp.maximum(late(p) - seqs, 0), 0, 0),
            ),
            pl.BlockSpec((1, half, width), lambda p, *_: (jnp.minimum(late(p), seqs - 1), 0, 0)),
            row,
        ]
    else:
        out_shape.append(pltpu.HBM((seqs * count, width), BF16))
        out_specs.append(pl.BlockSpec((half, width), lambda p, *_: (late(p), 0)))
    return pl.pallas_call(
        functools.partial(attend_back_kernel, seqs=seqs, steps=steps, finish=ends is not None),
        grid_spec=pltpu.PrefetchScalarGridSpec(
            num_scalar_prefetch=1,
            grid=(steps + 2 * seqs,),
            in_specs=specs,
            out_specs=out_specs,
            scratch_shapes=[pltpu.VMEM((seqs * count, width), F32)],
        ),
        out_shape=out_shape,
        compiler_params=pltpu.CompilerParams(vmem_limit_bytes=VMEM_LIMIT),
        cost_estimate=pl.CostEstimate(flops=0, bytes_accessed=0, transcendentals=0),
    )(scalars, *operands)


def store_product(left, right, core, sent_ref, kept_ref, folds=1, columns=256):
    for start in range(0, right.shape[1], columns):
        grad = dot(left, right[:, start : start + columns], 0, 0)
        store_shares(grad, core, sent_ref, kept_ref, start, folds)


def in_weight_kernel(scalars, ffn_in_ref, pre_ref, sent_ref, kept_ref):
    width = sent_ref.shape[2]
    columns = pl.ds(pl.multiple_of(pl.program_id(0) * width, width), width)
    store_product(ffn_in_ref[...], pre_ref[:, columns], scalars[0], sent_ref, kept_ref)


def in_weights(scalars, ffn_in, grad_pre):
    tokens, width = ffn_in.shape
    steps = grad_pre.shape[1] // width
    size = lax.axis_size("dp")
    share = pl.BlockSpec((size // 2, width // size, width), lambda j, *_: (0, 0, j))
    return pl.pallas_call(
        in_weight_kernel,
        grid_spec=pltpu.PrefetchScalarGridSpec(
            num_scalar_prefetch=1,
            grid=(steps,),
            in_specs=[RESIDENT, RESIDENT],
            out_specs=[share, share],
        ),
        out_shape=[pltpu.HBM((size // 2, width // size, steps * width), BF16)] * 2,
        compiler_params=pltpu.CompilerParams(vmem_limit_bytes=VMEM_LIMIT),
        cost_estimate=pl.CostEstimate(flops=0, bytes_accessed=0, transcendentals=0),
    )(scalars, *resident(ffn_in, grad_pre))


def out_weight_kernel(scalars, act_ref, upstream_ref, sent_ref, kept_ref, *, folds):
    width = upstream_ref.shape[1]
    columns = pl.ds(pl.multiple_of(pl.program_id(0) * width, width), width)
    store_product(act_ref[:, columns], upstream_ref[...], scalars[0], sent_ref, kept_ref, folds)


def out_weights(scalars, act, upstream):
    tokens, width = upstream.shape
    units = act.shape[1]
    size = lax.axis_size("dp")
    folds = steps = units // width
    shape = (size // 2, width // size, units)
    share = pl.BlockSpec((size // 2 // steps,) + shape[1:], lambda j, *_: (j, 0, 0))
    return pl.pallas_call(
        functools.partial(out_weight_kernel, folds=folds),
        grid_spec=pltpu.PrefetchScalarGridSpec(
            num_scalar_prefetch=1,
            grid=(steps,),
            in_specs=[RESIDENT, RESIDENT],
            out_specs=[share, share],
        ),
        out_shape=[pltpu.HBM(shape, BF16)] * 2,
        compiler_params=pltpu.CompilerParams(vmem_limit_bytes=VMEM_LIMIT),
        cost_estimate=pl.CostEstimate(flops=0, bytes_accessed=0, transcendentals=0),
    )(scalars, *resident(act, upstream))


def middle_kernel(scalars, *refs, seqs, chunk):
    context_refs, hidden_refs = refs[:seqs], refs[seqs : 2 * seqs]
    upstream_ref, w_out_ref, gain_ref, w_in_ref, w_ffn_out_ref = refs[2 * seqs : 2 * seqs + 5]
    act_ref, grad_pre_ref, ffn_in_ref, out_kept_ref, out_sent_ref = refs[2 * seqs + 5 : 2 * seqs + 10]
    grad_low_ref, grad_context_ref, sent_ref, kept_ref, grad_gain_ref = refs[
        2 * seqs + 10 : 2 * seqs + 15
    ]
    mixed_ref, total_ref, back_ref = refs[2 * seqs + 15 :]
    tokens, width = mixed_ref.shape
    count = tokens // seqs
    columns = w_in_ref.shape[1]
    step = pl.program_id(0)
    here = pl.ds(pl.multiple_of(step * columns, columns), columns)
    pieces = [
        (slice(start, start + chunk), start // count, slice(start % count, start % count + chunk))
        for start in range(0, tokens, chunk)
    ]

    @pl.when(step == 0)
    def _():
        for rows, seq, local in pieces:
            mixed = hidden_refs[seq][local, :].astype(F32)
            mixed = mixed + dot(context_refs[seq][local, :], w_out_ref[...], 1, 0)
            mixed_ref[rows, :] = mixed
            total_ref[rows, :] = mixed
            back_ref[rows, :] = jnp.zeros((chunk, width), F32)
            ffn_in_ref[rows, :] = (mixed * inverse_of(mixed) * gain_ref[...]).astype(BF16)

    for rows, _, _ in pieces:
        pre = dot(ffn_in_ref[rows, :], w_in_ref[...], 1, 0)
        grad_act = dot(upstream_ref[rows, :], w_ffn_out_ref[...], 1, 1)
        below = 0.5 + 0.5 * lax.erf(pre * 0.7071067811865476)
        density = jnp.exp2(pre * pre * (-0.5 * LOG2E)) * 0.3989422804014327
        act = (pre * below).astype(BF16)
        grad_pre = (grad_act * (below + pre * density)).astype(BF16)
        act_ref[rows, here] = act
        grad_pre_ref[rows, here] = grad_pre
        total_ref[rows, :] += dot(act, w_ffn_out_ref[...], 1, 0)
        back_ref[rows, :] += dot(grad_pre, w_in_ref[...], 1, 1)

    @pl.when(step == pl.num_programs(0) - 1)
    def _():
        grad_gain = jnp.zeros(gain_ref.shape, F32)
        weight = None
        for rows, seq, local in pieces:
            half, local_half = local.start // (count // 2), slice(
                local.start % (count // 2), local.start % (count // 2) + chunk
            )
            layer_out = total_ref[rows, :].astype(BF16)

            @pl.when(scalars[1] == half)
            def _():
                out_kept_ref[scalars[1] * seqs + seq, local_half, :] = layer_out

            @pl.when(scalars[1] != half)
            def _():
                out_sent_ref[seq, local_half, :] = layer_out

            mixed = mixed_ref[rows, :]
            inverse = inverse_of(mixed)
            normed = mixed * inverse
            back = back_ref[rows, :]
            grad_gain += jnp.sum(back * normed, axis=0, keepdims=True)
            back = back * gain_ref[...]
            mean = jnp.mean(back * normed, axis=1, keepdims=True)
            grad = upstream_ref[rows, :].astype(F32) + inverse * (back - normed * mean)
            low = grad.astype(BF16)
            grad_low_ref[rows, :] = low
            grad_context_ref[rows, :] = dot(low, w_out_ref[...], 1, 1).astype(BF16)
            part = dot(context_refs[seq][local, :], low, 0, 0)
            weight = part if weight is None else weight + part
        grad_gain_ref[...] = grad_gain
        store_shares(weight, scalars[0], sent_ref, kept_ref)


def middle(
    scalars, contexts, hidden, upstream, w_out, gain, w_in, w_ffn_out, columns=512, chunk=256
):
    tokens, width = upstream.shape
    units = w_in.shape[1]
    seqs = len(contexts)
    size = lax.axis_size("dp")
    once = pl.Buffered(1)

    def whole(*shape):
        return pl.BlockSpec(shape, lambda j, *_: (0,) * len(shape), pipeline_mode=once)

    shares = (size // 2, width // size, width)
    low = pltpu.HBM((tokens, width), BF16)
    return pl.pallas_call(
        functools.partial(middle_kernel, seqs=seqs, chunk=chunk),
        grid_spec=pltpu.PrefetchScalarGridSpec(
            num_scalar_prefetch=1,
            grid=(units // columns,),
            in_specs=[RESIDENT] * (2 * seqs + 1)
            + [
                whole(width, width),
                whole(1, width),
                pl.BlockSpec((width, columns), lambda j, *_: (0, j)),
                pl.BlockSpec((columns, width), lambda j, *_: (j, 0)),
            ],
            out_specs=[RESIDENT] * 3
            + [whole(2 * seqs, tokens // seqs // 2, width), whole(seqs, tokens // seqs // 2, width)]
            + [whole(tokens, width)] * 2
            + [whole(*shares), whole(*shares), whole(1, width)],
            scratch_shapes=[pltpu.VMEM((tokens, width), F32)] * 3,
        ),
        out_shape=[
            pltpu.VMEM((tokens, units), BF16),
            pltpu.VMEM((tokens, units), BF16),
            pltpu.VMEM((tokens, width), BF16),
            pltpu.HBM((2 * seqs, tokens // seqs // 2, width), BF16),
            pltpu.HBM((seqs, tokens // seqs // 2, width), BF16),
            low,
            low,
        ]
        + [pltpu.HBM(shares, BF16)] * 2
        + [jax.ShapeDtypeStruct((1, width), F32)],
        compiler_params=pltpu.CompilerParams(vmem_limit_bytes=VMEM_LIMIT),
        cost_estimate=pl.CostEstimate(
            flops=8 * tokens * width * units, bytes_accessed=20 * 2**20, transcendentals=0
        ),
    )(
        scalars,
        *resident(*contexts, *hidden, upstream),
        in_hbm(w_out),
        gain.reshape(1, width),
        in_hbm(w_in),
        in_hbm(w_ffn_out),
    )


def bits_of(size):
    return size.bit_length() - 1


def flip(axis, mask):
    size = lax.axis_size(axis)
    return [(index, index ^ mask) for index in range(size)]


def swap_blk(values):
    return lax.ppermute(values, "blk", flip("blk", 1))


def pick(values, index, axis):
    return lax.dynamic_index_in_dim(values, index, axis, keepdims=False)


def part_of(values, index, axis):
    share = values.shape[axis] // 2
    return lax.dynamic_slice_in_dim(values, index * share, share, axis)


def put_got(own, whole, got):
    return lax.dynamic_update_slice_in_dim(whole, got, (1 - own) * got.shape[0], 0)


def in_order(own, kept, got, axis):
    share = kept.shape[axis]
    shape = kept.shape[:axis] + (2 * share,) + kept.shape[axis + 1 :]
    both = lax.dynamic_update_slice_in_dim(jnp.zeros(shape, kept.dtype), kept, own * share, axis)
    return lax.dynamic_update_slice_in_dim(both, got, (1 - own) * share, axis)


def join(parts, axis):
    return parts[0] if len(parts) == 1 else jnp.concatenate(parts, axis)


class Term:
    def __init__(self, values, bits):
        self.values = values.reshape((2,) * len(bits) + values.shape[1:])
        self.bits = bits
        self.fixed = {}
        self.rows = (0, values.shape[1])
        self.columns = (0, values.shape[2])

    def narrowed(self, fixed=None, rows=None, columns=None):
        other = copy.copy(self)
        other.fixed = {**self.fixed, **(fixed or {})}
        if rows is not None:
            other.rows = (self.rows[0] + rows[0], rows[1])
        if columns is not None:
            other.columns = (self.columns[0] + columns[0], columns[1])
        return other

    def read(self):
        starts = [self.fixed.get(bit, 0) for bit in self.bits] + [self.rows[0], self.columns[0]]
        sizes = [1 if bit in self.fixed else 2 for bit in self.bits]
        left = math.prod(sizes)
        part = lax.dynamic_slice(self.values, starts, sizes + [self.rows[1], self.columns[1]])
        return part.reshape((left, self.rows[1], self.columns[1])).astype(F32)


class Shares:
    def __init__(self, shares, order):
        self.left = list(range(1, bits_of(lax.axis_size("dp"))))[::-1]
        self.order = [0] + order
        self.shares = shares
        self.by_column = False
        self.widths = []
        self.got = None
        self.parts = []

    def joined(self, narrow, axis):
        sums = [sum(term.narrowed(**narrow(term)).read() for term in terms) for terms in self.parts]
        return join([total.astype(BF16) for total in sums], axis)

    def keep(self, narrow):
        self.kept = self.joined(narrow, 2)

    def send(self):
        if not self.order or self.got is not None:
            return
        stage = self.order[0]
        own = lax.axis_index("blk")
        if stage == 0:
            self.got = [lax.ppermute(sent, "dp", flip("dp", 1)) for sent, _ in self.shares]
        elif stage == "last":
            self.kept = self.joined(lambda term: {}, 2)[0]
            self.got = swap_blk(self.kept)
        elif stage == "blk":

            def half(index):
                return lambda term: {
                    "columns": (index * (term.columns[1] // 2), term.columns[1] // 2)
                }

            self.widths = [terms[0].columns[1] // 2 for terms in self.parts]
            self.got = swap_blk(self.joined(half(1 - own), 2))
            self.keep(half(own))
        else:
            mine = (lax.axis_index("dp") >> stage) & 1
            sent = self.joined(lambda term: {"fixed": {stage: 1 - mine}}, 2)
            self.got = lax.ppermute(sent, "dp", flip("dp", 1 << stage))
            self.keep(lambda term: {"fixed": {stage: mine}})
            self.left = [bit for bit in self.left if bit != stage]

    def receive(self):
        stage = self.order.pop(0)
        got, self.got = self.got, None
        if stage == 0:
            self.parts = [
                [Term(kept, self.left), Term(new, self.left)]
                for (_, kept), new in zip(self.shares, got)
            ]
        elif stage == "last":
            if self.by_column:
                total = in_order(lax.axis_index("blk"), self.kept, got, 1).astype(F32)
                half = total.shape[1] // 2
                parts, start = [], 0
                for width in self.widths:
                    parts.append(total[:, start : start + width])
                    parts.append(total[:, half + start : half + start + width])
                    start += width
                self.total = jnp.concatenate(parts, axis=1)
            else:
                self.total = self.kept.astype(F32) + got.astype(F32)
        else:
            self.by_column = self.by_column or stage == "blk"
            self.parts = [[Term(self.kept, self.left), Term(got, self.left)]]

    def take_over(self, other):
        rows = self.parts[0][0].rows[1]
        for terms in other.parts:
            for start in range(0, terms[0].rows[1], rows):
                self.parts.append([term.narrowed(rows=(start, rows)) for term in terms])
                self.widths.append(terms[0].columns[1])


def receive(shares, *values):
    shares = [share for share in shares if share.got is not None]
    gots, values = lax.optimization_barrier(([share.got for share in shares], values))
    for share, got in zip(shares, gots):
        share.got = got
        share.receive()
    return values if len(values) > 1 else values[0]


def body(
    hidden,
    lengths,
    flags,
    buckets,
    g_attn,
    w_query,
    w_key,
    w_value,
    w_out,
    g_ffn,
    w_in,
    w_ffn_out,
    bias_table,
    cotangent,
):
    own = lax.axis_index("blk")
    size = lax.axis_size("dp")
    rest = list(range(1, bits_of(size)))
    first, second, later = rest[:1], rest[1:2], rest[2:]
    width = hidden.shape[2]
    seqs = hidden.shape[0] // 2
    count = hidden.shape[1] * 2
    tokens = seqs * count
    each = range(seqs)
    buckets_used, heads = bias_table.shape
    bias_width = 2 * count - LANES
    length = 2 * count

    with jax.named_scope("exchange_in"):
        def take(values, start, number):
            kept = lax.dynamic_slice_in_dim(values, own * seqs + start, number, 0)
            return kept, lax.dynamic_slice_in_dim(values, (1 - own) * seqs + start, number, 0)

        sent = lax.dynamic_slice_in_dim(hidden, (1 - own) * seqs, 1, 0)
        hidden_got = [swap_blk(sent)]
        hidden, cotangent, sent = lax.optimization_barrier((hidden, cotangent, sent))
        hidden_kept = [
            lax.dynamic_slice_in_dim(hidden, own * seqs + seq, 1, 0) for seq in each
        ]
        hidden_sent = [
            lax.dynamic_slice_in_dim(hidden, (1 - own) * seqs + seq, 1, 0) for seq in each
        ]
        early = 2 * count // 16
        upstream_kept = lax.dynamic_slice_in_dim(cotangent, own * seqs, seqs, 0)
        upstream_sent = lax.dynamic_slice_in_dim(cotangent, (1 - own) * seqs, seqs, 0)
        upstream_sent = [upstream_sent[:, :early], upstream_sent[:, early:]]
        valid_all = jnp.where(flags == 1, lengths[:, 1], lengths[:, 0])
        valid = lax.dynamic_slice_in_dim(valid_all, own * seqs, seqs, 0)
        scalars = jnp.stack([lax.axis_index("dp") & 1, own]).astype(jnp.int32)

    with jax.named_scope("bias"):
        w_all = jnp.stack([w_query, w_key, w_value])
        one_hot = (
            buckets[None, :] == jnp.arange(buckets_used, dtype=jnp.int32)[:, None]
        ).astype(F32)
        one_hot = jnp.pad(one_hot, ((0, 0), (0, length - buckets.shape[0])))
        vector = lax.dot_general(
            bias_table * LOG2E,
            one_hot,
            (((0,), (0,)), ((), ())),
            precision=lax.Precision.HIGHEST,
        )
        bias = expand_bias(jnp.roll(vector, -(LANES - 1), axis=1), bias_width)

    with jax.named_scope("exchange_in"):
        ready = (hidden_kept, hidden_sent, upstream_kept, upstream_sent, w_all, bias, valid, scalars)
        ready, hidden_got[0] = lax.optimization_barrier((ready, hidden_got[0]))
        hidden_kept, hidden_sent, upstream_kept, upstream_sent, w_all, bias, valid, scalars = ready
        hidden_got += [swap_blk(sent) for sent in hidden_sent[1:]]

    contexts, saved, hidden_seq, attn_in_seq = [], [], [], []
    for seq in each:
        with jax.named_scope("project"):
            kept, got = hidden_kept[seq], hidden_got[seq]
            if seq > 0:
                got, contexts[-1] = lax.optimization_barrier((got, contexts[-1]))
            if seq == seqs - 1:
                late, got = lax.optimization_barrier((upstream_sent[1], got))
                late = swap_blk(late)
            whole_seq, attn_in, projected = project(scalars, kept, got, g_attn, w_all)
            if seq == 0:
                first_part, projected = lax.optimization_barrier(
                    (upstream_sent[0], projected)
                )
                upstream_got = swap_blk(first_part)
            hidden_seq.append(whole_seq)
            attn_in_seq.append(attn_in)
        with jax.named_scope("attend"):
            context, *rest_of = attend(projected, bias, valid, seq)
            contexts.append(context)
            saved.append([projected, *rest_of])

    with jax.named_scope("middle"):
        inputs, late = lax.optimization_barrier((jnp.concatenate(hidden_seq, axis=0), late))
        upstream_got = jnp.concatenate([upstream_got, late], axis=1)
        upstream = in_order(own, upstream_kept, upstream_got, 1).reshape(tokens, width)
        act, grad_pre, ffn_in, output_kept, output_sent, grad_low, grad_context, *rest_of = middle(
            scalars, contexts, hidden_seq, upstream, w_out, g_ffn, w_in, w_ffn_out
        )
        sent, kept, grad_g_ffn = rest_of
    with jax.named_scope("output"):
        output_got = swap_blk(output_sent)

    with jax.named_scope("ffn_weights"):
        out_shares = Shares([out_weights(scalars, act, upstream)], first + ["blk"] + second)
        out_shares.send()
        in_sent, in_kept = in_weights(scalars, ffn_in, grad_pre)
        in_sent, in_kept = receive([out_shares], in_sent, in_kept)
        in_shares = Shares([(in_sent, in_kept)], second + first + ["blk"])
        in_shares.send()
        out_shares.send()
        grad_context = receive([in_shares], grad_context)
        in_shares.send()

    with jax.named_scope("attend_back"):
        pairs = width // LANES
        parting = 2 * pairs // 3
        weights = (w_query, w_key, w_value)
        bias_one, one_sent, one_kept, before = attend_back(
            scalars, saved, attn_in_seq, grad_context, weights, bias_width,
            (0, parting), None,
        )
        one_shares = Shares([(one_sent, one_kept), (sent, kept)], second + first + later + ["last"])
        one_shares.send()
        before, grad_context, output_got = receive(
            [out_shares, in_shares], before, grad_context, output_got
        )
        out_shares.send()
        in_shares.send()
        before, grad_context = receive([one_shares], before, grad_context)
        one_shares.send()
        bias_two, two_sent, two_kept, input_kept, input_sent, grad_g_attn = attend_back(
            scalars, saved, attn_in_seq, grad_context, weights, bias_width,
            (parting, pairs), (before, inputs, grad_low, g_attn),
        )
        two_shares = Shares([(two_sent, two_kept)], first + second + later + ["last"])
        two_shares.send()
        bias_one, bias_two, input_sent = receive(
            [one_shares, in_shares, out_shares], bias_one, bias_two, input_sent
        )

    with jax.named_scope("rounds"):
        for shares in (out_shares, in_shares, one_shares):
            shares.send()
        input_got = swap_blk(input_sent)
        folded = fold_bias(bias_one, length), fold_bias(bias_two, length)
        folded = receive([two_shares, one_shares, out_shares, in_shares], *folded)
        in_shares.take_over(out_shares)
        in_shares.order = later + ["last"]
        two_shares.send()
        in_shares.send()

    with jax.named_scope("small"):
        table = lax.dot_general(
            one_hot,
            jnp.concatenate(folded, axis=0),
            (((1,), (1,)), ((), ())),
            precision=lax.Precision.HIGHEST,
        )
        flat = jnp.concatenate([grad_g_attn[0], grad_g_ffn[0], table.reshape(-1)])
        flat = jnp.pad(flat, (0, -flat.shape[0] % 1024)).reshape(-1, LANES)
        if size > 1:
            flat = flat + lax.ppermute(flat, "dp", flip("dp", 1))
        small_bits = list(range(1, bits_of(size))) + ["blk"]

    def small_step(flat, chains, *others):
        if not small_bits:
            flat, *others = receive(chains, flat, *others, 0)[:-1]
            return flat, *others
        bit = small_bits.pop(0)
        got = swap_blk(flat) if bit == "blk" else lax.ppermute(flat, "dp", flip("dp", 1 << bit))
        flat, got, *others = receive(chains, flat, got, *others)
        return flat + got, *others

    with jax.named_scope("rounds"):
        one_shares.send()
        flat, input_got = small_step(flat, [two_shares], input_got)
        two_shares.send()
        (flat,) = small_step(flat, [two_shares, in_shares, one_shares])
        chains = [two_shares, one_shares, in_shares]
        while any(shares.order for shares in chains) or small_bits:
            for shares in chains:
                shares.send()
            (flat,) = small_step(flat, chains)

    one, two = one_shares.total, two_shares.total
    pieces = jnp.split(one[:, : 3 * LANES * parting], 3 * parting, axis=1)
    pieces += jnp.split(two, 3 * (pairs - parting), axis=1)
    grad_query_w, grad_key_w, grad_value_w = (
        jnp.concatenate(pieces[part::3], axis=1) for part in range(3)
    )
    grad_out_w = one[:, 3 * LANES * parting :]
    two = in_shares.total
    units = w_in.shape[1]
    grad_in = two[:, :units]
    grad_ffn_out = jnp.concatenate(
        [two[:, start : start + width] for start in range(units, two.shape[1], width)], axis=0
    )
    with jax.named_scope("output"):
        output = put_got(own, output_kept, output_got)
        input_grad = put_got(own, input_kept, input_got)

    with jax.named_scope("small"):
        flat = flat.reshape(-1)
        share = width // size
        at = lax.axis_index("dp") * share
        gains = flat[: 2 * width].reshape(2, width)
        gain_attn, gain_ffn = lax.dynamic_slice_in_dim(gains, at, share, 1)
        table = flat[2 * width : 2 * width + buckets_used * heads].reshape(buckets_used, heads)

    return (
        output,
        input_grad,
        gain_attn,
        grad_query_w,
        grad_key_w,
        grad_value_w,
        grad_out_w,
        gain_ffn,
        grad_in,
        grad_ffn_out,
        table,
    )


def solution(mesh):
    split = P("dp", "blk", None)
    rows = P("dp", None)
    in_specs = (split, rows, P("dp")) + (P(),) * 10 + (split,)
    out_specs = (split, split, P("dp")) + (rows,) * 4 + (P("dp"), rows, rows, P())
    return jax.shard_map(body, mesh=mesh, in_specs=in_specs, out_specs=out_specs, check_vma=False)
```
